32 devices in a mesh: row: 4 (over y, x), tile: 8 (over z, core).
Axes of the slice: x: 2, y: 2, z: 4, core: 2. Of those that a mesh axis runs over, the one named last changes fastest.
Arguments:
- row_points: float32 [3, 16384], replicated, may hold values from 0 to 6, as said below
- source_points: float32 [3, 32768], P(None, 'tile'), may hold values from -2.5 to 6, as said below
- sketch: bfloat16 [32768, 128], P('tile'), may hold values from -6 to 6
- admissible: int32 [4, 256], P('row', 'tile'), may hold values from 0 to 1, as said below
Outputs:
- basis: float32 [16384, 128], P(('row', 'tile'))
- projected: bfloat16 [4, 128, 32768], P('row', None, 'tile')
The draws below stay inside these ranges and needn't reach their ends.
Inputs may be any that keep to these rules, and one draw needn't show every extreme that they name: In every block row, the 32 panels of some index of tile are all admissible; how many panels of an index of tile are admissible varies widely. `row_points`: the first two coordinates lie in 0 to 6 and the third in 0 to 0.25. `source_points`: the first two coordinates lie in 0 to 6 and the third in -2.5 to -0.5.
All inputs are finite; a program needn't handle non-finite values.
Results may differ from the reference program's by a relative error of at most 0.0055.
Values may be sent and summed in bfloat16 or wider, within the bound.
No kernel may reach another device: no remote copies, remote signals or barrier semaphores. Data moves between devices by JAX's collectives and lax.ppermute only.
A program may use at most 64 MiB of HBM per device.

```python
import math
import jax
import jax.numpy as jnp
from jax import lax

CS = 4096
K = 128
PW = 128
PAN_DEV = 32
NPTS = 32768
NPAN = 256
BLOCKS = 4
ROWS = 16384


def draw_points(key, count, low, high):
    first = jax.random.fold_in(key, 0)
    third = jax.random.fold_in(key, 2)
    plane = jax.random.uniform(first, (2, count), dtype=jnp.float32, minval=0.0, maxval=6.0)
    depth = jax.random.uniform(third, (1, count), dtype=jnp.float32, minval=low, maxval=high)
    return jnp.concatenate([plane, depth], 0).astype(jnp.float32)


def draw_row_points(key, part):
    return draw_points(jax.random.fold_in(key, 11), ROWS, 0.0, 0.25)


def draw_source_points(key, part):
    return draw_points(jax.random.fold_in(key, 23), NPTS, -2.5, -0.5)


def draw_admissible(key, part):
    tiles = NPAN // PAN_DEV
    one, two, three, four = jax.random.split(key, 4)
    first = jax.random.randint(one, (BLOCKS, tiles), 0, PAN_DEV + 1)
    second = jax.random.randint(two, (BLOCKS, tiles), 0, PAN_DEV + 1)
    count = first * second // PAN_DEV
    full = jax.random.randint(three, (BLOCKS, 1), 0, tiles)
    count = jnp.where(jnp.arange(tiles)[None, :] == full, PAN_DEV, count)
    scores = jax.random.randint(four, (BLOCKS, tiles, PAN_DEV), 0, 1 << 20) * PAN_DEV + jnp.arange(PAN_DEV)[None, None, :]
    place = jnp.argsort(jnp.argsort(scores, axis=-1, stable=True), axis=-1, stable=True)
    mask = (place < count[:, :, None]).astype(jnp.int32)
    return mask.reshape(BLOCKS, NPAN)


def shard_levels(key, dims, cuts, low, top_value):
    loudness = 1.0
    for axis_at, parts in cuts:
        steps = jax.random.uniform(jax.random.fold_in(jax.random.fold_in(key, 6), axis_at), (parts,), jnp.float32, low / len(cuts), top_value / len(cuts))
        loudness = loudness * jnp.repeat(jnp.exp(steps), dims[axis_at] // parts).reshape((-1,) + (1,) * (len(dims) - 1 - axis_at))
    return loudness


def noise(key, dims, scale, most, pieces=(), held_as=jnp.bfloat16):
    array = jax.random.normal(key, dims, jnp.float32) * scale
    if len(pieces) > 0:
        array = shard_levels(key, dims, pieces, -0.22, 0.18) * array
    return jnp.clip(array, min=-most, max=most).astype(held_as)


def setup_inputs(seed: int = 0) -> dict:
    key_list = jax.random.split(jax.random.key(seed), 5)
    return {
        "row_points": draw_row_points(jax.random.fold_in(key_list[4], 71), 0),
        "source_points": draw_source_points(jax.random.fold_in(key_list[4], 71), 0),
        "sketch": noise(key_list[2], (NPTS, K), 1.0, 6.0, ((0, 8),)),
        "admissible": draw_admissible(jax.random.fold_in(key_list[4], 71), 0),
    }


DAMPING = 0.25
WAVENUM = 24.0

def kernel_block(targets, sources):
    dx = targets[0][:, None] - sources[0][None, :]
    dy = targets[1][:, None] - sources[1][None, :]
    dz = targets[2][:, None] - sources[2][None, :]
    dist = jnp.sqrt(dx * dx + dy * dy + dz * dz)
    value = jnp.exp(-DAMPING * dist) * jnp.cos(WAVENUM * dist) / (4.0 * math.pi * dist)
    return value.astype(jnp.bfloat16)

def factor(gram):
    shift = 0.0001 * jnp.trace(gram) / gram.shape[0]
    return jnp.linalg.cholesky(gram + shift * jnp.eye(gram.shape[0], dtype=jnp.float32))

def reference(row_points, source_points, sketch, admissible):
    pan_src = source_points.reshape(3, NPAN, PW).transpose(1, 0, 2)
    pan_sk = sketch.reshape(NPAN, PW, K)
    blk_pts = row_points.reshape(3, BLOCKS, CS).transpose(1, 0, 2)

    def one_block(item):
        targets, flags = item

        def add_panel(total, entry):
            src, omega, flag = entry
            term = lax.cond(flag > 0, lambda: jnp.dot(kernel_block(targets, src).astype(jnp.float32), omega.astype(jnp.float32), preferred_element_type=jnp.float32), lambda: jnp.zeros((CS, K), jnp.float32))
            return (total + term, None)
        sampled, _ = lax.scan(add_panel, jnp.zeros((CS, K), jnp.float32), (pan_src, pan_sk, flags))
        sampled_low = sampled.astype(jnp.bfloat16)
        gram = jnp.dot(sampled_low.T.astype(jnp.float32), sampled_low.astype(jnp.float32), preferred_element_type=jnp.float32)
        lower = factor(gram)
        basis = jax.scipy.linalg.solve_triangular(lower, sampled_low.astype(jnp.float32).T, lower=True).T
        basis_low = basis.astype(jnp.bfloat16)

        def project(carry, entry):
            src, flag = entry
            out = lax.cond(flag > 0, lambda: jnp.dot(basis_low.T.astype(jnp.float32), kernel_block(targets, src).astype(jnp.float32), preferred_element_type=jnp.float32), lambda: jnp.zeros((K, PW), jnp.float32))
            return (carry, out.astype(jnp.bfloat16))
        _, panels = lax.scan(project, jnp.zeros((), jnp.float32), (pan_src, flags))
        return (basis, panels.transpose(1, 0, 2).reshape(K, NPTS))
    bases, projs = lax.map(one_block, (blk_pts, admissible))
    return (bases.reshape(ROWS, K), projs)
```

```python
import functools
import math

import jax
import jax.numpy as jnp
import numpy as np
from jax import lax
from jax.experimental import pallas as pl
from jax.experimental.pallas import tpu as pltpu
from jax.sharding import PartitionSpec as P

DAMPING = 0.25
WAVENUM = 24.0
SHIFT = 0.0001

TURNS = WAVENUM / (2.0 * math.pi)
DECAY = -DAMPING / TURNS / math.log(2.0)
AMP = TURNS / (4.0 * math.pi)
S0, S1, S2 = 6.28127979 * AMP, -41.0952178 * AMP, 73.5851113 * AMP

WIDTH = 128
TERMS = 32
SUB = 8


def head(x):
    return x.astype(jnp.bfloat16).astype(jnp.float32)


def three(x):
    a = head(x)
    b = head(x - a)
    return a, b, x - a - b


def fill_terms(ref, points, side):
    x = points - CENTER_COL(points)
    scale = TURNS * TURNS
    norm = scale * jnp.sum(x * x, axis=0, keepdims=True)
    nh, nm, nl = three(norm)
    one = jnp.ones_like(norm)
    if side == 0:
        h, m, l = three(x)
        rows = [h, h, m, h, l, m]
        tail = [nh, nm, nl, one, one, one]
    else:
        h, m, l = three(x * (-2.0 * scale))
        rows = [h, m, h, l, h, m]
        tail = [one, one, one, nh, nm, nl]
    ref[...] = jnp.zeros_like(ref)
    for at, row in enumerate(rows):
        ref[3 * at : 3 * at + 3, :] = row
    for at, row in enumerate(tail):
        ref[18 + at : 19 + at, :] = row


def CENTER_COL(points):
    at = lax.broadcasted_iota(jnp.int32, points.shape, 0)
    return jnp.where(at == 2, -0.5, 3.0).astype(jnp.float32)


def near_field(square):
    inv = lax.rsqrt(square)
    t = square * inv
    f = t - jnp.round(t)
    g = 0.25 - jnp.abs(f)
    v = g * g
    wave = ((S2 * v + S1) * v + S0) * g
    amp = jnp.exp2(DECAY * t) * inv
    return (wave * amp).astype(jnp.bfloat16)


def order_panels(flags_ref, order_ref, count_panels):
    def step(p, count):
        @pl.when(flags_ref[p] > 0)
        def _():
            order_ref[count] = p

        return count + (flags_ref[p] > 0).astype(jnp.int32)

    return lax.fori_loop(0, count_panels, step, jnp.int32(0))


def sketch_kernel(
    flags_ref, rows_ref, src_ref, omega_ref, part_ref, tiles_ref,
    order_ref, count_ref, row_terms, src_terms, src_pick, omega_pick, total, *, panels, strip
):
    rb = rows_ref.shape[1]

    @pl.when(pl.program_id(0) == 0)
    def _():
        count = order_panels(flags_ref, order_ref, panels)
        count_ref[0] = count
        fill_terms(src_terms, src_ref[...], 1)

        def pick(slot, carry):
            at = pl.multiple_of(order_ref[slot] * WIDTH, WIDTH)
            to = pl.multiple_of(slot * WIDTH, WIDTH)
            src_pick[:, pl.ds(to, WIDTH)] = src_terms[:, pl.ds(at, WIDTH)].astype(jnp.bfloat16)
            omega_pick[pl.ds(to, WIDTH), :] = omega_ref[pl.ds(at, WIDTH), :]
            return carry

        lax.fori_loop(0, count, pick, 0)
        to = pl.multiple_of(count * WIDTH, WIDTH)
        src_pick[:, pl.ds(to, WIDTH)] = src_terms[:, :WIDTH].astype(jnp.bfloat16)
        omega_pick[pl.ds(to, WIDTH), :] = jnp.zeros((WIDTH, omega_pick.shape[1]), jnp.bfloat16)

    fill_terms(row_terms, rows_ref[...], 0)
    row_mat = row_terms[...].T.astype(jnp.bfloat16)
    total[...] = jnp.zeros_like(total)

    def pair(j, carry):
        at = pl.multiple_of(j * 2 * WIDTH, 2 * WIDTH)
        src = src_pick[:, pl.ds(at, 2 * WIDTH)]
        omega = omega_pick[pl.ds(at, 2 * WIDTH), :]
        for s in range(rb // strip):
            part = slice(s * strip, (s + 1) * strip)
            square = jnp.dot(row_mat[part], src, preferred_element_type=jnp.float32)
            tile = near_field(square)
            tiles_ref[2 * j, part, :] = tile[:, :WIDTH]
            tiles_ref[2 * j + 1, part, :] = tile[:, WIDTH:]
            total[part, :] += jnp.dot(tile, omega, preferred_element_type=jnp.float32)
        return carry

    lax.fori_loop(0, (count_ref[0] + 1) // 2, pair, 0)
    part_ref[...] = total[...].astype(part_ref.dtype)


def sketch_pass(flags, row_points, source_points, sketch, rows, rb=512, strip=128):
    panels = flags.shape[0]
    cols = source_points.shape[1]
    rank = sketch.shape[1]
    steps = rows // rb
    return pl.pallas_call(
        functools.partial(sketch_kernel, panels=panels, strip=strip),
        grid_spec=pltpu.PrefetchScalarGridSpec(
            num_scalar_prefetch=1,
            grid=(steps,),
            in_specs=[
                pl.BlockSpec((3, rb), lambda i, f: (0, lax.axis_index("row") * steps + i)),
                pl.BlockSpec((3, cols), lambda i, f: (0, 0)),
                pl.BlockSpec((cols, rank), lambda i, f: (0, 0)),
            ],
            out_specs=[
                pl.BlockSpec((rb, rank), lambda i, f: (i, 0)),
                pl.BlockSpec((panels, rb, WIDTH), lambda i, f: (0, i, 0)),
            ],
            scratch_shapes=[
                pltpu.SMEM((panels + 1,), jnp.int32),
                pltpu.SMEM((1,), jnp.int32),
                pltpu.VMEM((TERMS, rb), jnp.float32),
                pltpu.VMEM((TERMS, cols), jnp.float32),
                pltpu.VMEM((TERMS, cols + WIDTH), jnp.bfloat16),
                pltpu.VMEM((cols + WIDTH, rank), jnp.bfloat16),
                pltpu.VMEM((rb, rank), jnp.float32),
            ],
        ),
        out_shape=[
            jax.ShapeDtypeStruct((rows, rank), jnp.bfloat16),
            jax.ShapeDtypeStruct((panels, rows, WIDTH), jnp.bfloat16),
        ],
        compiler_params=pltpu.CompilerParams(vmem_limit_bytes=40 * 2**20),
        name="sketch_pass",
    )(flags, row_points, source_points, sketch)


def sum_kernel(parts_ref, out_ref):
    total = parts_ref[0].astype(jnp.float32)
    for k in range(1, parts_ref.shape[0]):
        total = total + parts_ref[k].astype(jnp.float32)
    low = total.astype(jnp.bfloat16)
    for k in range(out_ref.shape[0]):
        out_ref[k] = low


def sum_copies(parts):
    return pl.pallas_call(
        sum_kernel,
        out_shape=jax.ShapeDtypeStruct(parts.shape, jnp.bfloat16),
        name="sum_copies",
    )(parts)


def invert_factor(gram):
    n = gram.shape[0]
    pieces = n // SUB
    lane = lax.broadcasted_iota(jnp.int32, (SUB, n), 1)
    sub = lax.broadcasted_iota(jnp.int32, (SUB, n), 0)
    trace = jnp.zeros((SUB, n), jnp.float32)
    for v in range(pieces):
        trace = trace + jnp.where(lane == sub + v * SUB, gram[v * SUB : (v + 1) * SUB, :], 0.0)
    shift = (SHIFT / n) * jnp.sum(trace)
    a = [
        gram[v * SUB : (v + 1) * SUB, :] + jnp.where(lane == sub + v * SUB, shift, 0.0)
        for v in range(pieces)
    ]
    for b in range(pieces):
        cols = [
            {v: jnp.broadcast_to(a[v][:, b * SUB + c : b * SUB + c + 1], (SUB, n)) for v in range(b, pieces)}
            for c in range(SUB)
        ]
        for c in range(SUB):
            j = b * SUB + c
            pivot = jnp.broadcast_to(cols[c][b][c : c + 1, :], (SUB, n))
            inv = 1.0 / pivot
            row = jnp.broadcast_to(a[b][c : c + 1, :], (SUB, n))
            row = jnp.where(lane == j, 1.0, row)
            nexts = {
                c2: jnp.broadcast_to(cols[c2][b][c : c + 1, :], (SUB, n)) for c2 in range(c + 1, SUB)
            }
            for v in range(b, pieces):
                m = cols[c][v] * inv
                here = lane == j
                if v == b:
                    m = jnp.where(sub > c, m, 0.0)
                    here = here & (sub > c)
                a[v] = jnp.where(here, 0.0, a[v]) - m * row
                for c2 in range(c + 1, SUB):
                    cols[c2][v] = cols[c2][v] - m * nexts[c2]
    out = []
    for v in range(pieces):
        diag = lane == sub + v * SUB
        d = jnp.sum(jnp.where(diag, a[v], 0.0), axis=1, keepdims=True)
        low = jnp.where(lane < sub + v * SUB, a[v], jnp.where(diag, 1.0, 0.0))
        out.append(low * lax.rsqrt(d))
    return jnp.concatenate(out, axis=0)


def dot_exact(x, y, dims):
    pieces = [p.astype(jnp.bfloat16) for p in three(x)]
    parts = [lax.dot_general(p, y, dims, preferred_element_type=jnp.float32) for p in pieces]
    return parts[0] + (parts[1] + parts[2])


def project_kernel(
    flags_ref, low_ref, tiles_hbm, basis_ref, out_ref,
    order_ref, held, sems, *, panels, own_rows
):
    copies = [pltpu.make_async_copy(tiles_hbm.at[k], held.at[k], sems.at[k]) for k in range(panels)]
    for copy in copies:
        copy.start()
    count = order_panels(flags_ref, order_ref, panels)
    out_ref[...] = jnp.zeros_like(out_ref)
    low = low_ref[...]
    low_t = low.T
    gram = jnp.dot(low_t, low, preferred_element_type=jnp.float32)
    inverse = invert_factor(gram)
    at = pl.multiple_of(lax.axis_index("tile") * own_rows, own_rows)
    own = low_ref[pl.ds(at, own_rows), :]
    inv_t = [p.astype(jnp.bfloat16) for p in three(inverse.T)]
    basis = [jnp.dot(own, p, preferred_element_type=jnp.float32) for p in inv_t]
    basis_ref[...] = basis[0] + (basis[1] + basis[2])
    basis_t = dot_exact(inverse, low_t, (((1,), (0,)), ((), ()))).astype(jnp.bfloat16)
    for copy in copies:
        copy.wait()

    def pair(j, carry):
        tile = jnp.concatenate([held[2 * j], held[2 * j + 1]], axis=1)
        cols = jnp.dot(basis_t, tile, preferred_element_type=jnp.float32).astype(jnp.bfloat16)

        out_ref[0, :, pl.ds(pl.multiple_of(order_ref[2 * j] * WIDTH, WIDTH), WIDTH)] = cols[:, :WIDTH]

        @pl.when(2 * j + 1 < count)
        def _():
            at = pl.multiple_of(order_ref[2 * j + 1] * WIDTH, WIDTH)
            out_ref[0, :, pl.ds(at, WIDTH)] = cols[:, WIDTH:]

        return carry

    lax.fori_loop(0, (count + 1) // 2, pair, 0)


def project_pass(flags, low, tiles, own_rows):
    panels, rows, _ = tiles.shape
    rank = low.shape[1]
    return pl.pallas_call(
        functools.partial(project_kernel, panels=panels, own_rows=own_rows),
        grid_spec=pltpu.PrefetchScalarGridSpec(
            num_scalar_prefetch=1,
            grid=(1,),
            in_specs=[
                pl.BlockSpec((rows, rank), lambda i, f: (0, 0)),
                pl.BlockSpec(memory_space=pl.ANY),
            ],
            out_specs=[
                pl.BlockSpec((own_rows, rank), lambda i, f: (0, 0)),
                pl.BlockSpec((1, rank, panels * WIDTH), lambda i, f: (0, 0, 0)),
            ],
            scratch_shapes=[
                pltpu.SMEM((panels + 1,), jnp.int32),
                pltpu.VMEM((panels, rows, WIDTH), jnp.bfloat16),
                pltpu.SemaphoreType.DMA((panels,)),
            ],
        ),
        out_shape=[
            jax.ShapeDtypeStruct((own_rows, rank), jnp.float32),
            jax.ShapeDtypeStruct((1, rank, panels * WIDTH), jnp.bfloat16),
        ],
        compiler_params=pltpu.CompilerParams(vmem_limit_bytes=56 * 2**20),
        name="project_pass",
    )(flags, low, tiles)


def local(row_points, source_points, sketch, admissible):
    tiles_axis = lax.axis_size("tile")
    rows = row_points.shape[1] // lax.axis_size("row")
    rank = sketch.shape[1]
    own_rows = rows // tiles_axis
    flags = admissible[0]
    part, tiles = sketch_pass(flags, row_points, source_points, sketch, rows)
    part = part.reshape(tiles_axis, own_rows, rank)
    parts = lax.all_to_all(part, "tile", 0, 0, tiled=True)
    copies = sum_copies(parts)
    low = lax.all_to_all(copies, "tile", 0, 0, tiled=True).reshape(rows, rank)
    basis, projected = project_pass(flags, low, tiles, own_rows)
    return basis, projected


def solution(mesh):
    in_specs = (P(), P(None, "tile"), P("tile", None), P("row", "tile"))
    out_specs = (P(("row", "tile"), None), P("row", None, "tile"))
    return jax.shard_map(local, mesh=mesh, in_specs=in_specs, out_specs=out_specs, check_vma=False)
```

```python
import functools
import math

import jax
import jax.numpy as jnp
from jax import lax
from jax.experimental import pallas as pl
from jax.experimental.pallas import tpu as pltpu
from jax.sharding import PartitionSpec as P

DAMPING = 0.25
WAVENUM = 24.0
SHIFT = 0.0001

TURNS = WAVENUM / (2.0 * math.pi)
DECAY = -DAMPING / TURNS / math.log(2.0)
AMP = TURNS / (4.0 * math.pi)
S0, S1, S2 = 6.28127979 * AMP, -41.0952178 * AMP, 73.5851113 * AMP

WIDTH = 128
PAIR = 2 * WIDTH
TERMS = 32
SUB = 8
PIECE = 32


def head(x):
    return x.astype(jnp.bfloat16).astype(jnp.float32)


def three(x):
    a = head(x)
    b = head(x - a)
    return a, b, x - a - b


def fill_terms(ref, points, side):
    at = lax.broadcasted_iota(jnp.int32, points.shape, 0)
    x = points - jnp.where(at == 2, -0.5, 3.0)
    scale = TURNS * TURNS
    norm = three(scale * jnp.sum(x * x, axis=0, keepdims=True))
    one = jnp.ones_like(norm[0])
    if side == 0:
        h, m, l = three(x)
        rows = [h, h, m, h, l, m]
        tail = [*norm, one, one, one]
    else:
        h, m, l = three(x * (-2.0 * scale))
        rows = [h, m, h, l, h, m]
        tail = [one, one, one, *norm]
    ref[...] = jnp.zeros_like(ref)
    for at, row in enumerate(rows):
        ref[3 * at : 3 * at + 3, :] = row
    for at, row in enumerate(tail):
        ref[18 + at : 19 + at, :] = row


def near_field(square):
    inv = lax.rsqrt(square)
    t = square * inv
    f = t - jnp.round(t)
    g = 0.25 - jnp.abs(f)
    v = g * g
    wave = ((S2 * v + S1) * v + S0) * g
    amp = jnp.exp2(DECAY * t) * inv
    return (wave * amp).astype(jnp.bfloat16)


def order_panels(flags_ref, order_ref, panels):
    def step(p, count):
        @pl.when(flags_ref[0, p] > 0)
        def _():
            order_ref[count] = p

        return count + (flags_ref[0, p] > 0).astype(jnp.int32)

    count = lax.fori_loop(0, panels, step, jnp.int32(0))
    order_ref[panels] = count
    return count


def prep_kernel(
    flags_hbm, rows_hbm, src_hbm, omega_hbm, order_ref, src_pick, omega_pick, row_mat,
    flags, points, picked, row_terms, src_terms, sources, sems, sem, *, slices, place
):
    panels = flags.shape[1]
    rows = points.shape[1]
    me = lax.axis_index("tile")
    at = pl.multiple_of(lax.axis_index("row") * rows, rows) if place else 0
    copies = [
        pltpu.make_async_copy(flags_hbm, flags, sems.at[0]),
        pltpu.make_async_copy(rows_hbm.at[:, pl.ds(at, rows)], points, sems.at[1]),
        pltpu.make_async_copy(src_hbm, sources, sems.at[2]),
    ]
    for copy in copies:
        copy.start()
    copies[0].wait()
    count = order_panels(flags, order_ref, panels)

    def fetch(slot):
        at = pl.multiple_of(order_ref[slot] * WIDTH, WIDTH)
        to = pl.multiple_of(slot * WIDTH, WIDTH)
        return pltpu.make_async_copy(
            omega_hbm.at[pl.ds(at, WIDTH), :], omega_pick.at[pl.ds(to, WIDTH), :], sem
        )

    def start(slot, carry):
        fetch(slot).start()
        return carry

    lax.fori_loop(0, count, start, 0)
    copies[1].wait()
    if place:
        to = 0
        for k, first, size in slices:
            at = pl.multiple_of((me ^ k) * (rows // lax.axis_size("tile")) + first, WIDTH)
            picked[:, to : to + size] = points[:, pl.ds(at, size)]
            to += size
        fill_terms(row_terms, picked[...], 0)
    else:
        fill_terms(row_terms, points[...], 0)
    step = min(512, rows)
    for r in range(0, rows, step):
        row_mat[r : r + step, :] = row_terms[:, r : r + step].T.astype(jnp.bfloat16)
    copies[2].wait()
    fill_terms(src_terms, sources[...], 1)

    def pick(slot, carry):
        at = pl.multiple_of(order_ref[slot] * WIDTH, WIDTH)
        to = pl.multiple_of(slot * WIDTH, WIDTH)
        src_pick[:, pl.ds(to, WIDTH)] = src_terms[:, pl.ds(at, WIDTH)].astype(jnp.bfloat16)
        return carry

    lax.fori_loop(0, count, pick, 0)
    spare = src_terms[:, :WIDTH].astype(jnp.bfloat16)

    def pad(slot, carry):
        to = pl.multiple_of(slot * WIDTH, WIDTH)
        src_pick[:, pl.ds(to, WIDTH)] = spare
        omega_pick[pl.ds(to, WIDTH), :] = jnp.zeros((WIDTH, omega_pick.shape[1]), jnp.bfloat16)
        return carry

    lax.fori_loop(count, 4 * ((count + 3) // 4) + 2, pad, 0)

    def finish(slot, carry):
        fetch(slot).wait()
        return carry

    lax.fori_loop(0, count, finish, 0)


def in_hbm(x):
    return pltpu.with_memory_space_constraint(x, pltpu.HBM)


def prep(admissible, points, source_points, sketch, rows, slices, place):
    panels = admissible.shape[1]
    cols, rank = sketch.shape
    spare = cols + 4 * WIDTH
    hbm = pl.BlockSpec(memory_space=pltpu.HBM)
    vmem = pl.BlockSpec(memory_space=pltpu.VMEM)
    return pl.pallas_call(
        functools.partial(prep_kernel, slices=slices, place=place),
        in_specs=[hbm] * 4,
        out_specs=[pl.BlockSpec(memory_space=pltpu.SMEM), vmem, vmem, vmem],
        out_shape=[
            jax.ShapeDtypeStruct((panels + 8,), jnp.int32),
            jax.ShapeDtypeStruct((TERMS, spare), jnp.bfloat16),
            jax.ShapeDtypeStruct((spare, rank), jnp.bfloat16),
            jax.ShapeDtypeStruct((rows, TERMS), jnp.bfloat16),
        ],
        scratch_shapes=[
            pltpu.SMEM((1, panels), jnp.int32),
            pltpu.VMEM((3, rows), jnp.float32),
            pltpu.VMEM((3, rows), jnp.float32),
            pltpu.VMEM((TERMS, rows), jnp.float32),
            pltpu.VMEM((TERMS, cols), jnp.float32),
            pltpu.VMEM((3, cols), jnp.float32),
            pltpu.SemaphoreType.DMA((3,)),
            pltpu.SemaphoreType.DMA,
        ],
        compiler_params=pltpu.CompilerParams(vmem_limit_bytes=16 * 2**20),
        name="prep",
    )(*(in_hbm(x) for x in (admissible, points, source_points, sketch)))


def sketch_kernel(
    order_ref, src_pick, omega_pick, row_mat, part_ref, tiles_hbm,
    squares, tiles, total, sems, *, first, panels, rb
):
    pairs = 2 * ((order_ref[panels] + 3) // 4)

    def block(b, carry):
        here = pl.ds(pl.multiple_of(b * rb, rb), rb)
        rows = row_mat[pl.ds(pl.multiple_of(first + b * rb, rb), rb), :]
        total[...] = jnp.zeros_like(total)
        tiles[1] = jnp.zeros(tiles.shape[1:], tiles.dtype)

        def square_of(j):
            src = src_pick[:, pl.ds(pl.multiple_of(j * PAIR, PAIR), PAIR)]
            return jnp.dot(rows, src, preferred_element_type=jnp.float32)

        def add(j, slot):
            omega = omega_pick[pl.ds(pl.multiple_of(j * PAIR, PAIR), PAIR), :]
            tile = jnp.concatenate([tiles[slot, 0], tiles[slot, 1]], axis=1)
            total[...] += jnp.dot(tile, omega, preferred_element_type=jnp.float32)

        def keep(j, slot):
            return pltpu.make_async_copy(
                tiles.at[slot], tiles_hbm.at[pl.ds(2 * j, 2), here, :], sems.at[slot]
            )

        squares[0] = square_of(0)

        def body(j, slot):
            @pl.when(j >= 2)
            def _():
                keep(j - 2, slot).wait()

            add(jnp.maximum(j - 1, 0), 1 - slot)
            squares[1 - slot] = square_of(j + 1)
            for r in range(0, rb, PIECE):
                part = slice(r, r + PIECE)
                tile = near_field(squares[slot, part, :])
                tiles[slot, 0, part, :] = tile[:, :WIDTH]
                tiles[slot, 1, part, :] = tile[:, WIDTH:]
            keep(j, slot).start()

        def two(i, carry):
            body(2 * i, 0)
            body(2 * i + 1, 1)
            return carry

        lax.fori_loop(0, pairs // 2, two, 0)

        @pl.when(pairs > 0)
        def _():
            add(pairs - 1, 1)
            keep(pairs - 2, 0).wait()
            keep(pairs - 1, 1).wait()

        part_ref[here, :] = total[...]
        return carry

    lax.fori_loop(0, part_ref.shape[0] // rb, block, 0)


def sketch_pass(order, src_pick, omega_pick, row_mat, first, rows, panels):
    rank = omega_pick.shape[1]
    rb = min(512, rows)
    vmem = pl.BlockSpec(memory_space=pltpu.VMEM)
    return pl.pallas_call(
        functools.partial(sketch_kernel, first=first, panels=panels, rb=rb),
        in_specs=[pl.BlockSpec(memory_space=pltpu.SMEM), vmem, vmem, vmem],
        out_specs=[vmem, pl.BlockSpec(memory_space=pltpu.HBM)],
        out_shape=[
            jax.ShapeDtypeStruct((rows, rank), jnp.float32),
            pltpu.HBM((4 * ((panels + 3) // 4), rows, WIDTH), jnp.bfloat16),
        ],
        scratch_shapes=[
            pltpu.VMEM((2, rb, PAIR), jnp.float32),
            pltpu.VMEM((2, 2, rb, WIDTH), jnp.bfloat16),
            pltpu.VMEM((rb, rank), jnp.float32),
            pltpu.SemaphoreType.DMA((2,)),
        ],
        compiler_params=pltpu.CompilerParams(vmem_limit_bytes=16 * 2**20),
        cost_estimate=pl.CostEstimate(
            flops=rows * panels * WIDTH * rank * 16, bytes_accessed=rows * panels * WIDTH * 2, transcendentals=0
        ),
        name="sketch_pass",
    )(order, src_pick, omega_pick, row_mat)


def pair_sum_kernel(own_ref, got_ref, kept_ref, *sent_refs):
    q = kept_ref.shape[0]
    for k in range(1 + len(sent_refs)):
        part = slice(k * q, (k + 1) * q)
        value = own_ref[part, :] + got_ref[part, :].astype(jnp.float32)
        if k == 0:
            kept_ref[...] = value
        else:
            sent_refs[k - 1][...] = value.astype(jnp.bfloat16)


def pair_sum(own, got, slots):
    q, rank = own.shape[0] // slots, own.shape[1]
    shapes = [jax.ShapeDtypeStruct((q, rank), jnp.float32)]
    shapes += [jax.ShapeDtypeStruct((q, rank), jnp.bfloat16)] * (slots - 1)
    return pl.pallas_call(pair_sum_kernel, out_shape=shapes, name="pair_sum")(own, got)


def row_sum_kernel(kept_ref, *refs):
    total = kept_ref[...]
    for ref in refs[:-1]:
        total = total + ref[...].astype(jnp.float32)
    refs[-1][...] = total.astype(jnp.bfloat16)


def row_sum(kept, got):
    shape = jax.ShapeDtypeStruct(kept.shape, jnp.bfloat16)
    return pl.pallas_call(row_sum_kernel, out_shape=shape, name="row_sum")(kept, *got)


def invert_factor(gram):
    n = gram.shape[0]
    pieces = n // SUB
    lane = lax.broadcasted_iota(jnp.int32, (SUB, n), 1)
    sub = lax.broadcasted_iota(jnp.int32, (SUB, n), 0)
    trace = jnp.zeros((SUB, n), jnp.float32)
    for v in range(pieces):
        trace = trace + jnp.where(lane == sub + v * SUB, gram[v * SUB : (v + 1) * SUB, :], 0.0)
    shift = (SHIFT / n) * jnp.sum(trace)
    a = [
        gram[v * SUB : (v + 1) * SUB, :] + jnp.where(lane == sub + v * SUB, shift, 0.0)
        for v in range(pieces)
    ]
    for b in range(pieces):
        cols = [
            {v: jnp.broadcast_to(a[v][:, b * SUB + c : b * SUB + c + 1], (SUB, n)) for v in range(b, pieces)}
            for c in range(SUB)
        ]
        for c in range(SUB):
            j = b * SUB + c
            pivot = jnp.broadcast_to(cols[c][b][c : c + 1, :], (SUB, n))
            inv = 1.0 / pivot
            row = jnp.broadcast_to(a[b][c : c + 1, :], (SUB, n))
            row = jnp.where(lane == j, 1.0, row)
            nexts = {
                c2: jnp.broadcast_to(cols[c2][b][c : c + 1, :], (SUB, n)) for c2 in range(c + 1, SUB)
            }
            for v in range(b, pieces):
                m = cols[c][v] * inv
                here = lane == j
                if v == b:
                    m = jnp.where(sub > c, m, 0.0)
                    here = here & (sub > c)
                a[v] = jnp.where(here, 0.0, a[v]) - m * row
                for c2 in range(c + 1, SUB):
                    cols[c2][v] = cols[c2][v] - m * nexts[c2]
    out = []
    for v in range(pieces):
        diag = lane == sub + v * SUB
        d = jnp.sum(jnp.where(diag, a[v], 0.0), axis=1, keepdims=True)
        low = jnp.where(lane < sub + v * SUB, a[v], jnp.where(diag, 1.0, 0.0))
        out.append(low * lax.rsqrt(d))
    return jnp.concatenate(out, axis=0)


def project_kernel(order_ref, *refs, panels, calls, own_at):
    low_refs = refs[: -(calls + 5)]
    tiles_hbm = refs[-(calls + 5) : -5]
    basis_ref, out_ref, low_all, held, sems = refs[-5:]
    per_call = tiles_hbm[0].shape[1]
    copies = [
        pltpu.make_async_copy(
            tiles_hbm[i], held.at[:, i * per_call : (i + 1) * per_call, :], sems.at[i]
        )
        for i in range(calls)
    ]
    for copy in copies:
        copy.start()
    count = order_ref[panels]
    out_ref[...] = jnp.zeros_like(out_ref)
    q = low_refs[0].shape[0]
    for i, ref in enumerate(low_refs):
        low_all[i * q : (i + 1) * q, :] = ref[...]
    low = low_all[...]
    low_t = low.T
    gram = jnp.dot(low_t, low, preferred_element_type=jnp.float32)
    inverse = invert_factor(gram)
    inv_t = [p.astype(jnp.bfloat16) for p in three(inverse.T)]
    for i, at in enumerate(own_at):
        own = low_refs[at][...]
        parts = [jnp.dot(own, p, preferred_element_type=jnp.float32) for p in inv_t]
        basis_ref[i * q : (i + 1) * q, :] = parts[0] + (parts[1] + parts[2])
    parts = [
        jnp.dot(p.astype(jnp.bfloat16), low_t, preferred_element_type=jnp.float32)
        for p in three(inverse)
    ]
    basis_t = (parts[0] + (parts[1] + parts[2])).astype(jnp.bfloat16)
    for copy in copies:
        copy.wait()

    def pair(j, carry):
        tile = jnp.concatenate([held[2 * j], held[2 * j + 1]], axis=1)
        cols = jnp.dot(basis_t, tile, preferred_element_type=jnp.float32).astype(jnp.bfloat16)
        at = pl.multiple_of(order_ref[2 * j] * WIDTH, WIDTH)
        out_ref[0, :, pl.ds(at, WIDTH)] = cols[:, :WIDTH]

        @pl.when(2 * j + 1 < count)
        def _():
            at = pl.multiple_of(order_ref[2 * j + 1] * WIDTH, WIDTH)
            out_ref[0, :, pl.ds(at, WIDTH)] = cols[:, WIDTH:]

        return carry

    lax.fori_loop(0, (count + 1) // 2, pair, 0)


def project_pass(order, lows, tiles, own_at, panels):
    rows = sum(t.shape[1] for t in tiles)
    held = tiles[0].shape[0]
    q, rank = lows[0].shape
    vmem = pl.BlockSpec(memory_space=pltpu.VMEM)
    return pl.pallas_call(
        functools.partial(project_kernel, panels=panels, calls=len(tiles), own_at=own_at),
        in_specs=[pl.BlockSpec(memory_space=pltpu.SMEM)]
        + [vmem] * len(lows)
        + [pl.BlockSpec(memory_space=pltpu.HBM)] * len(tiles),
        out_specs=[vmem, vmem],
        out_shape=[
            jax.ShapeDtypeStruct((q * len(own_at), rank), jnp.float32),
            jax.ShapeDtypeStruct((1, rank, panels * WIDTH), jnp.bfloat16),
        ],
        scratch_shapes=[
            pltpu.VMEM((rows, rank), jnp.bfloat16),
            pltpu.VMEM((held, rows, WIDTH), jnp.bfloat16),
            pltpu.SemaphoreType.DMA((len(tiles),)),
        ],
        compiler_params=pltpu.CompilerParams(vmem_limit_bytes=44 * 2**20),
        name="project_pass",
    )(order, *lows, *(in_hbm(x) for x in tiles))


def after(x, *deps):
    return lax.optimization_barrier((x, *deps))[0]


def swap(x, k, n):
    return lax.ppermute(x, "tile", [(i, i ^ k) for i in range(n)])


CHUNKS = 2


def local(row_points, source_points, sketch, admissible):
    n = lax.axis_size("tile")
    panels = admissible.shape[1]
    rows = row_points.shape[1] // lax.axis_size("row")
    own_rows = rows // n
    q = own_rows // CHUNKS
    odd, even = list(range(1, n, 2)), list(range(0, n, 2))
    slices = [(k, c * q, q) for c in range(CHUNKS) for k in odd + even]
    place = q % WIDTH == 0
    points = row_points
    if not place:
        me = lax.axis_index("tile")
        points = lax.dynamic_slice_in_dim(row_points, lax.axis_index("row") * rows, rows, 1)
        points = jnp.concatenate(
            [lax.dynamic_slice_in_dim(points, (me ^ k) * own_rows + first, q, 1) for k, first, _ in slices], 1
        )
    order, src_pick, omega_pick, row_mat = prep(
        admissible, points, source_points, sketch, rows, slices, place
    )

    call_rows = rows // CHUNKS // 2

    def sketch_part(at, *deps):
        return sketch_pass(
            after(order, *deps), src_pick, omega_pick, row_mat, at * call_rows, call_rows, panels
        )

    def sum_cores(got, own):
        kept, *sent = pair_sum(own, got, n // 2)
        return kept, [swap(x, k, n) for x, k in zip(sent, even[1:])]

    def spread(kept, got):
        low = row_sum(kept, got)
        held = [low] + [swap(low, k, n) for k in even[1:]]
        return [swap(x, 1, n) for x in held] + held

    lows, tiles, own_at, waiting = [], [], [], None
    last = ()
    for c in range(CHUNKS):
        theirs, kept = sketch_part(2 * c, *last)
        tiles.append(kept)
        got = swap(theirs, 1, n)
        if waiting is not None:
            lows += spread(after(waiting[0], theirs), waiting[1])
        own, kept = sketch_part(2 * c + 1, theirs, *lows[-n // 2 :][:1])
        tiles.append(kept)
        waiting = sum_cores(got, own)
        last = (own, waiting[0])
    lows += spread(*waiting)
    own_at = [c * n + n // 2 for c in range(CHUNKS)]
    return project_pass(order, lows, tiles, own_at, panels)


def solution(mesh):
    in_specs = (P(), P(None, "tile"), P("tile", None), P("row", "tile"))
    out_specs = (P(("row", "tile"), None), P("row", None, "tile"))
    return jax.shard_map(local, mesh=mesh, in_specs=in_specs, out_specs=out_specs, check_vma=False)
```

```python
import functools
import math

import jax
import jax.numpy as jnp
from jax import lax
from jax.experimental import pallas as pl
from jax.experimental.pallas import tpu as pltpu
from jax.sharding import PartitionSpec as P

DAMPING = 0.25
WAVENUM = 24.0
SHIFT = 0.0001

TURNS = WAVENUM / (2.0 * math.pi)
DECAY = -DAMPING / TURNS / math.log(2.0)
AMP = TURNS / (4.0 * math.pi)
S0, S1, S2 = 6.28127979 * AMP, -41.0952178 * AMP, 73.5851113 * AMP

WIDTH = 128
PAIR = 2 * WIDTH
TERMS = 32
SUB = 8
PIECE = 16
GROUP = 4
WHOLE = 1.5 * 2.0**23


def head(x):
    return x.astype(jnp.bfloat16).astype(jnp.float32)


def three(x):
    a = head(x)
    b = head(x - a)
    return a, b, x - a - b


def fill_terms(ref, points, side):
    at = lax.broadcasted_iota(jnp.int32, points.shape, 0)
    x = points - jnp.where(at == 2, -0.5, 3.0)
    scale = TURNS * TURNS
    norm = three(scale * jnp.sum(x * x, axis=0, keepdims=True))
    one = jnp.ones_like(norm[0])
    if side == 0:
        h, m, l = three(x)
        rows = [h, h, m, h, l, m]
        tail = [*norm, one, one, one]
    else:
        h, m, l = three(x * (-2.0 * scale))
        rows = [h, m, h, l, h, m]
        tail = [one, one, one, *norm]
    ref[...] = jnp.zeros_like(ref)
    for at, row in enumerate(rows):
        ref[3 * at : 3 * at + 3, :] = row
    for at, row in enumerate(tail):
        ref[18 + at : 19 + at, :] = row


def near_field(square):
    inv = lax.rsqrt(square)
    t = square * inv
    f = t - ((t + WHOLE) - WHOLE)
    g = 0.25 - jnp.abs(f)
    v = g * g
    wave = ((S2 * v + S1) * v + S0) * g
    amp = jnp.exp2(DECAY * t) * inv
    return (wave * amp).astype(jnp.bfloat16)


def order_panels(flags_ref, order_ref, panels):
    def step(p, count):
        @pl.when(flags_ref[0, p] > 0)
        def _():
            order_ref[count] = p

        return count + (flags_ref[0, p] > 0).astype(jnp.int32)

    count = lax.fori_loop(0, panels, step, jnp.int32(0))
    order_ref[panels] = count
    return count


def prep_kernel(
    flags_hbm, rows_hbm, src_hbm, omega_hbm, order_ref, src_pick, omega_pick, row_mat,
    flags, points, picked, row_terms, src_terms, sources, sems, sem, *, slices, place
):
    panels = flags.shape[1]
    rows = points.shape[1]
    me = lax.axis_index("tile")
    at = pl.multiple_of(lax.axis_index("row") * rows, rows) if place else 0
    copies = [
        pltpu.make_async_copy(flags_hbm, flags, sems.at[0]),
        pltpu.make_async_copy(rows_hbm.at[:, pl.ds(at, rows)], points, sems.at[1]),
        pltpu.make_async_copy(src_hbm, sources, sems.at[2]),
    ]
    for copy in copies:
        copy.start()
    copies[0].wait()
    count = order_panels(flags, order_ref, panels)

    def fetch(slot):
        at = pl.multiple_of(order_ref[slot] * WIDTH, WIDTH)
        to = pl.multiple_of(slot * WIDTH, WIDTH)
        return pltpu.make_async_copy(
            omega_hbm.at[pl.ds(at, WIDTH), :], omega_pick.at[pl.ds(to, WIDTH), :], sem
        )

    def start(slot, carry):
        fetch(slot).start()
        return carry

    lax.fori_loop(0, count, start, 0)
    copies[1].wait()
    if place:
        to = 0
        for k, first, size in slices:
            at = pl.multiple_of((me ^ k) * (rows // lax.axis_size("tile")) + first, WIDTH)
            picked[:, to : to + size] = points[:, pl.ds(at, size)]
            to += size
        fill_terms(row_terms, picked[...], 0)
    else:
        fill_terms(row_terms, points[...], 0)
    step = min(512, rows)
    for r in range(0, rows, step):
        row_mat[r : r + step, :] = row_terms[:, r : r + step].T.astype(jnp.bfloat16)
    copies[2].wait()
    fill_terms(src_terms, sources[...], 1)

    def pick(slot, carry):
        at = pl.multiple_of(order_ref[slot] * WIDTH, WIDTH)
        to = pl.multiple_of(slot * WIDTH, WIDTH)
        src_pick[:, pl.ds(to, WIDTH)] = src_terms[:, pl.ds(at, WIDTH)].astype(jnp.bfloat16)
        return carry

    lax.fori_loop(0, count, pick, 0)
    spare = src_terms[:, :WIDTH].astype(jnp.bfloat16)

    def pad(slot, carry):
        to = pl.multiple_of(slot * WIDTH, WIDTH)
        src_pick[:, pl.ds(to, WIDTH)] = spare
        omega_pick[pl.ds(to, WIDTH), :] = jnp.zeros((WIDTH, omega_pick.shape[1]), jnp.bfloat16)
        return carry

    lax.fori_loop(count, GROUP * ((count + GROUP - 1) // GROUP), pad, 0)

    def finish(slot, carry):
        fetch(slot).wait()
        return carry

    lax.fori_loop(0, count, finish, 0)


def in_hbm(x):
    return pltpu.with_memory_space_constraint(x, pltpu.HBM)


def prep(admissible, points, source_points, sketch, rows, slices, place):
    panels = admissible.shape[1]
    cols, rank = sketch.shape
    spare = cols + GROUP * WIDTH
    hbm = pl.BlockSpec(memory_space=pltpu.HBM)
    vmem = pl.BlockSpec(memory_space=pltpu.VMEM)
    return pl.pallas_call(
        functools.partial(prep_kernel, slices=slices, place=place),
        in_specs=[hbm] * 4,
        out_specs=[pl.BlockSpec(memory_space=pltpu.SMEM), vmem, vmem, vmem],
        out_shape=[
            jax.ShapeDtypeStruct((panels + 8,), jnp.int32),
            jax.ShapeDtypeStruct((TERMS, spare), jnp.bfloat16),
            jax.ShapeDtypeStruct((spare, rank), jnp.bfloat16),
            jax.ShapeDtypeStruct((rows, TERMS), jnp.bfloat16),
        ],
        scratch_shapes=[
            pltpu.SMEM((1, panels), jnp.int32),
            pltpu.VMEM((3, rows), jnp.float32),
            pltpu.VMEM((3, rows), jnp.float32),
            pltpu.VMEM((TERMS, rows), jnp.float32),
            pltpu.VMEM((TERMS, cols), jnp.float32),
            pltpu.VMEM((3, cols), jnp.float32),
            pltpu.SemaphoreType.DMA((3,)),
            pltpu.SemaphoreType.DMA,
        ],
        compiler_params=pltpu.CompilerParams(vmem_limit_bytes=16 * 2**20),
        name="prep",
    )(*(in_hbm(x) for x in (admissible, points, source_points, sketch)))


def sketch_kernel(
    order_ref, src_pick, omega_pick, row_mat, part_ref, tiles_hbm, tiles, total, sems,
    *, first, panels, rb
):
    groups = (order_ref[panels] + GROUP - 1) // GROUP
    cols = GROUP * WIDTH

    def block(b, carry):
        here = pl.ds(pl.multiple_of(b * rb, rb), rb)
        total[...] = jnp.zeros_like(total)

        def keep(j):
            slot = lax.rem(j, 2)
            return pltpu.make_async_copy(
                tiles.at[slot], tiles_hbm.at[pl.ds(GROUP * j, GROUP), here, :], sems.at[slot]
            )

        def body(j, carry):
            @pl.when(j >= 2)
            def _():
                keep(j - 2).wait()

            rows = row_mat[pl.ds(pl.multiple_of(first + b * rb, rb), rb), :]
            at = pl.ds(pl.multiple_of(j * cols, cols), cols)
            src = src_pick[:, at]
            omega = omega_pick[at, :]
            before = total[...]
            near = []
            for c in range(0, cols, PAIR):
                square = jnp.dot(rows, src[:, c : c + PAIR], preferred_element_type=jnp.float32)
                parts = [near_field(square[r : r + PIECE]) for r in range(0, rb, PIECE)]
                near.append(jnp.concatenate(parts, axis=0))
            tile = jnp.concatenate(near, axis=1)
            total[...] = before + jnp.dot(tile, omega, preferred_element_type=jnp.float32)
            slot = lax.rem(j, 2)
            for k in range(GROUP):
                tiles[slot, k] = tile[:, k * WIDTH : (k + 1) * WIDTH]
            keep(j).start()
            return carry

        lax.fori_loop(0, groups, body, 0)

        @pl.when(groups > 1)
        def _():
            keep(groups - 2).wait()

        @pl.when(groups > 0)
        def _():
            keep(groups - 1).wait()

        part_ref[here, :] = total[...]
        return carry

    lax.fori_loop(0, part_ref.shape[0] // rb, block, 0)


def sketch_pass(order, src_pick, omega_pick, row_mat, first, rows, panels):
    rank = omega_pick.shape[1]
    rb = min(512, rows)
    vmem = pl.BlockSpec(memory_space=pltpu.VMEM)
    return pl.pallas_call(
        functools.partial(sketch_kernel, first=first, panels=panels, rb=rb),
        in_specs=[pl.BlockSpec(memory_space=pltpu.SMEM), vmem, vmem, vmem],
        out_specs=[vmem, pl.BlockSpec(memory_space=pltpu.HBM)],
        out_shape=[
            jax.ShapeDtypeStruct((rows, rank), jnp.float32),
            pltpu.HBM((GROUP * ((panels + GROUP - 1) // GROUP), rows, WIDTH), jnp.bfloat16),
        ],
        scratch_shapes=[
            pltpu.VMEM((2, GROUP, rb, WIDTH), jnp.bfloat16),
            pltpu.VMEM((rb, rank), jnp.float32),
            pltpu.SemaphoreType.DMA((2,)),
        ],
        compiler_params=pltpu.CompilerParams(vmem_limit_bytes=16 * 2**20),
        cost_estimate=pl.CostEstimate(
            flops=rows * panels * WIDTH * rank * 16, bytes_accessed=rows * panels * WIDTH * 2, transcendentals=0
        ),
        name="sketch_pass",
    )(order, src_pick, omega_pick, row_mat)


def pair_sum_kernel(own_ref, got_ref, kept_ref, *sent_refs):
    q = kept_ref.shape[0]
    for k in range(1 + len(sent_refs)):
        part = slice(k * q, (k + 1) * q)
        value = own_ref[part, :] + got_ref[part, :].astype(jnp.float32)
        if k == 0:
            kept_ref[...] = value
        else:
            sent_refs[k - 1][...] = value.astype(jnp.bfloat16)


def pair_sum(own, got, slots):
    q, rank = own.shape[0] // slots, own.shape[1]
    shapes = [jax.ShapeDtypeStruct((q, rank), jnp.float32)]
    shapes += [jax.ShapeDtypeStruct((q, rank), jnp.bfloat16)] * (slots - 1)
    return pl.pallas_call(pair_sum_kernel, out_shape=shapes, name="pair_sum")(own, got)


def row_sum_kernel(kept_ref, *refs):
    total = kept_ref[...]
    for ref in refs[:-1]:
        total = total + ref[...].astype(jnp.float32)
    refs[-1][...] = total.astype(jnp.bfloat16)


def row_sum(kept, got):
    shape = jax.ShapeDtypeStruct(kept.shape, jnp.bfloat16)
    return pl.pallas_call(row_sum_kernel, out_shape=shape, name="row_sum")(kept, *got)


def invert_factor(gram):
    n = gram.shape[0]
    pieces = n // SUB
    lane = lax.broadcasted_iota(jnp.int32, (SUB, n), 1)
    sub = lax.broadcasted_iota(jnp.int32, (SUB, n), 0)
    trace = jnp.zeros((SUB, n), jnp.float32)
    for v in range(pieces):
        trace = trace + jnp.where(lane == sub + v * SUB, gram[v * SUB : (v + 1) * SUB, :], 0.0)
    shift = (SHIFT / n) * jnp.sum(trace)
    a = [
        gram[v * SUB : (v + 1) * SUB, :] + jnp.where(lane == sub + v * SUB, shift, 0.0)
        for v in range(pieces)
    ]
    for b in range(pieces):
        cols = [
            {v: jnp.broadcast_to(a[v][:, b * SUB + c : b * SUB + c + 1], (SUB, n)) for v in range(b, pieces)}
            for c in range(SUB)
        ]
        for c in range(SUB):
            j = b * SUB + c
            pivot = jnp.broadcast_to(cols[c][b][c : c + 1, :], (SUB, n))
            inv = 1.0 / pivot
            row = jnp.broadcast_to(a[b][c : c + 1, :], (SUB, n))
            row = jnp.where(lane == j, 1.0, row)
            nexts = {
                c2: jnp.broadcast_to(cols[c2][b][c : c + 1, :], (SUB, n)) for c2 in range(c + 1, SUB)
            }
            for v in range(b, pieces):
                m = cols[c][v] * inv
                here = lane == j
                if v == b:
                    m = jnp.where(sub > c, m, 0.0)
                    here = here & (sub > c)
                a[v] = jnp.where(here, 0.0, a[v]) - m * row
                for c2 in range(c + 1, SUB):
                    cols[c2][v] = cols[c2][v] - m * nexts[c2]
    out = []
    for v in range(pieces):
        diag = lane == sub + v * SUB
        d = jnp.sum(jnp.where(diag, a[v], 0.0), axis=1, keepdims=True)
        low = jnp.where(lane < sub + v * SUB, a[v], jnp.where(diag, 1.0, 0.0))
        out.append(low * lax.rsqrt(d))
    return jnp.concatenate(out, axis=0)


def project_kernel(order_ref, *refs, panels, calls, own_at):
    low_refs = refs[: -(calls + 5)]
    tiles_hbm = refs[-(calls + 5) : -5]
    basis_ref, out_ref, low_all, held, sems = refs[-5:]
    per_call = tiles_hbm[0].shape[1]
    copies = [
        pltpu.make_async_copy(
            tiles_hbm[i], held.at[:, i * per_call : (i + 1) * per_call, :], sems.at[i]
        )
        for i in range(calls)
    ]
    for copy in copies:
        copy.start()
    count = order_ref[panels]
    out_ref[...] = jnp.zeros_like(out_ref)
    q = low_refs[0].shape[0]
    for i, ref in enumerate(low_refs):
        low_all[i * q : (i + 1) * q, :] = ref[...]
    low = low_all[...]
    low_t = low.T
    gram = jnp.dot(low_t, low, preferred_element_type=jnp.float32)
    inverse = invert_factor(gram)
    inv_t = [p.astype(jnp.bfloat16) for p in three(inverse.T)]
    for i, at in enumerate(own_at):
        own = low_refs[at][...]
        parts = [jnp.dot(own, p, preferred_element_type=jnp.float32) for p in inv_t]
        basis_ref[i * q : (i + 1) * q, :] = parts[0] + (parts[1] + parts[2])
    parts = [
        jnp.dot(p.astype(jnp.bfloat16), low_t, preferred_element_type=jnp.float32)
        for p in three(inverse)
    ]
    basis_t = (parts[0] + (parts[1] + parts[2])).astype(jnp.bfloat16)
    for copy in copies:
        copy.wait()

    def pair(j, carry):
        tile = jnp.concatenate([held[2 * j], held[2 * j + 1]], axis=1)
        cols = jnp.dot(basis_t, tile, preferred_element_type=jnp.float32).astype(jnp.bfloat16)
        at = pl.multiple_of(order_ref[2 * j] * WIDTH, WIDTH)
        out_ref[0, :, pl.ds(at, WIDTH)] = cols[:, :WIDTH]

        @pl.when(2 * j + 1 < count)
        def _():
            at = pl.multiple_of(order_ref[2 * j + 1] * WIDTH, WIDTH)
            out_ref[0, :, pl.ds(at, WIDTH)] = cols[:, WIDTH:]

        return carry

    lax.fori_loop(0, (count + 1) // 2, pair, 0)


def project_pass(order, lows, tiles, own_at, panels):
    rows = sum(t.shape[1] for t in tiles)
    held = tiles[0].shape[0]
    q, rank = lows[0].shape
    vmem = pl.BlockSpec(memory_space=pltpu.VMEM)
    return pl.pallas_call(
        functools.partial(project_kernel, panels=panels, calls=len(tiles), own_at=own_at),
        in_specs=[pl.BlockSpec(memory_space=pltpu.SMEM)]
        + [vmem] * len(lows)
        + [pl.BlockSpec(memory_space=pltpu.HBM)] * len(tiles),
        out_specs=[vmem, vmem],
        out_shape=[
            jax.ShapeDtypeStruct((q * len(own_at), rank), jnp.float32),
            jax.ShapeDtypeStruct((1, rank, panels * WIDTH), jnp.bfloat16),
        ],
        scratch_shapes=[
            pltpu.VMEM((rows, rank), jnp.bfloat16),
            pltpu.VMEM((held, rows, WIDTH), jnp.bfloat16),
            pltpu.SemaphoreType.DMA((len(tiles),)),
        ],
        compiler_params=pltpu.CompilerParams(vmem_limit_bytes=44 * 2**20),
        name="project_pass",
    )(order, *lows, *(in_hbm(x) for x in tiles))


def after(x, *deps):
    return lax.optimization_barrier((x, *deps))[0]


def swap(x, k, n):
    return lax.ppermute(x, "tile", [(i, i ^ k) for i in range(n)])


CHUNKS = 2


def local(row_points, source_points, sketch, admissible):
    n = lax.axis_size("tile")
    panels = admissible.shape[1]
    rows = row_points.shape[1] // lax.axis_size("row")
    own_rows = rows // n
    q = own_rows // CHUNKS
    odd, even = list(range(1, n, 2)), list(range(0, n, 2))
    slices = [(k, c * q, q) for c in range(CHUNKS) for k in odd + even]
    place = q % WIDTH == 0
    points = row_points
    if not place:
        me = lax.axis_index("tile")
        points = lax.dynamic_slice_in_dim(row_points, lax.axis_index("row") * rows, rows, 1)
        points = jnp.concatenate(
            [lax.dynamic_slice_in_dim(points, (me ^ k) * own_rows + first, q, 1) for k, first, _ in slices], 1
        )
    order, src_pick, omega_pick, row_mat = prep(
        admissible, points, source_points, sketch, rows, slices, place
    )

    call_rows = rows // CHUNKS // 2

    def sketch_part(at, *deps):
        return sketch_pass(
            after(order, *deps), src_pick, omega_pick, row_mat, at * call_rows, call_rows, panels
        )

    def sum_cores(got, own):
        kept, *sent = pair_sum(own, got, n // 2)
        return kept, [swap(x, k, n) for x, k in zip(sent, even[1:])]

    def spread(kept, got):
        low = row_sum(kept, got)
        held = [low] + [swap(low, k, n) for k in even[1:]]
        return [swap(x, 1, n) for x in held] + held

    lows, tiles, own_at, waiting = [], [], [], None
    last = ()
    for c in range(CHUNKS):
        theirs, kept = sketch_part(2 * c, *last)
        tiles.append(kept)
        got = swap(theirs, 1, n)
        if waiting is not None:
            lows += spread(after(waiting[0], theirs), waiting[1])
        own, kept = sketch_part(2 * c + 1, theirs, *lows[-n // 2 :][:1])
        tiles.append(kept)
        waiting = sum_cores(got, own)
        last = (own, waiting[0])
    lows += spread(*waiting)
    own_at = [c * n + n // 2 for c in range(CHUNKS)]
    return project_pass(order, lows, tiles, own_at, panels)


def solution(mesh):
    in_specs = (P(), P(None, "tile"), P("tile", None), P("row", "tile"))
    out_specs = (P(("row", "tile"), None), P("row", None, "tile"))
    return jax.shard_map(local, mesh=mesh, in_specs=in_specs, out_specs=out_specs, check_vma=False)
```

```python
import functools
import math

import jax
import jax.numpy as jnp
from jax import lax
from jax.experimental import pallas as pl
from jax.experimental.pallas import tpu as pltpu
from jax.sharding import PartitionSpec as P

DAMPING = 0.25
WAVENUM = 24.0
SHIFT = 0.0001

TURNS = WAVENUM / (2.0 * math.pi)
DECAY = -DAMPING / TURNS / math.log(2.0)
AMP = TURNS / (4.0 * math.pi)
S0, S1, S2 = 6.28127979 * AMP, -41.0952178 * AMP, 73.5851113 * AMP

WIDTH = 128
PAIR = 2 * WIDTH
TERMS = 32
SUB = 8
PIECE = 16
GROUP = 4
WHOLE = 1.5 * 2.0**23


def head(x):
    return x.astype(jnp.bfloat16).astype(jnp.float32)


def three(x):
    a = head(x)
    b = head(x - a)
    return a, b, x - a - b


def fill_terms(ref, points, side):
    at = lax.broadcasted_iota(jnp.int32, points.shape, 0)
    x = points - jnp.where(at == 2, -0.5, 3.0)
    scale = TURNS * TURNS
    norm = three(scale * jnp.sum(x * x, axis=0, keepdims=True))
    one = jnp.ones_like(norm[0])
    if side == 0:
        h, m, l = three(x)
        rows = [h, h, m, h, l, m]
        tail = [*norm, one, one, one]
    else:
        h, m, l = three(x * (-2.0 * scale))
        rows = [h, m, h, l, h, m]
        tail = [one, one, one, *norm]
    ref[...] = jnp.zeros_like(ref)
    for at, row in enumerate(rows):
        ref[3 * at : 3 * at + 3, :] = row
    for at, row in enumerate(tail):
        ref[18 + at : 19 + at, :] = row


def near_field(square):
    inv = lax.rsqrt(square)
    t = square * inv
    f = t - ((t + WHOLE) - WHOLE)
    g = 0.25 - jnp.abs(f)
    v = g * g
    wave = ((S2 * v + S1) * v + S0) * g
    amp = jnp.exp2(DECAY * t) * inv
    return (wave * amp).astype(jnp.bfloat16)


def order_panels(flags_ref, order_ref, panels):
    def step(p, count):
        @pl.when(flags_ref[0, p] > 0)
        def _():
            order_ref[count] = p

        return count + (flags_ref[0, p] > 0).astype(jnp.int32)

    count = lax.fori_loop(0, panels, step, jnp.int32(0))
    order_ref[panels] = count
    return count


def prep_kernel(
    flags_hbm, rows_hbm, src_hbm, omega_hbm, order_ref, src_pick, omega_pick, row_mat,
    flags, points, picked, row_terms, src_terms, sources, sems, sem, *, slices, place
):
    panels = flags.shape[1]
    rows = points.shape[1]
    me = lax.axis_index("tile")
    at = pl.multiple_of(lax.axis_index("row") * rows, rows) if place else 0
    copies = [
        pltpu.make_async_copy(flags_hbm, flags, sems.at[0]),
        pltpu.make_async_copy(rows_hbm.at[:, pl.ds(at, rows)], points, sems.at[1]),
        pltpu.make_async_copy(src_hbm, sources, sems.at[2]),
    ]
    for copy in copies:
        copy.start()
    copies[0].wait()
    count = order_panels(flags, order_ref, panels)

    def fetch(slot):
        at = pl.multiple_of(order_ref[slot] * WIDTH, WIDTH)
        to = pl.multiple_of(slot * WIDTH, WIDTH)
        return pltpu.make_async_copy(
            omega_hbm.at[pl.ds(at, WIDTH), :], omega_pick.at[pl.ds(to, WIDTH), :], sem
        )

    def start(slot, carry):
        fetch(slot).start()
        return carry

    lax.fori_loop(0, count, start, 0)
    copies[1].wait()
    if place:
        to = 0
        for k, first, size in slices:
            at = pl.multiple_of((me ^ k) * (rows // lax.axis_size("tile")) + first, WIDTH)
            picked[:, to : to + size] = points[:, pl.ds(at, size)]
            to += size
        fill_terms(row_terms, picked[...], 0)
    else:
        fill_terms(row_terms, points[...], 0)
    step = min(512, rows)
    for r in range(0, rows, step):
        row_mat[r : r + step, :] = row_terms[:, r : r + step].T.astype(jnp.bfloat16)
    copies[2].wait()
    fill_terms(src_terms, sources[...], 1)

    def pick(slot, carry):
        at = pl.multiple_of(order_ref[slot] * WIDTH, WIDTH)
        to = pl.multiple_of(slot * WIDTH, WIDTH)
        src_pick[:, pl.ds(to, WIDTH)] = src_terms[:, pl.ds(at, WIDTH)].astype(jnp.bfloat16)
        return carry

    lax.fori_loop(0, count, pick, 0)
    spare = src_terms[:, :WIDTH].astype(jnp.bfloat16)

    def pad(slot, carry):
        to = pl.multiple_of(slot * WIDTH, WIDTH)
        src_pick[:, pl.ds(to, WIDTH)] = spare
        omega_pick[pl.ds(to, WIDTH), :] = jnp.zeros((WIDTH, omega_pick.shape[1]), jnp.bfloat16)
        return carry

    lax.fori_loop(count, GROUP * ((count + GROUP - 1) // GROUP + 1), pad, 0)

    def finish(slot, carry):
        fetch(slot).wait()
        return carry

    lax.fori_loop(0, count, finish, 0)


def in_hbm(x):
    return pltpu.with_memory_space_constraint(x, pltpu.HBM)


def prep(admissible, points, source_points, sketch, rows, slices, place):
    panels = admissible.shape[1]
    cols, rank = sketch.shape
    spare = cols + 2 * GROUP * WIDTH
    hbm = pl.BlockSpec(memory_space=pltpu.HBM)
    vmem = pl.BlockSpec(memory_space=pltpu.VMEM)
    return pl.pallas_call(
        functools.partial(prep_kernel, slices=slices, place=place),
        in_specs=[hbm] * 4,
        out_specs=[pl.BlockSpec(memory_space=pltpu.SMEM), vmem, vmem, vmem],
        out_shape=[
            jax.ShapeDtypeStruct((panels + 8,), jnp.int32),
            jax.ShapeDtypeStruct((TERMS, spare), jnp.bfloat16),
            jax.ShapeDtypeStruct((spare, rank), jnp.bfloat16),
            jax.ShapeDtypeStruct((rows, TERMS), jnp.bfloat16),
        ],
        scratch_shapes=[
            pltpu.SMEM((1, panels), jnp.int32),
            pltpu.VMEM((3, rows), jnp.float32),
            pltpu.VMEM((3, rows), jnp.float32),
            pltpu.VMEM((TERMS, rows), jnp.float32),
            pltpu.VMEM((TERMS, cols), jnp.float32),
            pltpu.VMEM((3, cols), jnp.float32),
            pltpu.SemaphoreType.DMA((3,)),
            pltpu.SemaphoreType.DMA,
        ],
        compiler_params=pltpu.CompilerParams(vmem_limit_bytes=16 * 2**20),
        name="prep",
    )(*(in_hbm(x) for x in (admissible, points, source_points, sketch)))


def sketch_kernel(
    order_ref, src_pick, omega_pick, row_mat, part_ref, tiles_hbm, squares, tiles, total, sems,
    *, first, panels, rb
):
    groups = (order_ref[panels] + GROUP - 1) // GROUP
    cols = GROUP * WIDTH

    def block(b, carry):
        here = pl.ds(pl.multiple_of(b * rb, rb), rb)
        total[...] = jnp.zeros_like(total)
        tiles[1] = jnp.zeros(tiles.shape[1:], tiles.dtype)

        def columns(j):
            return pl.ds(pl.multiple_of(j * cols, cols), cols)

        def square_of(j):
            rows = row_mat[pl.ds(pl.multiple_of(first + b * rb, rb), rb), :]
            return jnp.dot(rows, src_pick[:, columns(j)], preferred_element_type=jnp.float32)

        def add(j, slot):
            tile = jnp.concatenate([tiles[slot, k] for k in range(GROUP)], axis=1)
            omega = omega_pick[columns(j), :]
            return total[...] + jnp.dot(tile, omega, preferred_element_type=jnp.float32)

        def keep(j):
            slot = lax.rem(j, 2)
            return pltpu.make_async_copy(
                tiles.at[slot], tiles_hbm.at[pl.ds(GROUP * j, GROUP), here, :], sems.at[slot]
            )

        squares[...] = square_of(0)

        def body(j, carry):
            @pl.when(j >= 2)
            def _():
                keep(j - 2).wait()

            slot = lax.rem(j, 2)
            square = squares[...]
            sums = add(jnp.maximum(j - 1, 0), 1 - slot)
            later = square_of(j + 1)
            near = [near_field(square[r : r + PIECE]) for r in range(0, rb, PIECE)]
            total[...] = sums
            squares[...] = later
            for r, piece in zip(range(0, rb, PIECE), near):
                for k in range(GROUP):
                    tiles[slot, k, r : r + PIECE, :] = piece[:, k * WIDTH : (k + 1) * WIDTH]
            keep(j).start()
            return carry

        lax.fori_loop(0, groups, body, 0)

        @pl.when(groups > 1)
        def _():
            keep(groups - 2).wait()

        @pl.when(groups > 0)
        def _():
            keep(groups - 1).wait()
            total[...] = add(groups - 1, lax.rem(groups - 1, 2))

        part_ref[here, :] = total[...]
        return carry

    lax.fori_loop(0, part_ref.shape[0] // rb, block, 0)


def sketch_pass(order, src_pick, omega_pick, row_mat, first, rows, panels):
    rank = omega_pick.shape[1]
    rb = min(512, rows)
    vmem = pl.BlockSpec(memory_space=pltpu.VMEM)
    return pl.pallas_call(
        functools.partial(sketch_kernel, first=first, panels=panels, rb=rb),
        in_specs=[pl.BlockSpec(memory_space=pltpu.SMEM), vmem, vmem, vmem],
        out_specs=[vmem, pl.BlockSpec(memory_space=pltpu.HBM)],
        out_shape=[
            jax.ShapeDtypeStruct((rows, rank), jnp.float32),
            pltpu.HBM((GROUP * ((panels + GROUP - 1) // GROUP), rows, WIDTH), jnp.bfloat16),
        ],
        scratch_shapes=[
            pltpu.VMEM((rb, GROUP * WIDTH), jnp.float32),
            pltpu.VMEM((2, GROUP, rb, WIDTH), jnp.bfloat16),
            pltpu.VMEM((rb, rank), jnp.float32),
            pltpu.SemaphoreType.DMA((2,)),
        ],
        compiler_params=pltpu.CompilerParams(vmem_limit_bytes=16 * 2**20),
        cost_estimate=pl.CostEstimate(
            flops=rows * panels * WIDTH * rank * 16, bytes_accessed=rows * panels * WIDTH * 2, transcendentals=0
        ),
        name="sketch_pass",
    )(order, src_pick, omega_pick, row_mat)


def pair_sum_kernel(own_ref, got_ref, kept_ref, *sent_refs):
    q = kept_ref.shape[0]
    for k in range(1 + len(sent_refs)):
        part = slice(k * q, (k + 1) * q)
        value = own_ref[part, :] + got_ref[part, :].astype(jnp.float32)
        if k == 0:
            kept_ref[...] = value
        else:
            sent_refs[k - 1][...] = value.astype(jnp.bfloat16)


def pair_sum(own, got, slots):
    q, rank = own.shape[0] // slots, own.shape[1]
    shapes = [jax.ShapeDtypeStruct((q, rank), jnp.float32)]
    shapes += [jax.ShapeDtypeStruct((q, rank), jnp.bfloat16)] * (slots - 1)
    return pl.pallas_call(pair_sum_kernel, out_shape=shapes, name="pair_sum")(own, got)


def row_sum_kernel(kept_ref, *refs):
    total = kept_ref[...]
    for ref in refs[:-1]:
        total = total + ref[...].astype(jnp.float32)
    refs[-1][...] = total.astype(jnp.bfloat16)


def row_sum(kept, got):
    shape = jax.ShapeDtypeStruct(kept.shape, jnp.bfloat16)
    return pl.pallas_call(row_sum_kernel, out_shape=shape, name="row_sum")(kept, *got)


def invert_factor(gram):
    n = gram.shape[0]
    pieces = n // SUB
    lane = lax.broadcasted_iota(jnp.int32, (SUB, n), 1)
    sub = lax.broadcasted_iota(jnp.int32, (SUB, n), 0)
    trace = jnp.zeros((SUB, n), jnp.float32)
    for v in range(pieces):
        trace = trace + jnp.where(lane == sub + v * SUB, gram[v * SUB : (v + 1) * SUB, :], 0.0)
    shift = (SHIFT / n) * jnp.sum(trace)
    a = [
        gram[v * SUB : (v + 1) * SUB, :] + jnp.where(lane == sub + v * SUB, shift, 0.0)
        for v in range(pieces)
    ]
    for b in range(pieces):
        cols = [
            {v: jnp.broadcast_to(a[v][:, b * SUB + c : b * SUB + c + 1], (SUB, n)) for v in range(b, pieces)}
            for c in range(SUB)
        ]
        for c in range(SUB):
            j = b * SUB + c
            pivot = jnp.broadcast_to(cols[c][b][c : c + 1, :], (SUB, n))
            inv = 1.0 / pivot
            row = jnp.broadcast_to(a[b][c : c + 1, :], (SUB, n))
            row = jnp.where(lane == j, 1.0, row)
            nexts = {
                c2: jnp.broadcast_to(cols[c2][b][c : c + 1, :], (SUB, n)) for c2 in range(c + 1, SUB)
            }
            for v in range(b, pieces):
                m = cols[c][v] * inv
                here = lane == j
                if v == b:
                    m = jnp.where(sub > c, m, 0.0)
                    here = here & (sub > c)
                a[v] = jnp.where(here, 0.0, a[v]) - m * row
                for c2 in range(c + 1, SUB):
                    cols[c2][v] = cols[c2][v] - m * nexts[c2]
    out = []
    for v in range(pieces):
        diag = lane == sub + v * SUB
        d = jnp.sum(jnp.where(diag, a[v], 0.0), axis=1, keepdims=True)
        low = jnp.where(lane < sub + v * SUB, a[v], jnp.where(diag, 1.0, 0.0))
        out.append(low * lax.rsqrt(d))
    return jnp.concatenate(out, axis=0)


def project_kernel(order_ref, *refs, panels, calls, own_at):
    low_refs = refs[: -(calls + 5)]
    tiles_hbm = refs[-(calls + 5) : -5]
    basis_ref, out_ref, low_all, held, sems = refs[-5:]
    per_call = tiles_hbm[0].shape[1]
    copies = [
        pltpu.make_async_copy(
            tiles_hbm[i], held.at[:, i * per_call : (i + 1) * per_call, :], sems.at[i]
        )
        for i in range(calls)
    ]
    for copy in copies:
        copy.start()
    count = order_ref[panels]
    out_ref[...] = jnp.zeros_like(out_ref)
    q = low_refs[0].shape[0]
    for i, ref in enumerate(low_refs):
        low_all[i * q : (i + 1) * q, :] = ref[...]
    low = low_all[...]
    low_t = low.T
    gram = jnp.dot(low_t, low, preferred_element_type=jnp.float32)
    inverse = invert_factor(gram)
    inv_t = [p.astype(jnp.bfloat16) for p in three(inverse.T)]
    for i, at in enumerate(own_at):
        own = low_refs[at][...]
        parts = [jnp.dot(own, p, preferred_element_type=jnp.float32) for p in inv_t]
        basis_ref[i * q : (i + 1) * q, :] = parts[0] + (parts[1] + parts[2])
    parts = [
        jnp.dot(p.astype(jnp.bfloat16), low_t, preferred_element_type=jnp.float32)
        for p in three(inverse)
    ]
    basis_t = (parts[0] + (parts[1] + parts[2])).astype(jnp.bfloat16)
    for copy in copies:
        copy.wait()

    def pair(j, carry):
        tile = jnp.concatenate([held[2 * j], held[2 * j + 1]], axis=1)
        cols = jnp.dot(basis_t, tile, preferred_element_type=jnp.float32).astype(jnp.bfloat16)
        at = pl.multiple_of(order_ref[2 * j] * WIDTH, WIDTH)
        out_ref[0, :, pl.ds(at, WIDTH)] = cols[:, :WIDTH]

        @pl.when(2 * j + 1 < count)
        def _():
            at = pl.multiple_of(order_ref[2 * j + 1] * WIDTH, WIDTH)
            out_ref[0, :, pl.ds(at, WIDTH)] = cols[:, WIDTH:]

        return carry

    lax.fori_loop(0, (count + 1) // 2, pair, 0)


def project_pass(order, lows, tiles, own_at, panels):
    rows = sum(t.shape[1] for t in tiles)
    held = tiles[0].shape[0]
    q, rank = lows[0].shape
    vmem = pl.BlockSpec(memory_space=pltpu.VMEM)
    return pl.pallas_call(
        functools.partial(project_kernel, panels=panels, calls=len(tiles), own_at=own_at),
        in_specs=[pl.BlockSpec(memory_space=pltpu.SMEM)]
        + [vmem] * len(lows)
        + [pl.BlockSpec(memory_space=pltpu.HBM)] * len(tiles),
        out_specs=[vmem, vmem],
        out_shape=[
            jax.ShapeDtypeStruct((q * len(own_at), rank), jnp.float32),
            jax.ShapeDtypeStruct((1, rank, panels * WIDTH), jnp.bfloat16),
        ],
        scratch_shapes=[
            pltpu.VMEM((rows, rank), jnp.bfloat16),
            pltpu.VMEM((held, rows, WIDTH), jnp.bfloat16),
            pltpu.SemaphoreType.DMA((len(tiles),)),
        ],
        compiler_params=pltpu.CompilerParams(vmem_limit_bytes=44 * 2**20),
        name="project_pass",
    )(order, *lows, *(in_hbm(x) for x in tiles))


def after(x, *deps):
    return lax.optimization_barrier((x, *deps))[0]


def swap(x, k, n):
    return lax.ppermute(x, "tile", [(i, i ^ k) for i in range(n)])


CHUNKS = 2


def local(row_points, source_points, sketch, admissible):
    n = lax.axis_size("tile")
    panels = admissible.shape[1]
    rows = row_points.shape[1] // lax.axis_size("row")
    own_rows = rows // n
    q = own_rows // CHUNKS
    odd, even = list(range(1, n, 2)), list(range(0, n, 2))
    slices = [(k, c * q, q) for c in range(CHUNKS) for k in odd + even]
    place = q % WIDTH == 0
    points = row_points
    if not place:
        me = lax.axis_index("tile")
        points = lax.dynamic_slice_in_dim(row_points, lax.axis_index("row") * rows, rows, 1)
        points = jnp.concatenate(
            [lax.dynamic_slice_in_dim(points, (me ^ k) * own_rows + first, q, 1) for k, first, _ in slices], 1
        )
    order, src_pick, omega_pick, row_mat = prep(
        admissible, points, source_points, sketch, rows, slices, place
    )

    call_rows = rows // CHUNKS // 2

    def sketch_part(at, *deps):
        return sketch_pass(
            after(order, *deps), src_pick, omega_pick, row_mat, at * call_rows, call_rows, panels
        )

    def sum_cores(got, own):
        kept, *sent = pair_sum(own, got, n // 2)
        return kept, [swap(x, k, n) for x, k in zip(sent, even[1:])]

    def spread(kept, got):
        low = row_sum(kept, got)
        held = [low] + [swap(low, k, n) for k in even[1:]]
        return [swap(x, 1, n) for x in held] + held

    lows, tiles, own_at, waiting = [], [], [], None
    last = ()
    for c in range(CHUNKS):
        theirs, kept = sketch_part(2 * c, *last)
        tiles.append(kept)
        got = swap(theirs, 1, n)
        if waiting is not None:
            lows += spread(after(waiting[0], theirs), waiting[1])
        own, kept = sketch_part(2 * c + 1, theirs, *lows[-n // 2 :][:1])
        tiles.append(kept)
        waiting = sum_cores(got, own)
        last = (own, waiting[0])
    lows += spread(*waiting)
    own_at = [c * n + n // 2 for c in range(CHUNKS)]
    return project_pass(order, lows, tiles, own_at, panels)


def solution(mesh):
    in_specs = (P(), P(None, "tile"), P("tile", None), P("row", "tile"))
    out_specs = (P(("row", "tile"), None), P("row", None, "tile"))
    return jax.shard_map(local, mesh=mesh, in_specs=in_specs, out_specs=out_specs, check_vma=False)
```

```python
import functools
import math

import jax
import jax.numpy as jnp
from jax import lax
from jax.experimental import pallas as pl
from jax.experimental.pallas import tpu as pltpu
from jax.sharding import PartitionSpec as P

DAMPING = 0.25
WAVENUM = 24.0
SHIFT = 0.0001

TURNS = WAVENUM / (2.0 * math.pi)
E3 = -5.419141508131567e-07
E2, E1, E0 = 0.00012955130357743643 / E3, -0.016325949681618327 / E3, 0.9999205420269909 / E3
AMP = TURNS / (4.0 * math.pi) * E3**4
S0, S1, S2 = 6.28127979 * AMP, -41.0952178 * AMP, 73.5851113 * AMP

WIDTH = 128
PAIR = 2 * WIDTH
TERMS = 32
SUB = 8
PIECE = 16
GROUP = 4
WHOLE = 1.5 * 2.0**23


def head(x):
    return x.astype(jnp.bfloat16).astype(jnp.float32)


def three(x):
    a = head(x)
    b = head(x - a)
    return a, b, x - a - b


def fill_terms(ref, points, side):
    at = lax.broadcasted_iota(jnp.int32, points.shape, 0)
    x = points - jnp.where(at == 2, -0.5, 3.0)
    scale = TURNS * TURNS
    norm = three(scale * jnp.sum(x * x, axis=0, keepdims=True))
    one = jnp.ones_like(norm[0])
    if side == 0:
        h, m, l = three(x)
        rows = [h, h, m, h, l, m]
        tail = [*norm, one, one, one]
    else:
        h, m, l = three(x * (-2.0 * scale))
        rows = [h, m, h, l, h, m]
        tail = [one, one, one, *norm]
    ref[...] = jnp.zeros_like(ref)
    for at, row in enumerate(rows):
        ref[3 * at : 3 * at + 3, :] = row
    for at, row in enumerate(tail):
        ref[18 + at : 19 + at, :] = row


def near_field(square):
    inv = lax.rsqrt(square)
    t = square * inv
    f = t - ((t + WHOLE) - WHOLE)
    g = 0.25 - jnp.abs(f)
    v = g * g
    wave = ((S2 * v + S1) * v + S0) * g
    fade = ((t + E2) * t + E1) * t + E0
    fade = fade * fade
    return (wave * inv * (fade * fade)).astype(jnp.bfloat16)


def order_panels(flags_ref, order_ref, panels):
    def step(p, count):
        @pl.when(flags_ref[0, p] > 0)
        def _():
            order_ref[count] = p

        return count + (flags_ref[0, p] > 0).astype(jnp.int32)

    count = lax.fori_loop(0, panels, step, jnp.int32(0))
    order_ref[panels] = count
    return count


def prep_kernel(
    flags_hbm, rows_hbm, src_hbm, omega_hbm, order_ref, src_pick, omega_pick, row_mat,
    flags, points, picked, row_terms, src_terms, sources, sems, sem, *, slices, place
):
    panels = flags.shape[1]
    rows = points.shape[1]
    me = lax.axis_index("tile")
    at = pl.multiple_of(lax.axis_index("row") * rows, rows) if place else 0
    copies = [
        pltpu.make_async_copy(flags_hbm, flags, sems.at[0]),
        pltpu.make_async_copy(rows_hbm.at[:, pl.ds(at, rows)], points, sems.at[1]),
        pltpu.make_async_copy(src_hbm, sources, sems.at[2]),
    ]
    for copy in copies:
        copy.start()
    copies[0].wait()
    count = order_panels(flags, order_ref, panels)

    def fetch(slot):
        at = pl.multiple_of(order_ref[slot] * WIDTH, WIDTH)
        to = pl.multiple_of(slot * WIDTH, WIDTH)
        return pltpu.make_async_copy(
            omega_hbm.at[pl.ds(at, WIDTH), :], omega_pick.at[pl.ds(to, WIDTH), :], sem
        )

    def start(slot, carry):
        fetch(slot).start()
        return carry

    lax.fori_loop(0, count, start, 0)
    copies[1].wait()
    if place:
        to = 0
        for k, first, size in slices:
            at = pl.multiple_of((me ^ k) * (rows // lax.axis_size("tile")) + first, WIDTH)
            picked[:, to : to + size] = points[:, pl.ds(at, size)]
            to += size
        fill_terms(row_terms, picked[...], 0)
    else:
        fill_terms(row_terms, points[...], 0)
    step = min(512, rows)
    for r in range(0, rows, step):
        row_mat[r : r + step, :] = row_terms[:, r : r + step].T.astype(jnp.bfloat16)
    copies[2].wait()
    fill_terms(src_terms, sources[...], 1)

    def pick(slot, carry):
        at = pl.multiple_of(order_ref[slot] * WIDTH, WIDTH)
        to = pl.multiple_of(slot * WIDTH, WIDTH)
        src_pick[:, pl.ds(to, WIDTH)] = src_terms[:, pl.ds(at, WIDTH)].astype(jnp.bfloat16)
        return carry

    lax.fori_loop(0, count, pick, 0)
    spare = src_terms[:, :WIDTH].astype(jnp.bfloat16)

    def pad(slot, carry):
        to = pl.multiple_of(slot * WIDTH, WIDTH)
        src_pick[:, pl.ds(to, WIDTH)] = spare
        omega_pick[pl.ds(to, WIDTH), :] = jnp.zeros((WIDTH, omega_pick.shape[1]), jnp.bfloat16)
        return carry

    lax.fori_loop(count, GROUP * ((count + GROUP - 1) // GROUP + 1), pad, 0)

    def finish(slot, carry):
        fetch(slot).wait()
        return carry

    lax.fori_loop(0, count, finish, 0)


def in_hbm(x):
    return pltpu.with_memory_space_constraint(x, pltpu.HBM)


def prep(admissible, points, source_points, sketch, rows, slices, place):
    panels = admissible.shape[1]
    cols, rank = sketch.shape
    spare = cols + 2 * GROUP * WIDTH
    hbm = pl.BlockSpec(memory_space=pltpu.HBM)
    vmem = pl.BlockSpec(memory_space=pltpu.VMEM)
    return pl.pallas_call(
        functools.partial(prep_kernel, slices=slices, place=place),
        in_specs=[hbm] * 4,
        out_specs=[pl.BlockSpec(memory_space=pltpu.SMEM), vmem, vmem, vmem],
        out_shape=[
            jax.ShapeDtypeStruct((panels + 8,), jnp.int32),
            jax.ShapeDtypeStruct((TERMS, spare), jnp.bfloat16),
            jax.ShapeDtypeStruct((spare, rank), jnp.bfloat16),
            jax.ShapeDtypeStruct((rows, TERMS), jnp.bfloat16),
        ],
        scratch_shapes=[
            pltpu.SMEM((1, panels), jnp.int32),
            pltpu.VMEM((3, rows), jnp.float32),
            pltpu.VMEM((3, rows), jnp.float32),
            pltpu.VMEM((TERMS, rows), jnp.float32),
            pltpu.VMEM((TERMS, cols), jnp.float32),
            pltpu.VMEM((3, cols), jnp.float32),
            pltpu.SemaphoreType.DMA((3,)),
            pltpu.SemaphoreType.DMA,
        ],
        compiler_params=pltpu.CompilerParams(vmem_limit_bytes=16 * 2**20),
        name="prep",
    )(*(in_hbm(x) for x in (admissible, points, source_points, sketch)))


def sketch_kernel(
    order_ref, src_pick, omega_pick, row_mat, part_ref, tiles_hbm, squares, tiles, total, sems,
    *, first, panels, rb
):
    groups = (order_ref[panels] + GROUP - 1) // GROUP
    cols = GROUP * WIDTH

    def block(b, carry):
        here = pl.ds(pl.multiple_of(b * rb, rb), rb)
        total[...] = jnp.zeros_like(total)
        tiles[1] = jnp.zeros(tiles.shape[1:], tiles.dtype)

        def columns(j):
            return pl.ds(pl.multiple_of(j * cols, cols), cols)

        def square_of(j):
            rows = row_mat[pl.ds(pl.multiple_of(first + b * rb, rb), rb), :]
            return jnp.dot(rows, src_pick[:, columns(j)], preferred_element_type=jnp.float32)

        def add(j, slot):
            tile = jnp.concatenate([tiles[slot, k] for k in range(GROUP)], axis=1)
            omega = omega_pick[columns(j), :]
            return total[...] + jnp.dot(tile, omega, preferred_element_type=jnp.float32)

        def keep(j):
            slot = lax.rem(j, 2)
            return pltpu.make_async_copy(
                tiles.at[slot], tiles_hbm.at[pl.ds(GROUP * j, GROUP), here, :], sems.at[slot]
            )

        squares[...] = square_of(0)

        def body(j, carry):
            @pl.when(j >= 2)
            def _():
                keep(j - 2).wait()

            slot = lax.rem(j, 2)
            square = squares[...]
            sums = add(jnp.maximum(j - 1, 0), 1 - slot)
            later = square_of(j + 1)
            near = [near_field(square[r : r + PIECE]) for r in range(0, rb, PIECE)]
            total[...] = sums
            squares[...] = later
            for r, piece in zip(range(0, rb, PIECE), near):
                for k in range(GROUP):
                    tiles[slot, k, r : r + PIECE, :] = piece[:, k * WIDTH : (k + 1) * WIDTH]
            keep(j).start()
            return carry

        lax.fori_loop(0, groups, body, 0)

        @pl.when(groups > 1)
        def _():
            keep(groups - 2).wait()

        @pl.when(groups > 0)
        def _():
            keep(groups - 1).wait()
            total[...] = add(groups - 1, lax.rem(groups - 1, 2))

        part_ref[here, :] = total[...]
        return carry

    lax.fori_loop(0, part_ref.shape[0] // rb, block, 0)


def sketch_pass(order, src_pick, omega_pick, row_mat, first, rows, panels):
    rank = omega_pick.shape[1]
    rb = min(512, rows)
    vmem = pl.BlockSpec(memory_space=pltpu.VMEM)
    return pl.pallas_call(
        functools.partial(sketch_kernel, first=first, panels=panels, rb=rb),
        in_specs=[pl.BlockSpec(memory_space=pltpu.SMEM), vmem, vmem, vmem],
        out_specs=[vmem, pl.BlockSpec(memory_space=pltpu.HBM)],
        out_shape=[
            jax.ShapeDtypeStruct((rows, rank), jnp.float32),
            pltpu.HBM((GROUP * ((panels + GROUP - 1) // GROUP), rows, WIDTH), jnp.bfloat16),
        ],
        scratch_shapes=[
            pltpu.VMEM((rb, GROUP * WIDTH), jnp.float32),
            pltpu.VMEM((2, GROUP, rb, WIDTH), jnp.bfloat16),
            pltpu.VMEM((rb, rank), jnp.float32),
            pltpu.SemaphoreType.DMA((2,)),
        ],
        compiler_params=pltpu.CompilerParams(vmem_limit_bytes=16 * 2**20),
        cost_estimate=pl.CostEstimate(
            flops=rows * panels * WIDTH * rank * 16, bytes_accessed=rows * panels * WIDTH * 2, transcendentals=0
        ),
        name="sketch_pass",
    )(order, src_pick, omega_pick, row_mat)


def in_vmem(kernel, out_shape, name):
    def call(*args):
        vmem = pl.BlockSpec(memory_space=pltpu.VMEM)
        return pl.pallas_call(
            kernel,
            in_specs=[vmem] * len(args),
            out_specs=jax.tree.map(lambda _: vmem, out_shape),
            out_shape=out_shape,
            compiler_params=pltpu.CompilerParams(vmem_limit_bytes=8 * 2**20),
            name=name,
        )(*args)

    return call


def pair_sum_kernel(own_ref, got_ref, kept_ref, *sent_refs):
    q = kept_ref.shape[0]
    for k in range(1 + len(sent_refs)):
        part = slice(k * q, (k + 1) * q)
        value = own_ref[part, :] + got_ref[part, :]
        if k == 0:
            kept_ref[...] = value
        else:
            sent_refs[k - 1][...] = value.astype(jnp.bfloat16)


def pair_sum(own, got, slots):
    q, rank = own.shape[0] // slots, own.shape[1]
    shapes = [jax.ShapeDtypeStruct((q, rank), jnp.float32)]
    shapes += [jax.ShapeDtypeStruct((q, rank), jnp.bfloat16)] * (slots - 1)
    return in_vmem(pair_sum_kernel, shapes, "pair_sum")(own, got)


def row_sum_kernel(kept_ref, *refs):
    total = kept_ref[...]
    for ref in refs[:-1]:
        total = total + ref[...].astype(jnp.float32)
    low = head(total)
    refs[-1][...] = (low if refs[-1].shape == low.shape else low.T).astype(jnp.bfloat16)


def row_sum(kept, got, flip):
    shape = kept.shape[::-1] if flip else kept.shape
    return in_vmem(row_sum_kernel, jax.ShapeDtypeStruct(shape, jnp.bfloat16), "row_sum")(kept, *got)


def invert_factor(gram):
    n = gram.shape[0]
    pieces = n // SUB
    lane = lax.broadcasted_iota(jnp.int32, (SUB, n), 1)
    sub = lax.broadcasted_iota(jnp.int32, (SUB, n), 0)
    trace = jnp.zeros((SUB, n), jnp.float32)
    for v in range(pieces):
        trace = trace + jnp.where(lane == sub + v * SUB, gram[v * SUB : (v + 1) * SUB, :], 0.0)
    shift = (SHIFT / n) * jnp.sum(trace)
    a = [
        gram[v * SUB : (v + 1) * SUB, :] + jnp.where(lane == sub + v * SUB, shift, 0.0)
        for v in range(pieces)
    ]
    for b in range(pieces):
        cols = [
            {v: jnp.broadcast_to(a[v][:, b * SUB + c : b * SUB + c + 1], (SUB, n)) for v in range(b, pieces)}
            for c in range(SUB)
        ]
        for c in range(SUB):
            j = b * SUB + c
            pivot = jnp.broadcast_to(cols[c][b][c : c + 1, :], (SUB, n))
            inv = 1.0 / pivot
            row = jnp.broadcast_to(a[b][c : c + 1, :], (SUB, n))
            row = jnp.where(lane == j, 1.0, row)
            nexts = {
                c2: jnp.broadcast_to(cols[c2][b][c : c + 1, :], (SUB, n)) for c2 in range(c + 1, SUB)
            }
            for v in range(b, pieces):
                m = cols[c][v] * inv
                here = lane == j
                if v == b:
                    m = jnp.where(sub > c, m, 0.0)
                    here = here & (sub > c)
                a[v] = jnp.where(here, 0.0, a[v]) - m * row
                for c2 in range(c + 1, SUB):
                    cols[c2][v] = cols[c2][v] - m * nexts[c2]
    out = []
    for v in range(pieces):
        diag = lane == sub + v * SUB
        d = jnp.sum(jnp.where(diag, a[v], 0.0), axis=1, keepdims=True)
        low = jnp.where(lane < sub + v * SUB, a[v], jnp.where(diag, 1.0, 0.0))
        out.append(low * lax.rsqrt(d))
    return jnp.concatenate(out, axis=0)


def project_kernel(order_ref, *refs, panels, calls, own_at, flip):
    low_refs = refs[: -(calls + 5)]
    tiles_hbm = refs[-(calls + 5) : -5]
    basis_ref, out_ref, low_all, held, sems = refs[-5:]
    per_call = tiles_hbm[0].shape[1]
    copies = [
        pltpu.make_async_copy(
            tiles_hbm[i], held.at[:, i * per_call : (i + 1) * per_call, :], sems.at[i]
        )
        for i in range(calls)
    ]
    for copy in copies:
        copy.start()
    count = order_ref[panels]
    q = low_refs[0].shape[1 if flip else 0]
    for i, ref in enumerate(low_refs):
        if flip:
            low_all[:, i * q : (i + 1) * q] = ref[...]
        else:
            low_all[i * q : (i + 1) * q, :] = ref[...]
    low_t = low_all[...] if flip else low_all[...].T
    gram = lax.dot_general(low_t, low_t, (((1,), (1,)), ((), ())), preferred_element_type=jnp.float32)
    inverse = [p.astype(jnp.bfloat16) for p in three(invert_factor(gram))]
    out_ref[...] = jnp.zeros_like(out_ref)
    parts = [jnp.dot(p, low_t, preferred_element_type=jnp.float32) for p in inverse]
    basis = parts[0] + (parts[1] + parts[2])
    basis_t = basis.astype(jnp.bfloat16)
    for i, at in enumerate(own_at):
        basis_ref[i * q : (i + 1) * q, :] = basis[:, at * q : (at + 1) * q].T
    for copy in copies:
        copy.wait()

    def group(j, carry):
        tile = jnp.concatenate([held[GROUP * j + k] for k in range(GROUP)], axis=1)
        cols = jnp.dot(basis_t, tile, preferred_element_type=jnp.float32).astype(jnp.bfloat16)
        for k in range(GROUP):

            @pl.when(GROUP * j + k < count)
            def _():
                at = pl.multiple_of(order_ref[GROUP * j + k] * WIDTH, WIDTH)
                out_ref[0, :, pl.ds(at, WIDTH)] = cols[:, k * WIDTH : (k + 1) * WIDTH]

        return carry

    lax.fori_loop(0, (count + GROUP - 1) // GROUP, group, 0)


def project_pass(order, lows, tiles, own_at, panels, rank, flip):
    rows = sum(t.shape[1] for t in tiles)
    held = tiles[0].shape[0]
    q = lows[0].shape[1 if flip else 0]
    vmem = pl.BlockSpec(memory_space=pltpu.VMEM)
    return pl.pallas_call(
        functools.partial(
            project_kernel, panels=panels, calls=len(tiles), own_at=own_at, flip=flip
        ),
        in_specs=[pl.BlockSpec(memory_space=pltpu.SMEM)]
        + [vmem] * len(lows)
        + [pl.BlockSpec(memory_space=pltpu.HBM)] * len(tiles),
        out_specs=[vmem, vmem],
        out_shape=[
            jax.ShapeDtypeStruct((q * len(own_at), rank), jnp.float32),
            jax.ShapeDtypeStruct((1, rank, panels * WIDTH), jnp.bfloat16),
        ],
        scratch_shapes=[
            pltpu.VMEM((rank, rows) if flip else (rows, rank), jnp.bfloat16),
            pltpu.VMEM((held, rows, WIDTH), jnp.bfloat16),
            pltpu.SemaphoreType.DMA((len(tiles),)),
        ],
        compiler_params=pltpu.CompilerParams(vmem_limit_bytes=48 * 2**20),
        name="project_pass",
    )(order, *lows, *(in_hbm(x) for x in tiles))


def after(x, *deps):
    return lax.optimization_barrier((x, *deps))[0]


def swap(x, k, n):
    return lax.ppermute(x, "tile", [(i, i ^ k) for i in range(n)])


CHUNKS = 2


def local(row_points, source_points, sketch, admissible):
    n = lax.axis_size("tile")
    panels = admissible.shape[1]
    rows = row_points.shape[1] // lax.axis_size("row")
    own_rows = rows // n
    q = own_rows // CHUNKS
    odd, even = list(range(1, n, 2)), list(range(0, n, 2))
    slices = [(k, c * q, q) for c in range(CHUNKS) for k in odd + even]
    place = flip = q % WIDTH == 0
    points = row_points
    if not place:
        me = lax.axis_index("tile")
        points = lax.dynamic_slice_in_dim(row_points, lax.axis_index("row") * rows, rows, 1)
        points = jnp.concatenate(
            [lax.dynamic_slice_in_dim(points, (me ^ k) * own_rows + first, q, 1) for k, first, _ in slices], 1
        )
    order, src_pick, omega_pick, row_mat = prep(
        admissible, points, source_points, sketch, rows, slices, place
    )

    call_rows = rows // CHUNKS // 2

    def sketch_part(at, *deps):
        return sketch_pass(
            after(order, *deps), src_pick, omega_pick, row_mat, at * call_rows, call_rows, panels
        )

    def sum_cores(got, own):
        kept, *sent = pair_sum(own, got, n // 2)
        return kept, [swap(x, k, n) for x, k in zip(sent, even[1:])]

    def spread(kept, got):
        low = row_sum(kept, got, flip)
        held = [low] + [swap(low, k, n) for k in even[1:]]
        return [swap(x, 1, n) for x in held] + held

    lows, tiles, own_at, waiting = [], [], [], None
    last = ()
    for c in range(CHUNKS):
        theirs, kept = sketch_part(2 * c, *last)
        tiles.append(kept)
        got = swap(theirs, 1, n)
        if waiting is not None:
            lows += spread(after(waiting[0], theirs), waiting[1])
        own, kept = sketch_part(2 * c + 1, theirs, *lows[-n // 2 :][:1])
        tiles.append(kept)
        waiting = sum_cores(got, own)
        last = (own, waiting[0])
    lows += spread(*waiting)
    own_at = [c * n + n // 2 for c in range(CHUNKS)]
    return project_pass(order, lows, tiles, own_at, panels, sketch.shape[1], flip)


def solution(mesh):
    in_specs = (P(), P(None, "tile"), P("tile", None), P("row", "tile"))
    out_specs = (P(("row", "tile"), None), P("row", None, "tile"))
    return jax.shard_map(local, mesh=mesh, in_specs=in_specs, out_specs=out_specs, check_vma=False)
```

```python
import functools
import math

import jax
import jax.numpy as jnp
from jax import lax
from jax.experimental import pallas as pl
from jax.experimental.pallas import tpu as pltpu
from jax.sharding import PartitionSpec as P

DAMPING = 0.25
WAVENUM = 24.0
SHIFT = 0.0001

TURNS = WAVENUM / (2.0 * math.pi)
DECAY = -DAMPING / TURNS / math.log(2.0)
AMP = TURNS / (4.0 * math.pi)
S0, S1, S2 = 6.28127979 * AMP, -41.0952178 * AMP, 73.5851113 * AMP

WIDTH = 128
PAIR = 2 * WIDTH
TERMS = 32
SUB = 8
PIECE = 16
GROUP = 4
WHOLE = 1.5 * 2.0**23


def head(x):
    return x.astype(jnp.bfloat16).astype(jnp.float32)


def three(x):
    a = head(x)
    b = head(x - a)
    return a, b, x - a - b


def fill_terms(ref, points, side):
    at = lax.broadcasted_iota(jnp.int32, points.shape, 0)
    x = points - jnp.where(at == 2, -0.5, 3.0)
    scale = TURNS * TURNS
    norm = three(scale * jnp.sum(x * x, axis=0, keepdims=True))
    one = jnp.ones_like(norm[0])
    if side == 0:
        h, m, l = three(x)
        rows = [h, h, m, h, l, m]
        tail = [*norm, one, one, one]
    else:
        h, m, l = three(x * (-2.0 * scale))
        rows = [h, m, h, l, h, m]
        tail = [one, one, one, *norm]
    ref[...] = jnp.zeros_like(ref)
    for at, row in enumerate(rows):
        ref[3 * at : 3 * at + 3, :] = row
    for at, row in enumerate(tail):
        ref[18 + at : 19 + at, :] = row


def near_field(square):
    inv = lax.rsqrt(square)
    t = square * inv
    f = t - ((t + WHOLE) - WHOLE)
    g = 0.25 - jnp.abs(f)
    v = g * g
    wave = ((S2 * v + S1) * v + S0) * g
    amp = jnp.exp2(DECAY * t) * inv
    return (wave * amp).astype(jnp.bfloat16)


def order_panels(flags_ref, order_ref, panels):
    def step(p, count):
        @pl.when(flags_ref[0, p] > 0)
        def _():
            order_ref[count] = p

        return count + (flags_ref[0, p] > 0).astype(jnp.int32)

    count = lax.fori_loop(0, panels, step, jnp.int32(0))
    order_ref[panels] = count
    return count


def prep_kernel(
    flags_hbm, rows_hbm, src_hbm, omega_hbm, order_ref, src_pick, omega_pick, row_mat,
    flags, points, picked, row_terms, src_terms, sources, sems, sem, *, slices, place
):
    panels = flags.shape[1]
    rows = points.shape[1]
    me = lax.axis_index("tile")
    at = pl.multiple_of(lax.axis_index("row") * rows, rows) if place else 0
    copies = [
        pltpu.make_async_copy(flags_hbm, flags, sems.at[0]),
        pltpu.make_async_copy(rows_hbm.at[:, pl.ds(at, rows)], points, sems.at[1]),
        pltpu.make_async_copy(src_hbm, sources, sems.at[2]),
    ]
    for copy in copies:
        copy.start()
    copies[0].wait()
    count = order_panels(flags, order_ref, panels)

    def fetch(slot):
        at = pl.multiple_of(order_ref[slot] * WIDTH, WIDTH)
        to = pl.multiple_of(slot * WIDTH, WIDTH)
        return pltpu.make_async_copy(
            omega_hbm.at[pl.ds(at, WIDTH), :], omega_pick.at[pl.ds(to, WIDTH), :], sem
        )

    def start(slot, carry):
        fetch(slot).start()
        return carry

    lax.fori_loop(0, count, start, 0)
    copies[1].wait()
    if place:
        to = 0
        for k, first, size in slices:
            at = pl.multiple_of((me ^ k) * (rows // lax.axis_size("tile")) + first, WIDTH)
            picked[:, to : to + size] = points[:, pl.ds(at, size)]
            to += size
        fill_terms(row_terms, picked[...], 0)
    else:
        fill_terms(row_terms, points[...], 0)
    step = min(512, rows)
    for r in range(0, rows, step):
        row_mat[r : r + step, :] = row_terms[:, r : r + step].T.astype(jnp.bfloat16)
    copies[2].wait()
    fill_terms(src_terms, sources[...], 1)

    def pick(slot, carry):
        at = pl.multiple_of(order_ref[slot] * WIDTH, WIDTH)
        to = pl.multiple_of(slot * WIDTH, WIDTH)
        src_pick[:, pl.ds(to, WIDTH)] = src_terms[:, pl.ds(at, WIDTH)].astype(jnp.bfloat16)
        return carry

    lax.fori_loop(0, count, pick, 0)
    spare = src_terms[:, :WIDTH].astype(jnp.bfloat16)

    def pad(slot, carry):
        to = pl.multiple_of(slot * WIDTH, WIDTH)
        src_pick[:, pl.ds(to, WIDTH)] = spare
        omega_pick[pl.ds(to, WIDTH), :] = jnp.zeros((WIDTH, omega_pick.shape[1]), jnp.bfloat16)
        return carry

    lax.fori_loop(count, GROUP * ((count + GROUP - 1) // GROUP + 1), pad, 0)

    def finish(slot, carry):
        fetch(slot).wait()
        return carry

    lax.fori_loop(0, count, finish, 0)


def in_hbm(x):
    return pltpu.with_memory_space_constraint(x, pltpu.HBM)


def prep(admissible, points, source_points, sketch, rows, slices, place):
    panels = admissible.shape[1]
    cols, rank = sketch.shape
    spare = cols + 2 * GROUP * WIDTH
    hbm = pl.BlockSpec(memory_space=pltpu.HBM)
    vmem = pl.BlockSpec(memory_space=pltpu.VMEM)
    return pl.pallas_call(
        functools.partial(prep_kernel, slices=slices, place=place),
        in_specs=[hbm] * 4,
        out_specs=[pl.BlockSpec(memory_space=pltpu.SMEM), vmem, vmem, vmem],
        out_shape=[
            jax.ShapeDtypeStruct((panels + 8,), jnp.int32),
            jax.ShapeDtypeStruct((TERMS, spare), jnp.bfloat16),
            jax.ShapeDtypeStruct((spare, rank), jnp.bfloat16),
            jax.ShapeDtypeStruct((rows, TERMS), jnp.bfloat16),
        ],
        scratch_shapes=[
            pltpu.SMEM((1, panels), jnp.int32),
            pltpu.VMEM((3, rows), jnp.float32),
            pltpu.VMEM((3, rows), jnp.float32),
            pltpu.VMEM((TERMS, rows), jnp.float32),
            pltpu.VMEM((TERMS, cols), jnp.float32),
            pltpu.VMEM((3, cols), jnp.float32),
            pltpu.SemaphoreType.DMA((3,)),
            pltpu.SemaphoreType.DMA,
        ],
        compiler_params=pltpu.CompilerParams(vmem_limit_bytes=16 * 2**20),
        name="prep",
    )(*(in_hbm(x) for x in (admissible, points, source_points, sketch)))


def sketch_kernel(
    order_ref, src_pick, omega_pick, row_mat, part_ref, tiles_ref, squares, total,
    *, first, panels, rb
):
    groups = (order_ref[panels] + GROUP - 1) // GROUP
    cols = GROUP * WIDTH

    def block(b, carry):
        here = pl.ds(pl.multiple_of(b * rb, rb), rb)
        total[...] = jnp.zeros_like(total)

        def columns(j):
            return pl.ds(pl.multiple_of(j * cols, cols), cols)

        def square_of(j):
            rows = row_mat[pl.ds(pl.multiple_of(first + b * rb, rb), rb), :]
            return jnp.dot(rows, src_pick[:, columns(j)], preferred_element_type=jnp.float32)

        squares[...] = square_of(0)

        def body(j, carry):
            square = squares[...]
            before = total[...]
            later = square_of(j + 1)
            near = [near_field(square[r : r + PIECE]) for r in range(0, rb, PIECE)]
            tile = jnp.concatenate(near, axis=0)
            sums = before + jnp.dot(tile, omega_pick[columns(j), :], preferred_element_type=jnp.float32)
            squares[...] = later
            total[...] = sums
            for k in range(GROUP):
                tiles_ref[GROUP * j + k, here, :] = tile[:, k * WIDTH : (k + 1) * WIDTH]
            return carry

        lax.fori_loop(0, groups, body, 0)
        part_ref[here, :] = total[...]
        return carry

    lax.fori_loop(0, part_ref.shape[0] // rb, block, 0)


def sketch_pass(order, src_pick, omega_pick, row_mat, first, rows, panels):
    rank = omega_pick.shape[1]
    rb = min(512, rows)
    vmem = pl.BlockSpec(memory_space=pltpu.VMEM)
    return pl.pallas_call(
        functools.partial(sketch_kernel, first=first, panels=panels, rb=rb),
        in_specs=[pl.BlockSpec(memory_space=pltpu.SMEM), vmem, vmem, vmem],
        out_specs=[vmem, vmem],
        out_shape=[
            jax.ShapeDtypeStruct((rows, rank), jnp.float32),
            pltpu.VMEM((GROUP * ((panels + GROUP - 1) // GROUP), rows, WIDTH), jnp.bfloat16),
        ],
        scratch_shapes=[
            pltpu.VMEM((rb, GROUP * WIDTH), jnp.float32),
            pltpu.VMEM((rb, rank), jnp.float32),
        ],
        compiler_params=pltpu.CompilerParams(vmem_limit_bytes=10 * 2**20),
        cost_estimate=pl.CostEstimate(
            flops=rows * panels * WIDTH * rank * 16, bytes_accessed=rows * panels * WIDTH * 2, transcendentals=0
        ),
        name="sketch_pass",
    )(order, src_pick, omega_pick, row_mat)


def in_vmem(kernel, out_shape, name):
    def call(*args):
        vmem = pl.BlockSpec(memory_space=pltpu.VMEM)
        return pl.pallas_call(
            kernel,
            in_specs=[vmem] * len(args),
            out_specs=jax.tree.map(lambda _: vmem, out_shape),
            out_shape=out_shape,
            compiler_params=pltpu.CompilerParams(vmem_limit_bytes=8 * 2**20),
            name=name,
        )(*args)

    return call


def pair_sum_kernel(own_ref, got_ref, kept_ref, *sent_refs):
    q = kept_ref.shape[0]
    for k in range(1 + len(sent_refs)):
        part = slice(k * q, (k + 1) * q)
        value = own_ref[part, :] + got_ref[part, :]
        if k == 0:
            kept_ref[...] = value
        else:
            sent_refs[k - 1][...] = value.astype(jnp.bfloat16)


def pair_sum(own, got, slots):
    q, rank = own.shape[0] // slots, own.shape[1]
    shapes = [jax.ShapeDtypeStruct((q, rank), jnp.float32)]
    shapes += [jax.ShapeDtypeStruct((q, rank), jnp.bfloat16)] * (slots - 1)
    return in_vmem(pair_sum_kernel, shapes, "pair_sum")(own, got)


def row_sum_kernel(kept_ref, *refs):
    total = kept_ref[...]
    for ref in refs[:-1]:
        total = total + ref[...].astype(jnp.float32)
    low = head(total)
    refs[-1][...] = (low if refs[-1].shape == low.shape else low.T).astype(jnp.bfloat16)


def row_sum(kept, got, flip):
    shape = kept.shape[::-1] if flip else kept.shape
    return in_vmem(row_sum_kernel, jax.ShapeDtypeStruct(shape, jnp.bfloat16), "row_sum")(kept, *got)


def invert_factor(gram):
    n = gram.shape[0]
    pieces = n // SUB
    lane = lax.broadcasted_iota(jnp.int32, (SUB, n), 1)
    sub = lax.broadcasted_iota(jnp.int32, (SUB, n), 0)
    trace = jnp.zeros((SUB, n), jnp.float32)
    for v in range(pieces):
        trace = trace + jnp.where(lane == sub + v * SUB, gram[v * SUB : (v + 1) * SUB, :], 0.0)
    shift = (SHIFT / n) * jnp.sum(trace)
    a = [
        gram[v * SUB : (v + 1) * SUB, :] + jnp.where(lane == sub + v * SUB, shift, 0.0)
        for v in range(pieces)
    ]
    for b in range(pieces):
        cols = [
            {v: jnp.broadcast_to(a[v][:, b * SUB + c : b * SUB + c + 1], (SUB, n)) for v in range(b, pieces)}
            for c in range(SUB)
        ]
        for c in range(SUB):
            j = b * SUB + c
            pivot = jnp.broadcast_to(cols[c][b][c : c + 1, :], (SUB, n))
            inv = 1.0 / pivot
            row = jnp.broadcast_to(a[b][c : c + 1, :], (SUB, n))
            row = jnp.where(lane == j, 1.0, row)
            nexts = {
                c2: jnp.broadcast_to(cols[c2][b][c : c + 1, :], (SUB, n)) for c2 in range(c + 1, SUB)
            }
            for v in range(b, pieces):
                m = cols[c][v] * inv
                here = lane == j
                if v == b:
                    m = jnp.where(sub > c, m, 0.0)
                    here = here & (sub > c)
                a[v] = jnp.where(here, 0.0, a[v]) - m * row
                for c2 in range(c + 1, SUB):
                    cols[c2][v] = cols[c2][v] - m * nexts[c2]
    out = []
    for v in range(pieces):
        diag = lane == sub + v * SUB
        d = jnp.sum(jnp.where(diag, a[v], 0.0), axis=1, keepdims=True)
        low = jnp.where(lane < sub + v * SUB, a[v], jnp.where(diag, 1.0, 0.0))
        out.append(low * lax.rsqrt(d))
    return jnp.concatenate(out, axis=0)


def project_kernel(order_ref, *refs, panels, calls, own_at, flip):
    low_refs = refs[: -(calls + 3)]
    tile_refs = refs[-(calls + 3) : -3]
    basis_ref, out_ref, low_all = refs[-3:]
    count = order_ref[panels]
    q = low_refs[0].shape[1 if flip else 0]
    for i, ref in enumerate(low_refs):
        if flip:
            low_all[:, i * q : (i + 1) * q] = ref[...]
        else:
            low_all[i * q : (i + 1) * q, :] = ref[...]
    low_t = low_all[...] if flip else low_all[...].T
    gram = lax.dot_general(low_t, low_t, (((1,), (1,)), ((), ())), preferred_element_type=jnp.float32)
    inverse = [p.astype(jnp.bfloat16) for p in three(invert_factor(gram))]
    out_ref[...] = jnp.zeros_like(out_ref)
    parts = [jnp.dot(p, low_t, preferred_element_type=jnp.float32) for p in inverse]
    basis = parts[0] + (parts[1] + parts[2])
    basis_t = basis.astype(jnp.bfloat16)
    for i, at in enumerate(own_at):
        basis_ref[i * q : (i + 1) * q, :] = basis[:, at * q : (at + 1) * q].T

    def group(j, carry):
        tile = jnp.concatenate(
            [
                jnp.concatenate([ref[GROUP * j + k] for k in range(GROUP)], axis=1)
                for ref in tile_refs
            ],
            axis=0,
        )
        cols = jnp.dot(basis_t, tile, preferred_element_type=jnp.float32).astype(jnp.bfloat16)
        for k in range(GROUP):

            @pl.when(GROUP * j + k < count)
            def _():
                at = pl.multiple_of(order_ref[GROUP * j + k] * WIDTH, WIDTH)
                out_ref[0, :, pl.ds(at, WIDTH)] = cols[:, k * WIDTH : (k + 1) * WIDTH]

        return carry

    lax.fori_loop(0, (count + GROUP - 1) // GROUP, group, 0)


def project_pass(order, lows, tiles, own_at, panels, rank, flip):
    rows = sum(t.shape[1] for t in tiles)
    q = lows[0].shape[1 if flip else 0]
    vmem = pl.BlockSpec(memory_space=pltpu.VMEM)
    return pl.pallas_call(
        functools.partial(
            project_kernel, panels=panels, calls=len(tiles), own_at=own_at, flip=flip
        ),
        in_specs=[pl.BlockSpec(memory_space=pltpu.SMEM)]
        + [vmem] * len(lows)
        + [vmem] * len(tiles),
        out_specs=[vmem, vmem],
        out_shape=[
            jax.ShapeDtypeStruct((q * len(own_at), rank), jnp.float32),
            jax.ShapeDtypeStruct((1, rank, panels * WIDTH), jnp.bfloat16),
        ],
        scratch_shapes=[
            pltpu.VMEM((rank, rows) if flip else (rows, rank), jnp.bfloat16),
        ],
        compiler_params=pltpu.CompilerParams(vmem_limit_bytes=16 * 2**20),
        name="project_pass",
    )(order, *lows, *(pltpu.with_memory_space_constraint(x, pltpu.VMEM) for x in tiles))


def after(x, *deps):
    return lax.optimization_barrier((x, *deps))[0]


def swap(x, k, n):
    return lax.ppermute(x, "tile", [(i, i ^ k) for i in range(n)])


CHUNKS = 2


def local(row_points, source_points, sketch, admissible):
    n = lax.axis_size("tile")
    panels = admissible.shape[1]
    rows = row_points.shape[1] // lax.axis_size("row")
    own_rows = rows // n
    q = own_rows // CHUNKS
    odd, even = list(range(1, n, 2)), list(range(0, n, 2))
    slices = [(k, c * q, q) for c in range(CHUNKS) for k in odd + even]
    place = flip = q % WIDTH == 0
    points = row_points
    if not place:
        me = lax.axis_index("tile")
        points = lax.dynamic_slice_in_dim(row_points, lax.axis_index("row") * rows, rows, 1)
        points = jnp.concatenate(
            [lax.dynamic_slice_in_dim(points, (me ^ k) * own_rows + first, q, 1) for k, first, _ in slices], 1
        )
    order, src_pick, omega_pick, row_mat = prep(
        admissible, points, source_points, sketch, rows, slices, place
    )

    call_rows = rows // CHUNKS // 2

    def sketch_part(at, *deps):
        return sketch_pass(
            after(order, *deps), src_pick, omega_pick, row_mat, at * call_rows, call_rows, panels
        )

    def sum_cores(got, own):
        kept, *sent = pair_sum(own, got, n // 2)
        return kept, [swap(x, k, n) for x, k in zip(sent, even[1:])]

    def spread(kept, got):
        low = row_sum(kept, got, flip)
        held = [low] + [swap(low, k, n) for k in even[1:]]
        return [swap(x, 1, n) for x in held] + held

    lows, tiles, own_at, waiting = [], [], [], None
    last = ()
    for c in range(CHUNKS):
        theirs, kept = sketch_part(2 * c, *last)
        tiles.append(kept)
        got = swap(theirs, 1, n)
        if waiting is not None:
            lows += spread(after(waiting[0], theirs), waiting[1])
        own, kept = sketch_part(2 * c + 1, theirs, *lows[-n // 2 :][:1])
        tiles.append(kept)
        waiting = sum_cores(got, own)
        last = (own, waiting[0])
    lows += spread(*waiting)
    own_at = [c * n + n // 2 for c in range(CHUNKS)]
    return project_pass(order, lows, tiles, own_at, panels, sketch.shape[1], flip)


def solution(mesh):
    in_specs = (P(), P(None, "tile"), P("tile", None), P("row", "tile"))
    out_specs = (P(("row", "tile"), None), P("row", None, "tile"))
    return jax.shard_map(local, mesh=mesh, in_specs=in_specs, out_specs=out_specs, check_vma=False)
```

```python
import functools
import math

import jax
import jax.numpy as jnp
from jax import lax
from jax.experimental import pallas as pl
from jax.experimental.pallas import tpu as pltpu
from jax.sharding import PartitionSpec as P

DAMPING = 0.25
WAVENUM = 24.0
SHIFT = 0.0001

TURNS = WAVENUM / (2.0 * math.pi)
DECAY = -DAMPING / TURNS / math.log(2.0)
AMP = TURNS / (4.0 * math.pi)
S0, S1, S2 = 6.28127979 * AMP, -41.0952178 * AMP, 73.5851113 * AMP

WIDTH = 128
PAIR = 2 * WIDTH
TERMS = 32
SUB = 8
PIECE = 16
GROUP = 8
FEW = 4
HALF = FEW * WIDTH
WHOLE = 1.5 * 2.0**23


def head(x):
    return x.astype(jnp.bfloat16).astype(jnp.float32)


def three(x):
    a = head(x)
    b = head(x - a)
    return a, b, x - a - b


def fill_terms(ref, points, side):
    at = lax.broadcasted_iota(jnp.int32, points.shape, 0)
    x = points - jnp.where(at == 2, -0.5, 3.0)
    scale = TURNS * TURNS
    norm = three(scale * jnp.sum(x * x, axis=0, keepdims=True))
    one = jnp.ones_like(norm[0])
    if side == 0:
        h, m, l = three(x)
        rows = [h, h, m, h, l, m]
        tail = [*norm, one, one, one]
    else:
        h, m, l = three(x * (-2.0 * scale))
        rows = [h, m, h, l, h, m]
        tail = [one, one, one, *norm]
    ref[...] = jnp.zeros_like(ref)
    for at, row in enumerate(rows):
        ref[3 * at : 3 * at + 3, :] = row
    for at, row in enumerate(tail):
        ref[18 + at : 19 + at, :] = row


def near_field(square):
    inv = lax.rsqrt(square)
    t = square * inv
    f = t - ((t + WHOLE) - WHOLE)
    g = 0.25 - jnp.abs(f)
    v = g * g
    wave = ((S2 * v + S1) * v + S0) * g
    amp = jnp.exp2(DECAY * t) * inv
    return (wave * amp).astype(jnp.bfloat16)


def order_panels(flags_ref, order_ref, panels):
    def step(p, count):
        @pl.when(flags_ref[0, p] > 0)
        def _():
            order_ref[count] = p

        return count + (flags_ref[0, p] > 0).astype(jnp.int32)

    count = lax.fori_loop(0, panels, step, jnp.int32(0))
    order_ref[panels] = count
    return count


def prep_kernel(
    flags_hbm, rows_hbm, src_hbm, omega_hbm, order_ref, src_pick, omega_pick, row_mat,
    flags, points, picked, row_terms, src_terms, sources, sems, sem, *, slices, place
):
    panels = flags.shape[1]
    rows = points.shape[1]
    me = lax.axis_index("tile")
    at = pl.multiple_of(lax.axis_index("row") * rows, rows) if place else 0
    copies = [
        pltpu.make_async_copy(flags_hbm, flags, sems.at[0]),
        pltpu.make_async_copy(rows_hbm.at[:, pl.ds(at, rows)], points, sems.at[1]),
        pltpu.make_async_copy(src_hbm, sources, sems.at[2]),
    ]
    for copy in copies:
        copy.start()
    copies[0].wait()
    count = order_panels(flags, order_ref, panels)

    def fetch(slot):
        at = pl.multiple_of(order_ref[slot] * WIDTH, WIDTH)
        to = pl.multiple_of(slot * WIDTH, WIDTH)
        return pltpu.make_async_copy(
            omega_hbm.at[pl.ds(at, WIDTH), :], omega_pick.at[pl.ds(to, WIDTH), :], sem
        )

    def start(slot, carry):
        fetch(slot).start()
        return carry

    lax.fori_loop(0, count, start, 0)
    copies[1].wait()
    if place:
        to = 0
        for k, first, size in slices:
            at = pl.multiple_of((me ^ k) * (rows // lax.axis_size("tile")) + first, WIDTH)
            picked[:, to : to + size] = points[:, pl.ds(at, size)]
            to += size
        fill_terms(row_terms, picked[...], 0)
    else:
        fill_terms(row_terms, points[...], 0)
    step = min(512, rows)
    for r in range(0, rows, step):
        row_mat[r : r + step, :] = row_terms[:, r : r + step].T.astype(jnp.bfloat16)
    copies[2].wait()
    fill_terms(src_terms, sources[...], 1)

    def pick(slot, carry):
        at = pl.multiple_of(order_ref[slot] * WIDTH, WIDTH)
        to = pl.multiple_of(slot * WIDTH, WIDTH)
        src_pick[:, pl.ds(to, WIDTH)] = src_terms[:, pl.ds(at, WIDTH)].astype(jnp.bfloat16)
        return carry

    lax.fori_loop(0, count, pick, 0)
    spare = src_terms[:, :WIDTH].astype(jnp.bfloat16)

    def pad(slot, carry):
        to = pl.multiple_of(slot * WIDTH, WIDTH)
        src_pick[:, pl.ds(to, WIDTH)] = spare
        omega_pick[pl.ds(to, WIDTH), :] = jnp.zeros((WIDTH, omega_pick.shape[1]), jnp.bfloat16)
        return carry

    lax.fori_loop(count, GROUP * ((count + GROUP - 1) // GROUP), pad, 0)

    def finish(slot, carry):
        fetch(slot).wait()
        return carry

    lax.fori_loop(0, count, finish, 0)


def in_hbm(x):
    return pltpu.with_memory_space_constraint(x, pltpu.HBM)


def prep(admissible, points, source_points, sketch, rows, slices, place):
    panels = admissible.shape[1]
    cols, rank = sketch.shape
    spare = GROUP * ((panels + GROUP - 1) // GROUP) * WIDTH
    hbm = pl.BlockSpec(memory_space=pltpu.HBM)
    vmem = pl.BlockSpec(memory_space=pltpu.VMEM)
    return pl.pallas_call(
        functools.partial(prep_kernel, slices=slices, place=place),
        in_specs=[hbm] * 4,
        out_specs=[pl.BlockSpec(memory_space=pltpu.SMEM), vmem, vmem, vmem],
        out_shape=[
            jax.ShapeDtypeStruct((panels + 8,), jnp.int32),
            jax.ShapeDtypeStruct((TERMS, spare), jnp.bfloat16),
            jax.ShapeDtypeStruct((spare, rank), jnp.bfloat16),
            jax.ShapeDtypeStruct((rows, TERMS), jnp.bfloat16),
        ],
        scratch_shapes=[
            pltpu.SMEM((1, panels), jnp.int32),
            pltpu.VMEM((3, rows), jnp.float32),
            pltpu.VMEM((3, rows), jnp.float32),
            pltpu.VMEM((TERMS, rows), jnp.float32),
            pltpu.VMEM((TERMS, cols), jnp.float32),
            pltpu.VMEM((3, cols), jnp.float32),
            pltpu.SemaphoreType.DMA((3,)),
            pltpu.SemaphoreType.DMA,
        ],
        compiler_params=pltpu.CompilerParams(vmem_limit_bytes=16 * 2**20),
        name="prep",
    )(*(in_hbm(x) for x in (admissible, points, source_points, sketch)))


def sketch_kernel(
    order_ref, src_pick, omega_pick, row_mat, part_ref, tiles_ref, total, *, first, panels, rb
):
    groups = (order_ref[panels] + GROUP - 1) // GROUP
    cols = GROUP * WIDTH

    def block(b, carry):
        here = pl.ds(pl.multiple_of(b * rb, rb), rb)
        total[...] = jnp.zeros_like(total)

        def body(j, carry):
            at = pl.ds(pl.multiple_of(j * cols, cols), cols)
            rows = row_mat[pl.ds(pl.multiple_of(first + b * rb, rb), rb), :]
            src = src_pick[:, at]
            omega = omega_pick[at, :]
            sums = total[...]
            near = []
            for c in range(0, cols, HALF):
                square = jnp.dot(rows, src[:, c : c + HALF], preferred_element_type=jnp.float32)
                tile = [near_field(square[r : r + PIECE]) for r in range(0, rb, PIECE)]
                tile = jnp.concatenate(tile, axis=0)
                sums += jnp.dot(tile, omega[c : c + HALF], preferred_element_type=jnp.float32)
                near.append(tile)
            total[...] = sums
            for k in range(GROUP):
                tile = near[k * WIDTH // HALF]
                at = k * WIDTH % HALF
                tiles_ref[GROUP * j + k, here, :] = tile[:, at : at + WIDTH]
            return carry

        lax.fori_loop(0, groups, body, 0)
        part_ref[here, :] = total[...]
        return carry

    lax.fori_loop(0, part_ref.shape[0] // rb, block, 0)


def sketch_pass(order, src_pick, omega_pick, row_mat, first, rows, panels):
    rank = omega_pick.shape[1]
    rb = min(512, rows)
    vmem = pl.BlockSpec(memory_space=pltpu.VMEM)
    return pl.pallas_call(
        functools.partial(sketch_kernel, first=first, panels=panels, rb=rb),
        in_specs=[pl.BlockSpec(memory_space=pltpu.SMEM), vmem, vmem, vmem],
        out_specs=[vmem, vmem],
        out_shape=[
            jax.ShapeDtypeStruct((rows, rank), jnp.float32),
            pltpu.VMEM((GROUP * ((panels + GROUP - 1) // GROUP), rows, WIDTH), jnp.bfloat16),
        ],
        scratch_shapes=[
            pltpu.VMEM((rb, rank), jnp.float32),
        ],
        compiler_params=pltpu.CompilerParams(vmem_limit_bytes=10 * 2**20),
        cost_estimate=pl.CostEstimate(
            flops=rows * panels * WIDTH * rank * 16, bytes_accessed=rows * panels * WIDTH * 2, transcendentals=0
        ),
        name="sketch_pass",
    )(order, src_pick, omega_pick, row_mat)


def in_vmem(kernel, out_shape, name):
    def call(*args):
        vmem = pl.BlockSpec(memory_space=pltpu.VMEM)
        return pl.pallas_call(
            kernel,
            in_specs=[vmem] * len(args),
            out_specs=jax.tree.map(lambda _: vmem, out_shape),
            out_shape=out_shape,
            compiler_params=pltpu.CompilerParams(vmem_limit_bytes=8 * 2**20),
            name=name,
        )(*args)

    return call


def pair_sum_kernel(own_ref, got_ref, kept_ref, *sent_refs):
    q = kept_ref.shape[0]
    for k in range(1 + len(sent_refs)):
        part = slice(k * q, (k + 1) * q)
        value = own_ref[part, :] + got_ref[part, :]
        if k == 0:
            kept_ref[...] = value
        else:
            sent_refs[k - 1][...] = value.astype(jnp.bfloat16)


def pair_sum(own, got, slots):
    q, rank = own.shape[0] // slots, own.shape[1]
    shapes = [jax.ShapeDtypeStruct((q, rank), jnp.float32)]
    shapes += [jax.ShapeDtypeStruct((q, rank), jnp.bfloat16)] * (slots - 1)
    return in_vmem(pair_sum_kernel, shapes, "pair_sum")(own, got)


def row_sum_kernel(kept_ref, *refs):
    total = kept_ref[...]
    for ref in refs[:-1]:
        total = total + ref[...].astype(jnp.float32)
    low = head(total)
    refs[-1][...] = (low if refs[-1].shape == low.shape else low.T).astype(jnp.bfloat16)


def row_sum(kept, got, flip):
    shape = kept.shape[::-1] if flip else kept.shape
    return in_vmem(row_sum_kernel, jax.ShapeDtypeStruct(shape, jnp.bfloat16), "row_sum")(kept, *got)


def invert_factor(gram):
    n = gram.shape[0]
    pieces = n // SUB
    lane = lax.broadcasted_iota(jnp.int32, (SUB, n), 1)
    sub = lax.broadcasted_iota(jnp.int32, (SUB, n), 0)
    trace = jnp.zeros((SUB, n), jnp.float32)
    for v in range(pieces):
        trace = trace + jnp.where(lane == sub + v * SUB, gram[v * SUB : (v + 1) * SUB, :], 0.0)
    shift = (SHIFT / n) * jnp.sum(trace)
    a = [
        gram[v * SUB : (v + 1) * SUB, :] + jnp.where(lane == sub + v * SUB, shift, 0.0)
        for v in range(pieces)
    ]
    for b in range(pieces):
        cols = [
            {v: jnp.broadcast_to(a[v][:, b * SUB + c : b * SUB + c + 1], (SUB, n)) for v in range(b, pieces)}
            for c in range(SUB)
        ]
        for c in range(SUB):
            j = b * SUB + c
            pivot = jnp.broadcast_to(cols[c][b][c : c + 1, :], (SUB, n))
            inv = 1.0 / pivot
            row = jnp.broadcast_to(a[b][c : c + 1, :], (SUB, n))
            row = jnp.where(lane == j, 1.0, row)
            nexts = {
                c2: jnp.broadcast_to(cols[c2][b][c : c + 1, :], (SUB, n)) for c2 in range(c + 1, SUB)
            }
            for v in range(b, pieces):
                m = cols[c][v] * inv
                here = lane == j
                if v == b:
                    m = jnp.where(sub > c, m, 0.0)
                    here = here & (sub > c)
                a[v] = jnp.where(here, 0.0, a[v]) - m * row
                for c2 in range(c + 1, SUB):
                    cols[c2][v] = cols[c2][v] - m * nexts[c2]
    out = []
    for v in range(pieces):
        diag = lane == sub + v * SUB
        d = jnp.sum(jnp.where(diag, a[v], 0.0), axis=1, keepdims=True)
        low = jnp.where(lane < sub + v * SUB, a[v], jnp.where(diag, 1.0, 0.0))
        out.append(low * lax.rsqrt(d))
    return jnp.concatenate(out, axis=0)


def project_kernel(order_ref, *refs, panels, calls, own_at, flip):
    low_refs = refs[: -(calls + 3)]
    tile_refs = refs[-(calls + 3) : -3]
    basis_ref, out_ref, low_all = refs[-3:]
    count = order_ref[panels]
    q = low_refs[0].shape[1 if flip else 0]
    for i, ref in enumerate(low_refs):
        if flip:
            low_all[:, i * q : (i + 1) * q] = ref[...]
        else:
            low_all[i * q : (i + 1) * q, :] = ref[...]
    low_t = low_all[...] if flip else low_all[...].T
    gram = lax.dot_general(low_t, low_t, (((1,), (1,)), ((), ())), preferred_element_type=jnp.float32)
    inverse = [p.astype(jnp.bfloat16) for p in three(invert_factor(gram))]
    out_ref[...] = jnp.zeros_like(out_ref)
    parts = [jnp.dot(p, low_t, preferred_element_type=jnp.float32) for p in inverse]
    basis = parts[0] + (parts[1] + parts[2])
    basis_t = basis.astype(jnp.bfloat16)
    for i, at in enumerate(own_at):
        basis_ref[i * q : (i + 1) * q, :] = basis[:, at * q : (at + 1) * q].T

    def group(j, carry):
        tile = jnp.concatenate(
            [
                jnp.concatenate([ref[FEW * j + k] for k in range(FEW)], axis=1)
                for ref in tile_refs
            ],
            axis=0,
        )
        cols = jnp.dot(basis_t, tile, preferred_element_type=jnp.float32).astype(jnp.bfloat16)
        for k in range(FEW):

            @pl.when(FEW * j + k < count)
            def _():
                at = pl.multiple_of(order_ref[FEW * j + k] * WIDTH, WIDTH)
                out_ref[0, :, pl.ds(at, WIDTH)] = cols[:, k * WIDTH : (k + 1) * WIDTH]

        return carry

    lax.fori_loop(0, (count + FEW - 1) // FEW, group, 0)


def project_pass(order, lows, tiles, own_at, panels, rank, flip):
    rows = sum(t.shape[1] for t in tiles)
    q = lows[0].shape[1 if flip else 0]
    vmem = pl.BlockSpec(memory_space=pltpu.VMEM)
    return pl.pallas_call(
        functools.partial(
            project_kernel, panels=panels, calls=len(tiles), own_at=own_at, flip=flip
        ),
        in_specs=[pl.BlockSpec(memory_space=pltpu.SMEM)]
        + [vmem] * len(lows)
        + [vmem] * len(tiles),
        out_specs=[vmem, vmem],
        out_shape=[
            jax.ShapeDtypeStruct((q * len(own_at), rank), jnp.float32),
            jax.ShapeDtypeStruct((1, rank, panels * WIDTH), jnp.bfloat16),
        ],
        scratch_shapes=[
            pltpu.VMEM((rank, rows) if flip else (rows, rank), jnp.bfloat16),
        ],
        compiler_params=pltpu.CompilerParams(vmem_limit_bytes=16 * 2**20),
        name="project_pass",
    )(order, *lows, *(pltpu.with_memory_space_constraint(x, pltpu.VMEM) for x in tiles))


def after(x, *deps):
    return lax.optimization_barrier((x, *deps))[0]


def swap(x, k, n):
    return lax.ppermute(x, "tile", [(i, i ^ k) for i in range(n)])


CHUNKS = 2


def local(row_points, source_points, sketch, admissible):
    n = lax.axis_size("tile")
    panels = admissible.shape[1]
    rows = row_points.shape[1] // lax.axis_size("row")
    own_rows = rows // n
    q = own_rows // CHUNKS
    odd, even = list(range(1, n, 2)), list(range(0, n, 2))
    slices = [(k, c * q, q) for c in range(CHUNKS) for k in odd + even]
    place = flip = q % WIDTH == 0
    points = row_points
    if not place:
        me = lax.axis_index("tile")
        points = lax.dynamic_slice_in_dim(row_points, lax.axis_index("row") * rows, rows, 1)
        points = jnp.concatenate(
            [lax.dynamic_slice_in_dim(points, (me ^ k) * own_rows + first, q, 1) for k, first, _ in slices], 1
        )
    order, src_pick, omega_pick, row_mat = prep(
        admissible, points, source_points, sketch, rows, slices, place
    )

    call_rows = rows // CHUNKS // 2

    def sketch_part(at, *deps):
        return sketch_pass(
            after(order, *deps), src_pick, omega_pick, row_mat, at * call_rows, call_rows, panels
        )

    def sum_cores(got, own):
        kept, *sent = pair_sum(own, got, n // 2)
        return kept, [swap(x, k, n) for x, k in zip(sent, even[1:])]

    def along_z(kept, got):
        low = row_sum(kept, got, flip)
        return [low] + [swap(low, k, n) for k in even[1:]]

    held, tiles, sums, last = [], [], None, ()
    for c in range(CHUNKS):
        theirs, kept = sketch_part(2 * c, *last)
        tiles.append(kept)
        got = swap(theirs, 1, n)
        if c > 0:
            held.append(along_z(after(sums[0], theirs), sums[1]))
        own, kept = sketch_part(2 * c + 1, theirs, *[h[0] for h in held[-1:]])
        tiles.append(kept)
        sums = sum_cores(got, after(own, *(x for h in held[-1:] for x in h)))
        last = (own, sums[0])
    held.append(along_z(*sums))
    lows = [x for h in held for x in [swap(y, 1, n) for y in h] + h]
    own_at = [c * n + n // 2 for c in range(CHUNKS)]
    return project_pass(order, lows, tiles, own_at, panels, sketch.shape[1], flip)


def solution(mesh):
    in_specs = (P(), P(None, "tile"), P("tile", None), P("row", "tile"))
    out_specs = (P(("row", "tile"), None), P("row", None, "tile"))
    return jax.shard_map(local, mesh=mesh, in_specs=in_specs, out_specs=out_specs, check_vma=False)
```

```python
import functools
import math

import jax
import jax.numpy as jnp
from jax import lax
from jax.experimental import pallas as pl
from jax.experimental.pallas import tpu as pltpu
from jax.sharding import PartitionSpec as P

DAMPING = 0.25
WAVENUM = 24.0
SHIFT = 0.0001

TURNS = WAVENUM / (2.0 * math.pi)
DECAY = -DAMPING / TURNS / math.log(2.0)
AMP = TURNS / (4.0 * math.pi)
S0, S1, S2 = 6.28127979 * AMP, -41.0952178 * AMP, 73.5851113 * AMP

WIDTH = 128
PAIR = 2 * WIDTH
TERMS = 32
SUB = 8
PIECE = 16
GROUP = 8
FEW = 4
HALF = FEW * WIDTH
WHOLE = 1.5 * 2.0**23


def head(x):
    return x.astype(jnp.bfloat16).astype(jnp.float32)


def three(x):
    a = head(x)
    b = head(x - a)
    return a, b, x - a - b


def fill_terms(ref, points, side):
    at = lax.broadcasted_iota(jnp.int32, points.shape, 0)
    x = points - jnp.where(at == 2, -0.5, 3.0)
    scale = TURNS * TURNS
    norm = three(scale * jnp.sum(x * x, axis=0, keepdims=True))
    one = jnp.ones_like(norm[0])
    if side == 0:
        h, m, l = three(x)
        rows = [h, h, m, h, l, m]
        tail = [*norm, one, one, one]
    else:
        h, m, l = three(x * (-2.0 * scale))
        rows = [h, m, h, l, h, m]
        tail = [one, one, one, *norm]
    ref[...] = jnp.zeros_like(ref)
    for at, row in enumerate(rows):
        ref[3 * at : 3 * at + 3, :] = row
    for at, row in enumerate(tail):
        ref[18 + at : 19 + at, :] = row


def near_field(square):
    inv = lax.rsqrt(square)
    t = square * inv
    f = t - ((t + WHOLE) - WHOLE)
    g = 0.25 - jnp.abs(f)
    v = g * g
    wave = ((S2 * v + S1) * v + S0) * g
    amp = jnp.exp2(DECAY * t) * inv
    return (wave * amp).astype(jnp.bfloat16)


def order_panels(flags_ref, order_ref, panels):
    def step(p, count):
        @pl.when(flags_ref[0, p] > 0)
        def _():
            order_ref[count] = p

        return count + (flags_ref[0, p] > 0).astype(jnp.int32)

    count = lax.fori_loop(0, panels, step, jnp.int32(0))
    order_ref[panels] = count
    return count


def prep_kernel(
    flags_hbm, rows_hbm, src_hbm, omega_hbm, order_ref, src_pick, omega_pick, row_mat,
    flags, points, picked, row_terms, src_terms, sources, sems, sem, *, slices, place
):
    panels = flags.shape[1]
    rows = points.shape[1]
    me = lax.axis_index("tile")
    at = pl.multiple_of(lax.axis_index("row") * rows, rows) if place else 0
    copies = [
        pltpu.make_async_copy(flags_hbm, flags, sems.at[0]),
        pltpu.make_async_copy(rows_hbm.at[:, pl.ds(at, rows)], points, sems.at[1]),
        pltpu.make_async_copy(src_hbm, sources, sems.at[2]),
    ]
    for copy in copies:
        copy.start()
    copies[0].wait()
    count = order_panels(flags, order_ref, panels)

    def fetch(slot):
        at = pl.multiple_of(order_ref[slot] * WIDTH, WIDTH)
        to = pl.multiple_of(slot * WIDTH, WIDTH)
        return pltpu.make_async_copy(
            omega_hbm.at[pl.ds(at, WIDTH), :], omega_pick.at[pl.ds(to, WIDTH), :], sem
        )

    def start(slot, carry):
        fetch(slot).start()
        return carry

    lax.fori_loop(0, count, start, 0)
    copies[1].wait()
    if place:
        to = 0
        for k, first, size in slices:
            at = pl.multiple_of((me ^ k) * (rows // lax.axis_size("tile")) + first, WIDTH)
            picked[:, to : to + size] = points[:, pl.ds(at, size)]
            to += size
        fill_terms(row_terms, picked[...], 0)
    else:
        fill_terms(row_terms, points[...], 0)
    step = min(512, rows)
    for r in range(0, rows, step):
        row_mat[r : r + step, :] = row_terms[:, r : r + step].T.astype(jnp.bfloat16)
    copies[2].wait()
    fill_terms(src_terms, sources[...], 1)

    def pick(slot, carry):
        at = pl.multiple_of(order_ref[slot] * WIDTH, WIDTH)
        to = pl.multiple_of(slot * WIDTH, WIDTH)
        src_pick[:, pl.ds(to, WIDTH)] = src_terms[:, pl.ds(at, WIDTH)].astype(jnp.bfloat16)
        return carry

    lax.fori_loop(0, count, pick, 0)
    spare = src_terms[:, :WIDTH].astype(jnp.bfloat16)

    def pad(slot, carry):
        to = pl.multiple_of(slot * WIDTH, WIDTH)
        src_pick[:, pl.ds(to, WIDTH)] = spare
        omega_pick[pl.ds(to, WIDTH), :] = jnp.zeros((WIDTH, omega_pick.shape[1]), jnp.bfloat16)
        return carry

    lax.fori_loop(count, GROUP * ((count + GROUP - 1) // GROUP), pad, 0)

    def finish(slot, carry):
        fetch(slot).wait()
        return carry

    lax.fori_loop(0, count, finish, 0)


def in_hbm(x):
    return pltpu.with_memory_space_constraint(x, pltpu.HBM)


def prep(admissible, points, source_points, sketch, rows, slices, place):
    panels = admissible.shape[1]
    cols, rank = sketch.shape
    spare = GROUP * ((panels + GROUP - 1) // GROUP) * WIDTH
    hbm = pl.BlockSpec(memory_space=pltpu.HBM)
    vmem = pl.BlockSpec(memory_space=pltpu.VMEM)
    return pl.pallas_call(
        functools.partial(prep_kernel, slices=slices, place=place),
        in_specs=[hbm] * 4,
        out_specs=[pl.BlockSpec(memory_space=pltpu.SMEM), vmem, vmem, vmem],
        out_shape=[
            jax.ShapeDtypeStruct((panels + 8,), jnp.int32),
            jax.ShapeDtypeStruct((TERMS, spare), jnp.bfloat16),
            jax.ShapeDtypeStruct((spare, rank), jnp.bfloat16),
            jax.ShapeDtypeStruct((rows, TERMS), jnp.bfloat16),
        ],
        scratch_shapes=[
            pltpu.SMEM((1, panels), jnp.int32),
            pltpu.VMEM((3, rows), jnp.float32),
            pltpu.VMEM((3, rows), jnp.float32),
            pltpu.VMEM((TERMS, rows), jnp.float32),
            pltpu.VMEM((TERMS, cols), jnp.float32),
            pltpu.VMEM((3, cols), jnp.float32),
            pltpu.SemaphoreType.DMA((3,)),
            pltpu.SemaphoreType.DMA,
        ],
        compiler_params=pltpu.CompilerParams(vmem_limit_bytes=16 * 2**20),
        name="prep",
    )(*(in_hbm(x) for x in (admissible, points, source_points, sketch)))


def sketch_kernel(
    order_ref, src_pick, omega_pick, row_mat, part_ref, tiles_ref, total, *, first, panels, rb
):
    groups = (order_ref[panels] + GROUP - 1) // GROUP
    cols = GROUP * WIDTH

    def block(b, carry):
        here = pl.ds(pl.multiple_of(b * rb, rb), rb)
        total[...] = jnp.zeros_like(total)

        def body(j, carry):
            at = pl.ds(pl.multiple_of(j * cols, cols), cols)
            rows = row_mat[pl.ds(pl.multiple_of(first + b * rb, rb), rb), :]
            src = src_pick[:, at]
            omega = omega_pick[at, :]
            sums = total[...]
            near = []
            for c in range(0, cols, HALF):
                square = jnp.dot(rows, src[:, c : c + HALF], preferred_element_type=jnp.float32)
                tile = [near_field(square[r : r + PIECE]) for r in range(0, rb, PIECE)]
                tile = jnp.concatenate(tile, axis=0)
                sums += jnp.dot(tile, omega[c : c + HALF], preferred_element_type=jnp.float32)
                near.append(tile)
            total[...] = sums
            for k in range(GROUP):
                tile = near[k * WIDTH // HALF]
                at = k * WIDTH % HALF
                tiles_ref[GROUP * j + k, here, :] = tile[:, at : at + WIDTH]
            return carry

        lax.fori_loop(0, groups, body, 0)
        part_ref[here, :] = total[...]
        return carry

    lax.fori_loop(0, part_ref.shape[0] // rb, block, 0)


def sketch_pass(order, src_pick, omega_pick, row_mat, first, rows, panels):
    rank = omega_pick.shape[1]
    rb = min(512, rows)
    vmem = pl.BlockSpec(memory_space=pltpu.VMEM)
    return pl.pallas_call(
        functools.partial(sketch_kernel, first=first, panels=panels, rb=rb),
        in_specs=[pl.BlockSpec(memory_space=pltpu.SMEM), vmem, vmem, vmem],
        out_specs=[vmem, vmem],
        out_shape=[
            jax.ShapeDtypeStruct((rows, rank), jnp.float32),
            pltpu.VMEM((GROUP * ((panels + GROUP - 1) // GROUP), rows, WIDTH), jnp.bfloat16),
        ],
        scratch_shapes=[
            pltpu.VMEM((rb, rank), jnp.float32),
        ],
        compiler_params=pltpu.CompilerParams(vmem_limit_bytes=10 * 2**20),
        cost_estimate=pl.CostEstimate(
            flops=rows * panels * WIDTH * rank * 16, bytes_accessed=rows * panels * WIDTH * 2, transcendentals=0
        ),
        name="sketch_pass",
    )(order, src_pick, omega_pick, row_mat)


def in_vmem(kernel, out_shape, name):
    def call(*args):
        vmem = pl.BlockSpec(memory_space=pltpu.VMEM)
        return pl.pallas_call(
            kernel,
            in_specs=[vmem] * len(args),
            out_specs=jax.tree.map(lambda _: vmem, out_shape),
            out_shape=out_shape,
            compiler_params=pltpu.CompilerParams(vmem_limit_bytes=8 * 2**20),
            name=name,
        )(*args)

    return call


def pair_sum_kernel(own_ref, got_ref, kept_ref, *sent_refs):
    q = kept_ref.shape[0]
    for k in range(1 + len(sent_refs)):
        part = slice(k * q, (k + 1) * q)
        value = own_ref[part, :] + got_ref[part, :]
        if k == 0:
            kept_ref[...] = value
        else:
            sent_refs[k - 1][...] = value.astype(jnp.bfloat16)


def pair_sum(own, got, slots):
    q, rank = own.shape[0] // slots, own.shape[1]
    shapes = [jax.ShapeDtypeStruct((q, rank), jnp.float32)]
    shapes += [jax.ShapeDtypeStruct((q, rank), jnp.bfloat16)] * (slots - 1)
    return in_vmem(pair_sum_kernel, shapes, "pair_sum")(own, got)


def row_sum_kernel(kept_ref, *refs):
    total = kept_ref[...]
    for ref in refs[:-1]:
        total = total + ref[...].astype(jnp.float32)
    low = head(total)
    refs[-1][...] = (low if refs[-1].shape == low.shape else low.T).astype(jnp.bfloat16)


def row_sum(kept, got, flip):
    shape = kept.shape[::-1] if flip else kept.shape
    return in_vmem(row_sum_kernel, jax.ShapeDtypeStruct(shape, jnp.bfloat16), "row_sum")(kept, *got)


def invert_factor(gram, beside):
    n = gram.shape[0]
    pieces = n // SUB
    lane = lax.broadcasted_iota(jnp.int32, (SUB, n), 1)
    sub = lax.broadcasted_iota(jnp.int32, (SUB, n), 0)
    trace = jnp.zeros((SUB, n), jnp.float32)
    for v in range(pieces):
        trace = trace + jnp.where(lane == sub + v * SUB, gram[v * SUB : (v + 1) * SUB, :], 0.0)
    shift = (SHIFT / n) * jnp.sum(trace)
    a = [
        gram[v * SUB : (v + 1) * SUB, :] + jnp.where(lane == sub + v * SUB, shift, 0.0)
        for v in range(pieces)
    ]
    for b in range(pieces):
        beside(b)
        cols = [
            {v: jnp.broadcast_to(a[v][:, b * SUB + c : b * SUB + c + 1], (SUB, n)) for v in range(b, pieces)}
            for c in range(SUB)
        ]
        for c in range(SUB):
            j = b * SUB + c
            pivot = jnp.broadcast_to(cols[c][b][c : c + 1, :], (SUB, n))
            inv = 1.0 / pivot
            row = jnp.broadcast_to(a[b][c : c + 1, :], (SUB, n))
            row = jnp.where(lane == j, 1.0, row)
            nexts = {
                c2: jnp.broadcast_to(cols[c2][b][c : c + 1, :], (SUB, n)) for c2 in range(c + 1, SUB)
            }
            for v in range(b, pieces):
                m = cols[c][v] * inv
                here = lane == j
                if v == b:
                    m = jnp.where(sub > c, m, 0.0)
                    here = here & (sub > c)
                a[v] = jnp.where(here, 0.0, a[v]) - m * row
                for c2 in range(c + 1, SUB):
                    cols[c2][v] = cols[c2][v] - m * nexts[c2]
    out = []
    for v in range(pieces):
        diag = lane == sub + v * SUB
        d = jnp.sum(jnp.where(diag, a[v], 0.0), axis=1, keepdims=True)
        low = jnp.where(lane < sub + v * SUB, a[v], jnp.where(diag, 1.0, 0.0))
        out.append(low * lax.rsqrt(d))
    return jnp.concatenate(out, axis=0)


def gather_low(odd_ref, even_refs, low_all, flip):
    half, q = odd_ref.shape[0], odd_ref.shape[2 if flip else 1]
    pieces = [odd_ref.at[k] for k in range(half)] + list(even_refs)
    for i, ref in enumerate(pieces):
        if flip:
            low_all[:, i * q : (i + 1) * q] = ref[...]
        else:
            low_all[i * q : (i + 1) * q, :] = ref[...]
    return low_all[...] if flip else low_all[...].T


def self_product(low_t):
    return lax.dot_general(low_t, low_t, (((1,), (1,)), ((), ())), preferred_element_type=jnp.float32)


def side_by_side(tile_refs, first, count):
    return jnp.concatenate(
        [jnp.concatenate([ref[first + k] for k in range(count)], axis=1) for ref in tile_refs], axis=0
    )


def first_kernel(order_ref, odd_ref, *refs, panels, half, flip):
    even_refs, tile_refs = refs[:half], refs[half:-3]
    product_ref, gram_ref, low_all = refs[-3:]
    low_t = gather_low(odd_ref, even_refs, low_all, flip)
    gram_ref[...] = self_product(low_t)

    def group(j, carry):
        at = pl.ds(pl.multiple_of(j * HALF, HALF), HALF)
        product_ref[:, at] = jnp.dot(
            low_t, side_by_side(tile_refs, FEW * j, FEW), preferred_element_type=jnp.float32
        )
        return carry

    lax.fori_loop(0, (order_ref[panels] + FEW - 1) // FEW, group, 0)


def first_pass(order, odd, even, tiles, panels, rank, flip):
    rows = sum(t.shape[1] for t in tiles)
    held = tiles[0].shape[0]
    vmem = pl.BlockSpec(memory_space=pltpu.VMEM)
    return pl.pallas_call(
        functools.partial(first_kernel, panels=panels, half=len(even), flip=flip),
        in_specs=[pl.BlockSpec(memory_space=pltpu.SMEM)] + [vmem] * (1 + len(even) + len(tiles)),
        out_specs=[vmem, vmem],
        out_shape=[
            jax.ShapeDtypeStruct((rank, held * WIDTH), jnp.float32),
            jax.ShapeDtypeStruct((rank, rank), jnp.float32),
        ],
        scratch_shapes=[pltpu.VMEM((rank, rows) if flip else (rows, rank), jnp.bfloat16)],
        compiler_params=pltpu.CompilerParams(vmem_limit_bytes=12 * 2**20),
        cost_estimate=pl.CostEstimate(
            flops=2 * rows * panels * WIDTH * rank, bytes_accessed=0, transcendentals=0
        ),
        name="first_pass",
    )(order, odd, *even, *(pltpu.with_memory_space_constraint(x, pltpu.VMEM) for x in tiles))


def project_kernel(order_ref, first_ref, gram_ref, odd_ref, *refs, panels, half, owns, flip):
    own_refs, even_refs = refs[:owns], refs[owns : owns + half]
    tile_refs = refs[owns + half : -4]
    basis_ref, out_ref, low_all, product = refs[-4:]
    count = order_ref[panels]
    low_t = gather_low(odd_ref, even_refs, low_all, flip)
    out_ref[...] = jnp.zeros_like(out_ref)
    pairs = tile_refs[0].shape[0] // 2
    blocks = gram_ref.shape[0] // SUB

    def beside(b):
        for j in range(b * pairs // blocks, (b + 1) * pairs // blocks):
            at = slice(j * PAIR, (j + 1) * PAIR)
            product[:, at] = first_ref[:, at] + jnp.dot(
                low_t, side_by_side(tile_refs, 2 * j, 2), preferred_element_type=jnp.float32
            )

    inverse = three(invert_factor(gram_ref[...] + self_product(low_t), beside))
    rank = inverse[0].shape[0]
    stack = jnp.concatenate(inverse, axis=0).astype(jnp.bfloat16)
    q = own_refs[0].shape[1 if flip else 0]
    for i, ref in enumerate(own_refs):
        own = ref[...] if flip else ref[...].T
        parts = jnp.dot(stack, own, preferred_element_type=jnp.float32)
        basis = parts[:rank] + (parts[rank : 2 * rank] + parts[2 * rank :])
        basis_ref[i * q : (i + 1) * q, :] = basis.T

    def group(j, carry):
        parts = three(product[:, pl.ds(pl.multiple_of(j * HALF, HALF), HALF)])
        cols, rest = 0.0, 0.0
        for k, part in enumerate(parts):
            got = jnp.dot(
                stack[: (3 - k) * rank], part.astype(jnp.bfloat16), preferred_element_type=jnp.float32
            )
            for i in range(3 - k):
                if i + k == 0:
                    cols = got[:rank]
                else:
                    rest = rest + got[i * rank : (i + 1) * rank]
        cols = (cols + rest).astype(jnp.bfloat16)
        for k in range(FEW):

            @pl.when(FEW * j + k < count)
            def _():
                at = pl.multiple_of(order_ref[FEW * j + k] * WIDTH, WIDTH)
                out_ref[0, :, pl.ds(at, WIDTH)] = cols[:, k * WIDTH : (k + 1) * WIDTH]

        return carry

    lax.fori_loop(0, (count + FEW - 1) // FEW, group, 0)


def project_pass(order, first, gram, odd, owns, even, tiles, panels, rank, flip):
    rows = sum(t.shape[1] for t in tiles)
    held = tiles[0].shape[0]
    q = owns[0].shape[1 if flip else 0]
    vmem = pl.BlockSpec(memory_space=pltpu.VMEM)
    return pl.pallas_call(
        functools.partial(
            project_kernel, panels=panels, half=len(even), owns=len(owns), flip=flip
        ),
        in_specs=[pl.BlockSpec(memory_space=pltpu.SMEM)]
        + [vmem] * (3 + len(owns) + len(even) + len(tiles)),
        out_specs=[vmem, vmem],
        out_shape=[
            jax.ShapeDtypeStruct((q * len(owns), rank), jnp.float32),
            jax.ShapeDtypeStruct((1, rank, panels * WIDTH), jnp.bfloat16),
        ],
        scratch_shapes=[
            pltpu.VMEM((rank, rows) if flip else (rows, rank), jnp.bfloat16),
            pltpu.VMEM((rank, held * WIDTH), jnp.float32),
        ],
        compiler_params=pltpu.CompilerParams(vmem_limit_bytes=14 * 2**20),
        name="project_pass",
    )(
        order, first, gram, odd, *owns, *even,
        *(pltpu.with_memory_space_constraint(x, pltpu.VMEM) for x in tiles),
    )


def join_kernel(*refs):
    for k, ref in enumerate(refs[:-1]):
        refs[-1][k] = ref[...]


def join(parts):
    shape = jax.ShapeDtypeStruct((len(parts), *parts[0].shape), parts[0].dtype)
    return in_vmem(join_kernel, shape, "join")(*parts)


def after(x, *deps):
    return lax.optimization_barrier((x, *deps))[0]


def swap(x, k, n):
    return lax.ppermute(x, "tile", [(i, i ^ k) for i in range(n)])


CHUNKS = 2


def local(row_points, source_points, sketch, admissible):
    n = lax.axis_size("tile")
    panels = admissible.shape[1]
    rows = row_points.shape[1] // lax.axis_size("row")
    own_rows = rows // n
    q = own_rows // CHUNKS
    odd, even = list(range(1, n, 2)), list(range(0, n, 2))
    slices = [(k, c * q, q) for c in range(CHUNKS) for k in odd + even]
    place = flip = q % WIDTH == 0
    points = row_points
    if not place:
        me = lax.axis_index("tile")
        points = lax.dynamic_slice_in_dim(row_points, lax.axis_index("row") * rows, rows, 1)
        points = jnp.concatenate(
            [lax.dynamic_slice_in_dim(points, (me ^ k) * own_rows + first, q, 1) for k, first, _ in slices], 1
        )
    order, src_pick, omega_pick, row_mat = prep(
        admissible, points, source_points, sketch, rows, slices, place
    )

    call_rows = rows // CHUNKS // 2

    def sketch_part(at, *deps):
        return sketch_pass(
            after(order, *deps), src_pick, omega_pick, row_mat, at * call_rows, call_rows, panels
        )

    def sum_cores(got, own):
        kept, *sent = pair_sum(own, got, n // 2)
        return kept, [swap(x, k, n) for x, k in zip(sent, even[1:])]

    def along_z(kept, got):
        low = row_sum(kept, got, flip)
        return [low] + [swap(low, k, n) for k in even[1:]]

    held, tiles, sums, last = [], [], None, ()
    for c in range(CHUNKS):
        theirs, kept = sketch_part(2 * c, *last)
        tiles.append(kept)
        got = swap(theirs, 1, n)
        if c > 0:
            held.append(along_z(after(sums[0], theirs), sums[1]))
        own, kept = sketch_part(2 * c + 1, theirs, *[h[0] for h in held[-1:]])
        tiles.append(kept)
        sums = sum_cores(got, after(own, *(x for h in held[-1:] for x in h)))
        last = (own, sums[0])
    held.append(along_z(*sums))
    rank = sketch.shape[1]
    odds = [swap(join([after(h[0], own), *h[1:]]), 1, n) for h in held]
    first, gram = first_pass(order, odds[0], held[0], tiles[:2], panels, rank, flip)
    owns = [h[0] for h in held]
    return project_pass(
        order, first, gram, odds[1], owns, held[1], tiles[2:], panels, rank, flip
    )


def solution(mesh):
    in_specs = (P(), P(None, "tile"), P("tile", None), P("row", "tile"))
    out_specs = (P(("row", "tile"), None), P("row", None, "tile"))
    return jax.shard_map(local, mesh=mesh, in_specs=in_specs, out_specs=out_specs, check_vma=False)
```

```python
import functools
import math

import jax
import jax.numpy as jnp
from jax import lax
from jax.experimental import pallas as pl
from jax.experimental.pallas import tpu as pltpu
from jax.sharding import PartitionSpec as P

DAMPING = 0.25
WAVENUM = 24.0
SHIFT = 0.0001

TURNS = WAVENUM / (2.0 * math.pi)
DECAY = -DAMPING / TURNS / math.log(2.0)
AMP = TURNS / (4.0 * math.pi)
S0, S1, S2 = 6.28127979 * AMP, -41.0952178 * AMP, 73.5851113 * AMP

WIDTH = 128
PAIR = 2 * WIDTH
TERMS = 32
SUB = 8
PIECE = 16
GROUP = 8
FEW = 4
HALF = FEW * WIDTH


def head(x):
    return x.astype(jnp.bfloat16).astype(jnp.float32)


def three(x):
    a = head(x)
    b = head(x - a)
    return a, b, x - a - b


def fill_terms(ref, points, side):
    at = lax.broadcasted_iota(jnp.int32, points.shape, 0)
    x = points - jnp.where(at == 2, -0.5, 3.0)
    scale = TURNS * TURNS
    norm = three(scale * jnp.sum(x * x, axis=0, keepdims=True))
    one = jnp.ones_like(norm[0])
    if side == 0:
        h, m, l = three(x)
        rows = [h, h, m, h, l, m]
        tail = [*norm, one, one, one]
    else:
        h, m, l = three(x * (-2.0 * scale))
        rows = [h, m, h, l, h, m]
        tail = [one, one, one, *norm]
    ref[...] = jnp.zeros_like(ref)
    for at, row in enumerate(rows):
        ref[3 * at : 3 * at + 3, :] = row
    for at, row in enumerate(tail):
        ref[18 + at : 19 + at, :] = row


def near_field(square):
    inv = lax.rsqrt(square)
    t = square * inv
    f = t - jnp.round(t)
    g = 0.25 - jnp.abs(f)
    v = g * g
    wave = ((S2 * v + S1) * v + S0) * g
    amp = jnp.exp2(DECAY * t) * inv
    return (wave * amp).astype(jnp.bfloat16)


def order_panels(flags_ref, order_ref, panels):
    def step(p, count):
        @pl.when(flags_ref[0, p] > 0)
        def _():
            order_ref[count] = p

        return count + (flags_ref[0, p] > 0).astype(jnp.int32)

    count = lax.fori_loop(0, panels, step, jnp.int32(0))
    order_ref[panels] = count
    return count


def prep_kernel(
    flags_hbm, rows_hbm, src_hbm, omega_hbm, order_ref, src_pick, omega_pick, row_mat,
    flags, points, picked, row_terms, src_terms, sources, sems, sem, *, slices, place
):
    panels = flags.shape[1]
    rows = points.shape[1]
    me = lax.axis_index("tile")
    at = pl.multiple_of(lax.axis_index("row") * rows, rows) if place else 0
    copies = [
        pltpu.make_async_copy(flags_hbm, flags, sems.at[0]),
        pltpu.make_async_copy(rows_hbm.at[:, pl.ds(at, rows)], points, sems.at[1]),
        pltpu.make_async_copy(src_hbm, sources, sems.at[2]),
    ]
    for copy in copies:
        copy.start()
    copies[0].wait()
    count = order_panels(flags, order_ref, panels)

    def fetch(slot):
        at = pl.multiple_of(order_ref[slot] * WIDTH, WIDTH)
        to = pl.multiple_of(slot * WIDTH, WIDTH)
        return pltpu.make_async_copy(
            omega_hbm.at[pl.ds(at, WIDTH), :], omega_pick.at[pl.ds(to, WIDTH), :], sem
        )

    def start(slot, carry):
        fetch(slot).start()
        return carry

    lax.fori_loop(0, count, start, 0)
    copies[1].wait()
    if place:
        to = 0
        for k, first, size in slices:
            at = pl.multiple_of((me ^ k) * (rows // lax.axis_size("tile")) + first, WIDTH)
            picked[:, to : to + size] = points[:, pl.ds(at, size)]
            to += size
        fill_terms(row_terms, picked[...], 0)
    else:
        fill_terms(row_terms, points[...], 0)
    step = min(512, rows)
    for r in range(0, rows, step):
        row_mat[r : r + step, :] = row_terms[:, r : r + step].T.astype(jnp.bfloat16)
    copies[2].wait()
    fill_terms(src_terms, sources[...], 1)

    def pick(slot, carry):
        at = pl.multiple_of(order_ref[slot] * WIDTH, WIDTH)
        to = pl.multiple_of(slot * WIDTH, WIDTH)
        src_pick[:, pl.ds(to, WIDTH)] = src_terms[:, pl.ds(at, WIDTH)].astype(jnp.bfloat16)
        return carry

    lax.fori_loop(0, count, pick, 0)
    spare = src_terms[:, :WIDTH].astype(jnp.bfloat16)

    def pad(slot, carry):
        to = pl.multiple_of(slot * WIDTH, WIDTH)
        src_pick[:, pl.ds(to, WIDTH)] = spare
        omega_pick[pl.ds(to, WIDTH), :] = jnp.zeros((WIDTH, omega_pick.shape[1]), jnp.bfloat16)
        return carry

    lax.fori_loop(count, GROUP * ((count + GROUP - 1) // GROUP), pad, 0)

    def finish(slot, carry):
        fetch(slot).wait()
        return carry

    lax.fori_loop(0, count, finish, 0)


def in_hbm(x):
    return pltpu.with_memory_space_constraint(x, pltpu.HBM)


def prep(admissible, points, source_points, sketch, rows, slices, place):
    panels = admissible.shape[1]
    cols, rank = sketch.shape
    spare = GROUP * ((panels + GROUP - 1) // GROUP) * WIDTH
    hbm = pl.BlockSpec(memory_space=pltpu.HBM)
    vmem = pl.BlockSpec(memory_space=pltpu.VMEM)
    return pl.pallas_call(
        functools.partial(prep_kernel, slices=slices, place=place),
        in_specs=[hbm] * 4,
        out_specs=[pl.BlockSpec(memory_space=pltpu.SMEM), vmem, vmem, vmem],
        out_shape=[
            jax.ShapeDtypeStruct((panels + 8,), jnp.int32),
            jax.ShapeDtypeStruct((TERMS, spare), jnp.bfloat16),
            jax.ShapeDtypeStruct((spare, rank), jnp.bfloat16),
            jax.ShapeDtypeStruct((rows, TERMS), jnp.bfloat16),
        ],
        scratch_shapes=[
            pltpu.SMEM((1, panels), jnp.int32),
            pltpu.VMEM((3, rows), jnp.float32),
            pltpu.VMEM((3, rows), jnp.float32),
            pltpu.VMEM((TERMS, rows), jnp.float32),
            pltpu.VMEM((TERMS, cols), jnp.float32),
            pltpu.VMEM((3, cols), jnp.float32),
            pltpu.SemaphoreType.DMA((3,)),
            pltpu.SemaphoreType.DMA,
        ],
        compiler_params=pltpu.CompilerParams(vmem_limit_bytes=16 * 2**20),
        name="prep",
    )(*(in_hbm(x) for x in (admissible, points, source_points, sketch)))


def sketch_kernel(
    order_ref, src_pick, omega_pick, row_mat, part_ref, tiles_ref, total, *, first, panels, rb
):
    groups = (order_ref[panels] + GROUP - 1) // GROUP
    cols = GROUP * WIDTH

    def block(b, carry):
        here = pl.ds(pl.multiple_of(b * rb, rb), rb)
        total[...] = jnp.zeros_like(total)

        def body(j, carry):
            at = pl.ds(pl.multiple_of(j * cols, cols), cols)
            rows = row_mat[pl.ds(pl.multiple_of(first + b * rb, rb), rb), :]
            src = src_pick[:, at]
            omega = omega_pick[at, :]
            sums = total[...]
            near = []
            for c in range(0, cols, HALF):
                square = jnp.dot(rows, src[:, c : c + HALF], preferred_element_type=jnp.float32)
                tile = [near_field(square[r : r + PIECE]) for r in range(0, rb, PIECE)]
                tile = jnp.concatenate(tile, axis=0)
                sums += jnp.dot(tile, omega[c : c + HALF], preferred_element_type=jnp.float32)
                near.append(tile)
            total[...] = sums
            for k in range(GROUP):
                tile = near[k * WIDTH // HALF]
                at = k * WIDTH % HALF
                tiles_ref[GROUP * j + k, here, :] = tile[:, at : at + WIDTH]
            return carry

        lax.fori_loop(0, groups, body, 0)
        part_ref[here, :] = total[...]
        return carry

    lax.fori_loop(0, part_ref.shape[0] // rb, block, 0)


def sketch_pass(order, src_pick, omega_pick, row_mat, first, rows, panels):
    rank = omega_pick.shape[1]
    rb = min(1024, rows)
    vmem = pl.BlockSpec(memory_space=pltpu.VMEM)
    return pl.pallas_call(
        functools.partial(sketch_kernel, first=first, panels=panels, rb=rb),
        in_specs=[pl.BlockSpec(memory_space=pltpu.SMEM), vmem, vmem, vmem],
        out_specs=[vmem, vmem],
        out_shape=[
            jax.ShapeDtypeStruct((rows, rank), jnp.float32),
            pltpu.VMEM((GROUP * ((panels + GROUP - 1) // GROUP), rows, WIDTH), jnp.bfloat16),
        ],
        scratch_shapes=[
            pltpu.VMEM((rb, rank), jnp.float32),
        ],
        compiler_params=pltpu.CompilerParams(vmem_limit_bytes=10 * 2**20),
        cost_estimate=pl.CostEstimate(
            flops=rows * panels * WIDTH * rank * 16, bytes_accessed=rows * panels * WIDTH * 2, transcendentals=0
        ),
        name="sketch_pass",
    )(order, src_pick, omega_pick, row_mat)


def in_vmem(kernel, out_shape, name):
    def call(*args):
        vmem = pl.BlockSpec(memory_space=pltpu.VMEM)
        return pl.pallas_call(
            kernel,
            in_specs=[vmem] * len(args),
            out_specs=jax.tree.map(lambda _: vmem, out_shape),
            out_shape=out_shape,
            compiler_params=pltpu.CompilerParams(vmem_limit_bytes=8 * 2**20),
            name=name,
        )(*args)

    return call


def pair_sum_kernel(own_ref, got_ref, kept_ref, *sent_refs):
    q = kept_ref.shape[0]
    for k in range(1 + len(sent_refs)):
        part = slice(k * q, (k + 1) * q)
        value = own_ref[part, :] + got_ref[part, :]
        if k == 0:
            kept_ref[...] = value
        else:
            sent_refs[k - 1][...] = value.astype(jnp.bfloat16)


def pair_sum(own, got, slots):
    q, rank = own.shape[0] // slots, own.shape[1]
    shapes = [jax.ShapeDtypeStruct((q, rank), jnp.float32)]
    shapes += [jax.ShapeDtypeStruct((q, rank), jnp.bfloat16)] * (slots - 1)
    return in_vmem(pair_sum_kernel, shapes, "pair_sum")(own, got)


def row_sum_kernel(kept_ref, *refs):
    total = kept_ref[...]
    for ref in refs[:-1]:
        total = total + ref[...].astype(jnp.float32)
    low = head(total)
    refs[-1][...] = (low if refs[-1].shape == low.shape else low.T).astype(jnp.bfloat16)


def row_sum(kept, got, flip):
    shape = kept.shape[::-1] if flip else kept.shape
    return in_vmem(row_sum_kernel, jax.ShapeDtypeStruct(shape, jnp.bfloat16), "row_sum")(kept, *got)


def invert_factor(gram, beside):
    n = gram.shape[0]
    pieces = n // SUB
    lane = lax.broadcasted_iota(jnp.int32, (SUB, n), 1)
    sub = lax.broadcasted_iota(jnp.int32, (SUB, n), 0)
    trace = jnp.zeros((SUB, n), jnp.float32)
    for v in range(pieces):
        trace = trace + jnp.where(lane == sub + v * SUB, gram[v * SUB : (v + 1) * SUB, :], 0.0)
    shift = (SHIFT / n) * jnp.sum(trace)
    a = [
        gram[v * SUB : (v + 1) * SUB, :] + jnp.where(lane == sub + v * SUB, shift, 0.0)
        for v in range(pieces)
    ]
    for b in range(pieces):
        beside(b)
        cols = [
            {v: jnp.broadcast_to(a[v][:, b * SUB + c : b * SUB + c + 1], (SUB, n)) for v in range(b, pieces)}
            for c in range(SUB)
        ]
        for c in range(SUB):
            j = b * SUB + c
            pivot = jnp.broadcast_to(cols[c][b][c : c + 1, :], (SUB, n))
            inv = 1.0 / pivot
            row = jnp.broadcast_to(a[b][c : c + 1, :], (SUB, n))
            row = jnp.where(lane == j, 1.0, row)
            nexts = {
                c2: jnp.broadcast_to(cols[c2][b][c : c + 1, :], (SUB, n)) for c2 in range(c + 1, SUB)
            }
            for v in range(b, pieces):
                m = cols[c][v] * inv
                here = lane == j
                if v == b:
                    m = jnp.where(sub > c, m, 0.0)
                    here = here & (sub > c)
                a[v] = jnp.where(here, 0.0, a[v]) - m * row
                for c2 in range(c + 1, SUB):
                    cols[c2][v] = cols[c2][v] - m * nexts[c2]
    out = []
    for v in range(pieces):
        diag = lane == sub + v * SUB
        d = jnp.sum(jnp.where(diag, a[v], 0.0), axis=1, keepdims=True)
        low = jnp.where(lane < sub + v * SUB, a[v], jnp.where(diag, 1.0, 0.0))
        out.append(low * lax.rsqrt(d))
    return jnp.concatenate(out, axis=0)


def gather_low(odd_ref, even_refs, low_all, flip):
    half, q = odd_ref.shape[0], odd_ref.shape[2 if flip else 1]
    pieces = [odd_ref.at[k] for k in range(half)] + list(even_refs)
    for i, ref in enumerate(pieces):
        if flip:
            low_all[:, i * q : (i + 1) * q] = ref[...]
        else:
            low_all[i * q : (i + 1) * q, :] = ref[...]
    return low_all[...] if flip else low_all[...].T


def self_product(low_t):
    return lax.dot_general(low_t, low_t, (((1,), (1,)), ((), ())), preferred_element_type=jnp.float32)


def side_by_side(tile_refs, first, count):
    return jnp.concatenate(
        [jnp.concatenate([ref[first + k] for k in range(count)], axis=1) for ref in tile_refs], axis=0
    )


def first_kernel(order_ref, odd_ref, *refs, panels, half, flip):
    even_refs, tile_refs = refs[:half], refs[half:-3]
    product_ref, gram_ref, low_all = refs[-3:]
    low_t = gather_low(odd_ref, even_refs, low_all, flip)
    gram_ref[...] = self_product(low_t)

    def group(j, carry):
        at = pl.ds(pl.multiple_of(j * HALF, HALF), HALF)
        product_ref[:, at] = jnp.dot(
            low_t, side_by_side(tile_refs, FEW * j, FEW), preferred_element_type=jnp.float32
        )
        return carry

    lax.fori_loop(0, (order_ref[panels] + FEW - 1) // FEW, group, 0)


def first_pass(order, odd, even, tiles, panels, rank, flip):
    rows = sum(t.shape[1] for t in tiles)
    held = tiles[0].shape[0]
    vmem = pl.BlockSpec(memory_space=pltpu.VMEM)
    return pl.pallas_call(
        functools.partial(first_kernel, panels=panels, half=len(even), flip=flip),
        in_specs=[pl.BlockSpec(memory_space=pltpu.SMEM)] + [vmem] * (1 + len(even) + len(tiles)),
        out_specs=[vmem, vmem],
        out_shape=[
            jax.ShapeDtypeStruct((rank, held * WIDTH), jnp.float32),
            jax.ShapeDtypeStruct((rank, rank), jnp.float32),
        ],
        scratch_shapes=[pltpu.VMEM((rank, rows) if flip else (rows, rank), jnp.bfloat16)],
        compiler_params=pltpu.CompilerParams(vmem_limit_bytes=12 * 2**20),
        cost_estimate=pl.CostEstimate(
            flops=2 * rows * panels * WIDTH * rank, bytes_accessed=0, transcendentals=0
        ),
        name="first_pass",
    )(order, odd, *even, *(pltpu.with_memory_space_constraint(x, pltpu.VMEM) for x in tiles))


def project_kernel(order_ref, first_ref, gram_ref, odd_ref, *refs, panels, half, owns, flip):
    own_refs, even_refs = refs[:owns], refs[owns : owns + half]
    tile_refs = refs[owns + half : -4]
    basis_ref, out_ref, low_all, product = refs[-4:]
    count = order_ref[panels]
    low_t = gather_low(odd_ref, even_refs, low_all, flip)
    out_ref[...] = jnp.zeros_like(out_ref)
    pairs = tile_refs[0].shape[0] // 2
    blocks = gram_ref.shape[0] // SUB

    def beside(b):
        for j in range(b * pairs // blocks, (b + 1) * pairs // blocks):
            at = slice(j * PAIR, (j + 1) * PAIR)
            product[:, at] = first_ref[:, at] + jnp.dot(
                low_t, side_by_side(tile_refs, 2 * j, 2), preferred_element_type=jnp.float32
            )

    inverse = three(invert_factor(gram_ref[...] + self_product(low_t), beside))
    rank = inverse[0].shape[0]
    stack = jnp.concatenate(inverse, axis=0).astype(jnp.bfloat16)
    q = own_refs[0].shape[1 if flip else 0]
    for i, ref in enumerate(own_refs):
        own = ref[...] if flip else ref[...].T
        parts = jnp.dot(stack, own, preferred_element_type=jnp.float32)
        basis = parts[:rank] + (parts[rank : 2 * rank] + parts[2 * rank :])
        basis_ref[i * q : (i + 1) * q, :] = basis.T

    def group(j, carry):
        parts = three(product[:, pl.ds(pl.multiple_of(j * HALF, HALF), HALF)])
        cols, rest = 0.0, 0.0
        for k, part in enumerate(parts):
            got = jnp.dot(
                stack[: (3 - k) * rank], part.astype(jnp.bfloat16), preferred_element_type=jnp.float32
            )
            for i in range(3 - k):
                if i + k == 0:
                    cols = got[:rank]
                else:
                    rest = rest + got[i * rank : (i + 1) * rank]
        cols = (cols + rest).astype(jnp.bfloat16)
        for k in range(FEW):

            @pl.when(FEW * j + k < count)
            def _():
                at = pl.multiple_of(order_ref[FEW * j + k] * WIDTH, WIDTH)
                out_ref[0, :, pl.ds(at, WIDTH)] = cols[:, k * WIDTH : (k + 1) * WIDTH]

        return carry

    lax.fori_loop(0, (count + FEW - 1) // FEW, group, 0)


def project_pass(order, first, gram, odd, owns, even, tiles, panels, rank, flip):
    rows = sum(t.shape[1] for t in tiles)
    held = tiles[0].shape[0]
    q = owns[0].shape[1 if flip else 0]
    vmem = pl.BlockSpec(memory_space=pltpu.VMEM)
    return pl.pallas_call(
        functools.partial(
            project_kernel, panels=panels, half=len(even), owns=len(owns), flip=flip
        ),
        in_specs=[pl.BlockSpec(memory_space=pltpu.SMEM)]
        + [vmem] * (3 + len(owns) + len(even) + len(tiles)),
        out_specs=[vmem, vmem],
        out_shape=[
            jax.ShapeDtypeStruct((q * len(owns), rank), jnp.float32),
            jax.ShapeDtypeStruct((1, rank, panels * WIDTH), jnp.bfloat16),
        ],
        scratch_shapes=[
            pltpu.VMEM((rank, rows) if flip else (rows, rank), jnp.bfloat16),
            pltpu.VMEM((rank, held * WIDTH), jnp.float32),
        ],
        compiler_params=pltpu.CompilerParams(vmem_limit_bytes=14 * 2**20),
        name="project_pass",
    )(
        order, first, gram, odd, *owns, *even,
        *(pltpu.with_memory_space_constraint(x, pltpu.VMEM) for x in tiles),
    )


def join_kernel(*refs):
    for k, ref in enumerate(refs[:-1]):
        refs[-1][k] = ref[...]


def join(parts):
    shape = jax.ShapeDtypeStruct((len(parts), *parts[0].shape), parts[0].dtype)
    return in_vmem(join_kernel, shape, "join")(*parts)


def after(x, *deps):
    return lax.optimization_barrier((x, *deps))[0]


def swap(x, k, n):
    return lax.ppermute(x, "tile", [(i, i ^ k) for i in range(n)])


CHUNKS = 2


def local(row_points, source_points, sketch, admissible):
    n = lax.axis_size("tile")
    panels = admissible.shape[1]
    rows = row_points.shape[1] // lax.axis_size("row")
    own_rows = rows // n
    q = own_rows // CHUNKS
    odd, even = list(range(1, n, 2)), list(range(0, n, 2))
    slices = [(k, c * q, q) for c in range(CHUNKS) for k in odd + even]
    place = flip = q % WIDTH == 0
    points = row_points
    if not place:
        me = lax.axis_index("tile")
        points = lax.dynamic_slice_in_dim(row_points, lax.axis_index("row") * rows, rows, 1)
        points = jnp.concatenate(
            [lax.dynamic_slice_in_dim(points, (me ^ k) * own_rows + first, q, 1) for k, first, _ in slices], 1
        )
    order, src_pick, omega_pick, row_mat = prep(
        admissible, points, source_points, sketch, rows, slices, place
    )

    call_rows = rows // CHUNKS // 2

    def sketch_part(at, *deps):
        return sketch_pass(
            after(order, *deps), src_pick, omega_pick, row_mat, at * call_rows, call_rows, panels
        )

    def sum_cores(got, own):
        kept, *sent = pair_sum(own, got, n // 2)
        return kept, [swap(x, k, n) for x, k in zip(sent, even[1:])]

    def along_z(kept, got):
        low = row_sum(kept, got, flip)
        return [low] + [swap(low, k, n) for k in even[1:]]

    held, tiles, sums, last = [], [], None, ()
    for c in range(CHUNKS):
        theirs, kept = sketch_part(2 * c, *last)
        tiles.append(kept)
        got = swap(theirs, 1, n)
        if c > 0:
            held.append(along_z(after(sums[0], theirs), sums[1]))
        own, kept = sketch_part(2 * c + 1, theirs, *[h[0] for h in held[-1:]])
        tiles.append(kept)
        sums = sum_cores(got, after(own, *(x for h in held[-1:] for x in h)))
        last = (own, sums[0])
    rank = sketch.shape[1]

    def across(pieces, *deps):
        return swap(join([after(pieces[0], *deps), *pieces[1:]]), 1, n)

    odd = across(held[0], own)
    first, gram = first_pass(order, odd, held[0], tiles[:2], panels, rank, flip)
    held.append(along_z(after(sums[0], gram), sums[1]))
    owns = [h[0] for h in held]
    return project_pass(
        order, first, gram, across(held[1]), owns, held[1], tiles[2:], panels, rank, flip
    )


def solution(mesh):
    in_specs = (P(), P(None, "tile"), P("tile", None), P("row", "tile"))
    out_specs = (P(("row", "tile"), None), P("row", None, "tile"))
    return jax.shard_map(local, mesh=mesh, in_specs=in_specs, out_specs=out_specs, check_vma=False)
```

```python
import functools
import math

import jax
import jax.numpy as jnp
from jax import lax
from jax.experimental import pallas as pl
from jax.experimental.pallas import tpu as pltpu
from jax.sharding import PartitionSpec as P

DAMPING = 0.25
WAVENUM = 24.0
SHIFT = 0.0001

TURNS = WAVENUM / (2.0 * math.pi)
DECAY = -DAMPING / TURNS / math.log(2.0)
AMP = TURNS / (4.0 * math.pi)
S0, S1, S2 = 6.28127979 * AMP, -41.0952178 * AMP, 73.5851113 * AMP

WIDTH = 128
PAIR = 2 * WIDTH
TERMS = 32
SUB = 8
PIECE = 16
GROUP = 16
FEW = 4
HALF = FEW * WIDTH


def head(x):
    return x.astype(jnp.bfloat16).astype(jnp.float32)


def three(x):
    a = head(x)
    b = head(x - a)
    return a, b, x - a - b


def fill_terms(ref, points, side):
    at = lax.broadcasted_iota(jnp.int32, points.shape, 0)
    x = points - jnp.where(at == 2, -0.5, 3.0)
    scale = TURNS * TURNS
    norm = three(scale * jnp.sum(x * x, axis=0, keepdims=True))
    one = jnp.ones_like(norm[0])
    if side == 0:
        h, m, l = three(x)
        rows = [h, h, m, h, l, m]
        tail = [*norm, one, one, one]
    else:
        h, m, l = three(x * (-2.0 * scale))
        rows = [h, m, h, l, h, m]
        tail = [one, one, one, *norm]
    ref[...] = jnp.zeros_like(ref)
    for at, row in enumerate(rows):
        ref[3 * at : 3 * at + 3, :] = row
    for at, row in enumerate(tail):
        ref[18 + at : 19 + at, :] = row


def near_field(square):
    inv = lax.rsqrt(square)
    t = square * inv
    f = t - jnp.round(t)
    g = 0.25 - jnp.abs(f)
    v = g * g
    wave = ((S2 * v + S1) * v + S0) * g
    amp = jnp.exp2(DECAY * t) * inv
    return (wave * amp).astype(jnp.bfloat16)


def order_panels(flags_ref, order_ref, panels):
    def step(p, count):
        @pl.when(flags_ref[0, p] > 0)
        def _():
            order_ref[count] = p

        return count + (flags_ref[0, p] > 0).astype(jnp.int32)

    count = lax.fori_loop(0, panels, step, jnp.int32(0))
    order_ref[panels] = count
    return count


def prep_kernel(
    flags_hbm, rows_hbm, src_hbm, omega_hbm, order_ref, src_pick, omega_pick, row_mat,
    flags, points, picked, row_terms, src_terms, sources, sems, sem, *, slices, place
):
    panels = flags.shape[1]
    rows = points.shape[1]
    me = lax.axis_index("tile")
    at = pl.multiple_of(lax.axis_index("row") * rows, rows) if place else 0
    copies = [
        pltpu.make_async_copy(flags_hbm, flags, sems.at[0]),
        pltpu.make_async_copy(rows_hbm.at[:, pl.ds(at, rows)], points, sems.at[1]),
        pltpu.make_async_copy(src_hbm, sources, sems.at[2]),
    ]
    for copy in copies:
        copy.start()
    copies[0].wait()
    count = order_panels(flags, order_ref, panels)

    def fetch(slot):
        at = pl.multiple_of(order_ref[slot] * WIDTH, WIDTH)
        to = pl.multiple_of(slot * WIDTH, WIDTH)
        return pltpu.make_async_copy(
            omega_hbm.at[pl.ds(at, WIDTH), :], omega_pick.at[pl.ds(to, WIDTH), :], sem
        )

    def start(slot, carry):
        fetch(slot).start()
        return carry

    lax.fori_loop(0, count, start, 0)
    copies[1].wait()
    if place:
        to = 0
        for k, first, size in slices:
            at = pl.multiple_of((me ^ k) * (rows // lax.axis_size("tile")) + first, WIDTH)
            picked[:, to : to + size] = points[:, pl.ds(at, size)]
            to += size
        fill_terms(row_terms, picked[...], 0)
    else:
        fill_terms(row_terms, points[...], 0)
    step = min(512, rows)
    for r in range(0, rows, step):
        row_mat[r : r + step, :] = row_terms[:, r : r + step].T.astype(jnp.bfloat16)
    copies[2].wait()
    fill_terms(src_terms, sources[...], 1)

    def pick(slot, carry):
        at = pl.multiple_of(order_ref[slot] * WIDTH, WIDTH)
        to = pl.multiple_of(slot * WIDTH, WIDTH)
        src_pick[:, pl.ds(to, WIDTH)] = src_terms[:, pl.ds(at, WIDTH)].astype(jnp.bfloat16)
        return carry

    lax.fori_loop(0, count, pick, 0)
    spare = src_terms[:, :WIDTH].astype(jnp.bfloat16)

    def pad(slot, carry):
        to = pl.multiple_of(slot * WIDTH, WIDTH)
        src_pick[:, pl.ds(to, WIDTH)] = spare
        omega_pick[pl.ds(to, WIDTH), :] = jnp.zeros((WIDTH, omega_pick.shape[1]), jnp.bfloat16)
        return carry

    lax.fori_loop(count, GROUP * ((count + GROUP - 1) // GROUP), pad, 0)

    def finish(slot, carry):
        fetch(slot).wait()
        return carry

    lax.fori_loop(0, count, finish, 0)


def in_hbm(x):
    return pltpu.with_memory_space_constraint(x, pltpu.HBM)


def prep(admissible, points, source_points, sketch, rows, slices, place):
    panels = admissible.shape[1]
    cols, rank = sketch.shape
    spare = GROUP * ((panels + GROUP - 1) // GROUP) * WIDTH
    hbm = pl.BlockSpec(memory_space=pltpu.HBM)
    vmem = pl.BlockSpec(memory_space=pltpu.VMEM)
    return pl.pallas_call(
        functools.partial(prep_kernel, slices=slices, place=place),
        in_specs=[hbm] * 4,
        out_specs=[pl.BlockSpec(memory_space=pltpu.SMEM), vmem, vmem, vmem],
        out_shape=[
            jax.ShapeDtypeStruct((panels + 8,), jnp.int32),
            jax.ShapeDtypeStruct((TERMS, spare), jnp.bfloat16),
            jax.ShapeDtypeStruct((spare, rank), jnp.bfloat16),
            jax.ShapeDtypeStruct((rows, TERMS), jnp.bfloat16),
        ],
        scratch_shapes=[
            pltpu.SMEM((1, panels), jnp.int32),
            pltpu.VMEM((3, rows), jnp.float32),
            pltpu.VMEM((3, rows), jnp.float32),
            pltpu.VMEM((TERMS, rows), jnp.float32),
            pltpu.VMEM((TERMS, cols), jnp.float32),
            pltpu.VMEM((3, cols), jnp.float32),
            pltpu.SemaphoreType.DMA((3,)),
            pltpu.SemaphoreType.DMA,
        ],
        compiler_params=pltpu.CompilerParams(vmem_limit_bytes=16 * 2**20),
        name="prep",
    )(*(in_hbm(x) for x in (admissible, points, source_points, sketch)))


def sketch_kernel(
    order_ref, src_pick, omega_pick, row_mat, part_ref, tiles_ref, total, *, first, panels, rb
):
    groups = (order_ref[panels] + GROUP - 1) // GROUP
    cols = GROUP * WIDTH

    def block(b, carry):
        here = pl.ds(pl.multiple_of(b * rb, rb), rb)
        total[...] = jnp.zeros_like(total)

        def body(j, carry):
            at = pl.ds(pl.multiple_of(j * cols, cols), cols)
            rows = row_mat[pl.ds(pl.multiple_of(first + b * rb, rb), rb), :]
            src = src_pick[:, at]
            omega = omega_pick[at, :]
            sums = total[...]
            near = []
            for c in range(0, cols, HALF):
                square = jnp.dot(rows, src[:, c : c + HALF], preferred_element_type=jnp.float32)
                tile = [near_field(square[r : r + PIECE]) for r in range(0, rb, PIECE)]
                tile = jnp.concatenate(tile, axis=0)
                sums += jnp.dot(tile, omega[c : c + HALF], preferred_element_type=jnp.float32)
                near.append(tile)
            total[...] = sums
            for k in range(GROUP):
                tile = near[k * WIDTH // HALF]
                at = k * WIDTH % HALF
                tiles_ref[GROUP * j + k, here, :] = tile[:, at : at + WIDTH]
            return carry

        lax.fori_loop(0, groups, body, 0)
        part_ref[here, :] = total[...]
        return carry

    lax.fori_loop(0, part_ref.shape[0] // rb, block, 0)


def sketch_pass(order, src_pick, omega_pick, row_mat, first, rows, panels):
    rank = omega_pick.shape[1]
    rb = min(512, rows)
    vmem = pl.BlockSpec(memory_space=pltpu.VMEM)
    return pl.pallas_call(
        functools.partial(sketch_kernel, first=first, panels=panels, rb=rb),
        in_specs=[pl.BlockSpec(memory_space=pltpu.SMEM), vmem, vmem, vmem],
        out_specs=[vmem, vmem],
        out_shape=[
            jax.ShapeDtypeStruct((rows, rank), jnp.float32),
            pltpu.VMEM((GROUP * ((panels + GROUP - 1) // GROUP), rows, WIDTH), jnp.bfloat16),
        ],
        scratch_shapes=[
            pltpu.VMEM((rb, rank), jnp.float32),
        ],
        compiler_params=pltpu.CompilerParams(vmem_limit_bytes=10 * 2**20),
        cost_estimate=pl.CostEstimate(
            flops=rows * panels * WIDTH * rank * 16, bytes_accessed=rows * panels * WIDTH * 2, transcendentals=0
        ),
        name="sketch_pass",
    )(order, src_pick, omega_pick, row_mat)


def in_vmem(kernel, out_shape, name):
    def call(*args):
        vmem = pl.BlockSpec(memory_space=pltpu.VMEM)
        return pl.pallas_call(
            kernel,
            in_specs=[vmem] * len(args),
            out_specs=jax.tree.map(lambda _: vmem, out_shape),
            out_shape=out_shape,
            compiler_params=pltpu.CompilerParams(vmem_limit_bytes=8 * 2**20),
            name=name,
        )(*args)

    return call


def pair_sum_kernel(*refs, parts):
    own_refs, got_refs, out_refs = refs[:parts], refs[parts : 2 * parts], refs[2 * parts :]
    q = out_refs[0].shape[0]
    each = len(out_refs) // parts
    for k, out_ref in enumerate(out_refs):
        rows = slice(k % each * q, (k % each + 1) * q)
        value = own_refs[k // each][rows, :] + got_refs[k // each][rows, :]
        out_ref[...] = value.astype(out_ref.dtype)


def pair_sum(owns, gots, slots):
    q, rank = sum(x.shape[0] for x in owns) // slots, owns[0].shape[1]
    shapes = [jax.ShapeDtypeStruct((q, rank), jnp.float32)]
    shapes += [jax.ShapeDtypeStruct((q, rank), jnp.bfloat16)] * (slots - 1)
    kernel = functools.partial(pair_sum_kernel, parts=len(owns))
    return in_vmem(kernel, shapes, "pair_sum")(*owns, *gots)


def row_sum_kernel(kept_ref, *refs):
    total = kept_ref[...]
    for ref in refs[:-1]:
        total = total + ref[...].astype(jnp.float32)
    low = head(total)
    refs[-1][...] = (low if refs[-1].shape == low.shape else low.T).astype(jnp.bfloat16)


def row_sum(kept, got, flip):
    shape = kept.shape[::-1] if flip else kept.shape
    return in_vmem(row_sum_kernel, jax.ShapeDtypeStruct(shape, jnp.bfloat16), "row_sum")(kept, *got)


def invert_factor(gram, beside):
    n = gram.shape[0]
    pieces = n // SUB
    lane = lax.broadcasted_iota(jnp.int32, (SUB, n), 1)
    sub = lax.broadcasted_iota(jnp.int32, (SUB, n), 0)
    trace = jnp.zeros((SUB, n), jnp.float32)
    for v in range(pieces):
        trace = trace + jnp.where(lane == sub + v * SUB, gram[v * SUB : (v + 1) * SUB, :], 0.0)
    shift = (SHIFT / n) * jnp.sum(trace)
    a = [
        gram[v * SUB : (v + 1) * SUB, :] + jnp.where(lane == sub + v * SUB, shift, 0.0)
        for v in range(pieces)
    ]
    for b in range(pieces):
        beside(b)
        cols = [
            {v: jnp.broadcast_to(a[v][:, b * SUB + c : b * SUB + c + 1], (SUB, n)) for v in range(b, pieces)}
            for c in range(SUB)
        ]
        for c in range(SUB):
            j = b * SUB + c
            pivot = jnp.broadcast_to(cols[c][b][c : c + 1, :], (SUB, n))
            inv = 1.0 / pivot
            row = jnp.broadcast_to(a[b][c : c + 1, :], (SUB, n))
            row = jnp.where(lane == j, 1.0, row)
            nexts = {
                c2: jnp.broadcast_to(cols[c2][b][c : c + 1, :], (SUB, n)) for c2 in range(c + 1, SUB)
            }
            for v in range(b, pieces):
                m = cols[c][v] * inv
                here = lane == j
                if v == b:
                    m = jnp.where(sub > c, m, 0.0)
                    here = here & (sub > c)
                a[v] = jnp.where(here, 0.0, a[v]) - m * row
                for c2 in range(c + 1, SUB):
                    cols[c2][v] = cols[c2][v] - m * nexts[c2]
    out = []
    for v in range(pieces):
        diag = lane == sub + v * SUB
        d = jnp.sum(jnp.where(diag, a[v], 0.0), axis=1, keepdims=True)
        low = jnp.where(lane < sub + v * SUB, a[v], jnp.where(diag, 1.0, 0.0))
        out.append(low * lax.rsqrt(d))
    return jnp.concatenate(out, axis=0)


def gather_low(odd_ref, even_refs, low_all, flip):
    half, q = odd_ref.shape[0], odd_ref.shape[2 if flip else 1]
    pieces = [odd_ref.at[k] for k in range(half)] + list(even_refs)
    for i, ref in enumerate(pieces):
        if flip:
            low_all[:, i * q : (i + 1) * q] = ref[...]
        else:
            low_all[i * q : (i + 1) * q, :] = ref[...]
    return low_all[...] if flip else low_all[...].T


def self_product(low_t):
    return lax.dot_general(low_t, low_t, (((1,), (1,)), ((), ())), preferred_element_type=jnp.float32)


def side_by_side(tile_refs, first, count):
    return jnp.concatenate(
        [jnp.concatenate([ref[first + k] for k in range(count)], axis=1) for ref in tile_refs], axis=0
    )


def first_kernel(order_ref, odd_ref, *refs, panels, half, flip):
    even_refs, tile_refs = refs[:half], refs[half:-3]
    product_ref, gram_ref, low_all = refs[-3:]
    low_t = gather_low(odd_ref, even_refs, low_all, flip)
    gram_ref[...] = self_product(low_t)

    def group(j, carry):
        at = pl.ds(pl.multiple_of(j * HALF, HALF), HALF)
        product_ref[:, at] = jnp.dot(
            low_t, side_by_side(tile_refs, FEW * j, FEW), preferred_element_type=jnp.float32
        )
        return carry

    lax.fori_loop(0, (order_ref[panels] + FEW - 1) // FEW, group, 0)


def first_pass(order, odd, even, tiles, panels, rank, flip):
    rows = sum(t.shape[1] for t in tiles)
    held = tiles[0].shape[0]
    vmem = pl.BlockSpec(memory_space=pltpu.VMEM)
    return pl.pallas_call(
        functools.partial(first_kernel, panels=panels, half=len(even), flip=flip),
        in_specs=[pl.BlockSpec(memory_space=pltpu.SMEM)] + [vmem] * (1 + len(even) + len(tiles)),
        out_specs=[vmem, vmem],
        out_shape=[
            jax.ShapeDtypeStruct((rank, held * WIDTH), jnp.float32),
            jax.ShapeDtypeStruct((rank, rank), jnp.float32),
        ],
        scratch_shapes=[pltpu.VMEM((rank, rows) if flip else (rows, rank), jnp.bfloat16)],
        compiler_params=pltpu.CompilerParams(vmem_limit_bytes=12 * 2**20),
        cost_estimate=pl.CostEstimate(
            flops=2 * rows * panels * WIDTH * rank, bytes_accessed=0, transcendentals=0
        ),
        name="first_pass",
    )(order, odd, *even, *(pltpu.with_memory_space_constraint(x, pltpu.VMEM) for x in tiles))


def project_kernel(order_ref, first_ref, gram_ref, odd_ref, *refs, panels, half, owns, flip):
    own_refs, even_refs = refs[:owns], refs[owns : owns + half]
    tile_refs = refs[owns + half : -4]
    basis_ref, out_ref, low_all, product = refs[-4:]
    count = order_ref[panels]
    low_t = gather_low(odd_ref, even_refs, low_all, flip)
    out_ref[...] = jnp.zeros_like(out_ref)
    pairs = tile_refs[0].shape[0] // 2
    blocks = gram_ref.shape[0] // SUB

    def beside(b):
        for j in range(b * pairs // blocks, (b + 1) * pairs // blocks):
            at = slice(j * PAIR, (j + 1) * PAIR)
            product[:, at] = first_ref[:, at] + jnp.dot(
                low_t, side_by_side(tile_refs, 2 * j, 2), preferred_element_type=jnp.float32
            )

    inverse = three(invert_factor(gram_ref[...] + self_product(low_t), beside))
    rank = inverse[0].shape[0]
    stack = jnp.concatenate(inverse, axis=0).astype(jnp.bfloat16)
    q = own_refs[0].shape[1 if flip else 0]
    for i, ref in enumerate(own_refs):
        own = ref[...] if flip else ref[...].T
        parts = jnp.dot(stack, own, preferred_element_type=jnp.float32)
        basis = parts[:rank] + (parts[rank : 2 * rank] + parts[2 * rank :])
        basis_ref[i * q : (i + 1) * q, :] = basis.T

    def group(j, carry):
        parts = three(product[:, pl.ds(pl.multiple_of(j * HALF, HALF), HALF)])
        cols, rest = 0.0, 0.0
        for k, part in enumerate(parts):
            got = jnp.dot(
                stack[: (3 - k) * rank], part.astype(jnp.bfloat16), preferred_element_type=jnp.float32
            )
            for i in range(3 - k):
                if i + k == 0:
                    cols = got[:rank]
                else:
                    rest = rest + got[i * rank : (i + 1) * rank]
        cols = (cols + rest).astype(jnp.bfloat16)
        for k in range(FEW):

            @pl.when(FEW * j + k < count)
            def _():
                at = pl.multiple_of(order_ref[FEW * j + k] * WIDTH, WIDTH)
                out_ref[0, :, pl.ds(at, WIDTH)] = cols[:, k * WIDTH : (k + 1) * WIDTH]

        return carry

    lax.fori_loop(0, (count + FEW - 1) // FEW, group, 0)


def project_pass(order, first, gram, odd, owns, even, tiles, panels, rank, flip):
    rows = sum(t.shape[1] for t in tiles)
    held = tiles[0].shape[0]
    q = owns[0].shape[1 if flip else 0]
    vmem = pl.BlockSpec(memory_space=pltpu.VMEM)
    return pl.pallas_call(
        functools.partial(
            project_kernel, panels=panels, half=len(even), owns=len(owns), flip=flip
        ),
        in_specs=[pl.BlockSpec(memory_space=pltpu.SMEM)]
        + [vmem] * (3 + len(owns) + len(even) + len(tiles)),
        out_specs=[vmem, vmem],
        out_shape=[
            jax.ShapeDtypeStruct((q * len(owns), rank), jnp.float32),
            jax.ShapeDtypeStruct((1, rank, panels * WIDTH), jnp.bfloat16),
        ],
        scratch_shapes=[
            pltpu.VMEM((rank, rows) if flip else (rows, rank), jnp.bfloat16),
            pltpu.VMEM((rank, held * WIDTH), jnp.float32),
        ],
        compiler_params=pltpu.CompilerParams(vmem_limit_bytes=14 * 2**20),
        name="project_pass",
    )(
        order, first, gram, odd, *owns, *even,
        *(pltpu.with_memory_space_constraint(x, pltpu.VMEM) for x in tiles),
    )


def join_kernel(*refs):
    for k, ref in enumerate(refs[:-1]):
        refs[-1][k] = ref[...]


def join(parts):
    shape = jax.ShapeDtypeStruct((len(parts), *parts[0].shape), parts[0].dtype)
    return in_vmem(join_kernel, shape, "join")(*parts)


def after(x, *deps):
    return lax.optimization_barrier((x, *deps))[0]


def swap(x, k, n):
    return lax.ppermute(x, "tile", [(i, i ^ k) for i in range(n)])


CHUNKS = 2


def local(row_points, source_points, sketch, admissible):
    n = lax.axis_size("tile")
    panels = admissible.shape[1]
    rows = row_points.shape[1] // lax.axis_size("row")
    own_rows = rows // n
    q = own_rows // CHUNKS
    odd, even = list(range(1, n, 2)), list(range(0, n, 2))
    slices = [(k, c * q, q) for c in range(CHUNKS) for k in odd + even]
    place = flip = q % WIDTH == 0
    points = row_points
    if not place:
        me = lax.axis_index("tile")
        points = lax.dynamic_slice_in_dim(row_points, lax.axis_index("row") * rows, rows, 1)
        points = jnp.concatenate(
            [lax.dynamic_slice_in_dim(points, (me ^ k) * own_rows + first, q, 1) for k, first, _ in slices], 1
        )
    order, src_pick, omega_pick, row_mat = prep(
        admissible, points, source_points, sketch, rows, slices, place
    )

    half_rows = rows // CHUNKS // 2

    def sketch_part(first, size, *deps):
        return sketch_pass(after(order, *deps), src_pick, omega_pick, row_mat, first, size, panels)

    def z_swaps(parts, *deps):
        got = []
        for x, k in zip(parts, even[1:]):
            if deps and k == even[-1]:
                x = after(x, *deps, *got)
            got.append(swap(x, k, n))
        return got

    def along_z(low, *deps):
        return [low, *z_swaps([low] * (n // 2 - 1), *deps)]

    theirs, kept0 = sketch_part(0, half_rows)
    got = swap(theirs, 1, n)
    own, kept1 = sketch_part(half_rows, half_rows, theirs)
    kept, *sent = pair_sum([own], [got], n // 2)

    part = half_rows // 2
    start = 2 * half_rows
    theirs_a, kept2 = sketch_part(start, part, own, kept)
    got_z = z_swaps(sent, theirs_a)
    got_a = swap(theirs_a, 1, n)
    theirs_b, kept3 = sketch_part(start + part, part, theirs_a)
    got_b = swap(theirs_b, 1, n)
    low = row_sum(after(kept, theirs_b), got_z, flip)
    own_a, kept4 = sketch_part(start + 2 * part, part, theirs_b, low)
    held = [along_z(low, own_a)]
    own_b, kept5 = sketch_part(start + 3 * part, part, own_a)
    kept, *sent = pair_sum([own_a, after(own_b, *held[0])], [got_a, got_b], n // 2)
    tiles = [kept0, kept1, kept2, kept3, kept4, kept5]
    rank = sketch.shape[1]

    def across(pieces, *deps):
        return swap(join([after(pieces[0], *deps), *pieces[1:]]), 1, n)

    odd = across(held[0], own_b)
    first, gram = first_pass(order, odd, held[0], tiles[:2], panels, rank, flip)
    got_z = z_swaps(sent, gram)
    held.append(along_z(row_sum(kept, got_z, flip)))
    owns = [h[0] for h in held]
    return project_pass(
        order, first, gram, across(held[1]), owns, held[1], tiles[2:], panels, rank, flip
    )


def solution(mesh):
    in_specs = (P(), P(None, "tile"), P("tile", None), P("row", "tile"))
    out_specs = (P(("row", "tile"), None), P("row", None, "tile"))
    return jax.shard_map(local, mesh=mesh, in_specs=in_specs, out_specs=out_specs, check_vma=False)
```

```python
import functools
import math

import jax
import jax.numpy as jnp
from jax import lax
from jax.experimental import pallas as pl
from jax.experimental.pallas import tpu as pltpu
from jax.sharding import PartitionSpec as P

DAMPING = 0.25
WAVENUM = 24.0
SHIFT = 0.0001

TURNS = WAVENUM / (2.0 * math.pi)
DECAY = -DAMPING / TURNS / math.log(2.0)
AMP = TURNS / (4.0 * math.pi)
S0, S1, S2 = 6.28127979 * AMP, -41.0952178 * AMP, 73.5851113 * AMP

WIDTH = 128
PAIR = 2 * WIDTH
TERMS = 32
SUB = 8
PIECE = 16
GROUP = 16
FEW = 4
HALF = FEW * WIDTH


def head(x):
    return x.astype(jnp.bfloat16).astype(jnp.float32)


def three(x):
    a = head(x)
    b = head(x - a)
    return a, b, x - a - b


def fill_terms(ref, points, side):
    at = lax.broadcasted_iota(jnp.int32, points.shape, 0)
    x = points - jnp.where(at == 2, -0.5, 3.0)
    scale = TURNS * TURNS
    norm = three(scale * jnp.sum(x * x, axis=0, keepdims=True))
    one = jnp.ones_like(norm[0])
    if side == 0:
        h, m, l = three(x)
        rows = [h, h, m, h, l, m]
        tail = [*norm, one, one, one]
    else:
        h, m, l = three(x * (-2.0 * scale))
        rows = [h, m, h, l, h, m]
        tail = [one, one, one, *norm]
    ref[...] = jnp.zeros_like(ref)
    for at, row in enumerate(rows):
        ref[3 * at : 3 * at + 3, :] = row
    for at, row in enumerate(tail):
        ref[18 + at : 19 + at, :] = row


def near_field(square):
    inv = lax.rsqrt(square)
    t = square * inv
    f = t - jnp.round(t)
    g = 0.25 - jnp.abs(f)
    v = g * g
    wave = ((S2 * v + S1) * v + S0) * g
    amp = jnp.exp2(DECAY * t) * inv
    return (wave * amp).astype(jnp.bfloat16)


def order_panels(flags_ref, order_ref, panels):
    def step(p, count):
        @pl.when(flags_ref[0, p] > 0)
        def _():
            order_ref[count] = p

        return count + (flags_ref[0, p] > 0).astype(jnp.int32)

    count = lax.fori_loop(0, panels, step, jnp.int32(0))
    order_ref[panels] = count
    return count


def prep_kernel(
    flags_hbm, rows_hbm, src_hbm, omega_hbm, order_ref, src_pick, omega_pick, row_mat,
    flags, points, picked, row_terms, src_terms, sources, sems, sem, *, slices, place
):
    panels = flags.shape[1]
    rows = points.shape[1]
    me = lax.axis_index("tile")
    at = pl.multiple_of(lax.axis_index("row") * rows, rows) if place else 0
    copies = [
        pltpu.make_async_copy(flags_hbm, flags, sems.at[0]),
        pltpu.make_async_copy(rows_hbm.at[:, pl.ds(at, rows)], points, sems.at[1]),
        pltpu.make_async_copy(src_hbm, sources, sems.at[2]),
    ]
    for copy in copies:
        copy.start()
    copies[0].wait()
    count = order_panels(flags, order_ref, panels)

    def fetch(slot):
        at = pl.multiple_of(order_ref[slot] * WIDTH, WIDTH)
        to = pl.multiple_of(slot * WIDTH, WIDTH)
        return pltpu.make_async_copy(
            omega_hbm.at[pl.ds(at, WIDTH), :], omega_pick.at[pl.ds(to, WIDTH), :], sem
        )

    def start(slot, carry):
        fetch(slot).start()
        return carry

    lax.fori_loop(0, count, start, 0)
    copies[1].wait()
    if place:
        to = 0
        for k, first, size in slices:
            at = pl.multiple_of((me ^ k) * (rows // lax.axis_size("tile")) + first, WIDTH)
            picked[:, to : to + size] = points[:, pl.ds(at, size)]
            to += size
        fill_terms(row_terms, picked[...], 0)
    else:
        fill_terms(row_terms, points[...], 0)
    step = min(512, rows)
    for r in range(0, rows, step):
        row_mat[r : r + step, :] = row_terms[:, r : r + step].T.astype(jnp.bfloat16)
    copies[2].wait()
    fill_terms(src_terms, sources[...], 1)

    def pick(slot, carry):
        at = pl.multiple_of(order_ref[slot] * WIDTH, WIDTH)
        to = pl.multiple_of(slot * WIDTH, WIDTH)
        src_pick[:, pl.ds(to, WIDTH)] = src_terms[:, pl.ds(at, WIDTH)].astype(jnp.bfloat16)
        return carry

    lax.fori_loop(0, count, pick, 0)
    spare = src_terms[:, :WIDTH].astype(jnp.bfloat16)

    def pad(slot, carry):
        to = pl.multiple_of(slot * WIDTH, WIDTH)
        src_pick[:, pl.ds(to, WIDTH)] = spare
        omega_pick[pl.ds(to, WIDTH), :] = jnp.zeros((WIDTH, omega_pick.shape[1]), jnp.bfloat16)
        return carry

    lax.fori_loop(count, GROUP * ((count + GROUP - 1) // GROUP), pad, 0)

    def finish(slot, carry):
        fetch(slot).wait()
        return carry

    lax.fori_loop(0, count, finish, 0)


def in_hbm(x):
    return pltpu.with_memory_space_constraint(x, pltpu.HBM)


def prep(admissible, points, source_points, sketch, rows, slices, place):
    panels = admissible.shape[1]
    cols, rank = sketch.shape
    spare = GROUP * ((panels + GROUP - 1) // GROUP) * WIDTH
    hbm = pl.BlockSpec(memory_space=pltpu.HBM)
    vmem = pl.BlockSpec(memory_space=pltpu.VMEM)
    return pl.pallas_call(
        functools.partial(prep_kernel, slices=slices, place=place),
        in_specs=[hbm] * 4,
        out_specs=[pl.BlockSpec(memory_space=pltpu.SMEM), vmem, vmem, vmem],
        out_shape=[
            jax.ShapeDtypeStruct((panels + 8,), jnp.int32),
            jax.ShapeDtypeStruct((TERMS, spare), jnp.bfloat16),
            jax.ShapeDtypeStruct((spare, rank), jnp.bfloat16),
            jax.ShapeDtypeStruct((rows, TERMS), jnp.bfloat16),
        ],
        scratch_shapes=[
            pltpu.SMEM((1, panels), jnp.int32),
            pltpu.VMEM((3, rows), jnp.float32),
            pltpu.VMEM((3, rows), jnp.float32),
            pltpu.VMEM((TERMS, rows), jnp.float32),
            pltpu.VMEM((TERMS, cols), jnp.float32),
            pltpu.VMEM((3, cols), jnp.float32),
            pltpu.SemaphoreType.DMA((3,)),
            pltpu.SemaphoreType.DMA,
        ],
        compiler_params=pltpu.CompilerParams(vmem_limit_bytes=16 * 2**20),
        name="prep",
    )(*(in_hbm(x) for x in (admissible, points, source_points, sketch)))


def sketch_kernel(
    order_ref, src_pick, omega_pick, row_mat, part_ref, tiles_ref, total, *, first, panels, rb
):
    groups = (order_ref[panels] + GROUP - 1) // GROUP
    cols = GROUP * WIDTH

    def block(b, carry):
        here = pl.ds(pl.multiple_of(b * rb, rb), rb)
        total[...] = jnp.zeros_like(total)

        def body(j, carry):
            at = pl.ds(pl.multiple_of(j * cols, cols), cols)
            rows = row_mat[pl.ds(pl.multiple_of(first + b * rb, rb), rb), :]
            src = src_pick[:, at]
            omega = omega_pick[at, :]
            sums = total[...]
            near = []
            for c in range(0, cols, HALF):
                square = jnp.dot(rows, src[:, c : c + HALF], preferred_element_type=jnp.float32)
                tile = [near_field(square[r : r + PIECE]) for r in range(0, rb, PIECE)]
                tile = jnp.concatenate(tile, axis=0)
                sums += jnp.dot(tile, omega[c : c + HALF], preferred_element_type=jnp.float32)
                near.append(tile)
            total[...] = sums
            for k in range(GROUP):
                tile = near[k * WIDTH // HALF]
                at = k * WIDTH % HALF
                tiles_ref[GROUP * j + k, here, :] = tile[:, at : at + WIDTH]
            return carry

        lax.fori_loop(0, groups, body, 0)
        part_ref[here, :] = total[...]
        return carry

    lax.fori_loop(0, part_ref.shape[0] // rb, block, 0)


def sketch_pass(order, src_pick, omega_pick, row_mat, first, rows, panels):
    rank = omega_pick.shape[1]
    rb = min(512, rows)
    vmem = pl.BlockSpec(memory_space=pltpu.VMEM)
    return pl.pallas_call(
        functools.partial(sketch_kernel, first=first, panels=panels, rb=rb),
        in_specs=[pl.BlockSpec(memory_space=pltpu.SMEM), vmem, vmem, vmem],
        out_specs=[vmem, vmem],
        out_shape=[
            jax.ShapeDtypeStruct((rows, rank), jnp.float32),
            pltpu.VMEM((GROUP * ((panels + GROUP - 1) // GROUP), rows, WIDTH), jnp.bfloat16),
        ],
        scratch_shapes=[
            pltpu.VMEM((rb, rank), jnp.float32),
        ],
        compiler_params=pltpu.CompilerParams(vmem_limit_bytes=10 * 2**20),
        cost_estimate=pl.CostEstimate(
            flops=rows * panels * WIDTH * rank * 16, bytes_accessed=rows * panels * WIDTH * 2, transcendentals=0
        ),
        name="sketch_pass",
    )(order, src_pick, omega_pick, row_mat)


def in_vmem(kernel, out_shape, name):
    def call(*args):
        vmem = pl.BlockSpec(memory_space=pltpu.VMEM)
        return pl.pallas_call(
            kernel,
            in_specs=[vmem] * len(args),
            out_specs=jax.tree.map(lambda _: vmem, out_shape),
            out_shape=out_shape,
            compiler_params=pltpu.CompilerParams(vmem_limit_bytes=8 * 2**20),
            name=name,
        )(*args)

    return call


def pair_sum_kernel(*refs, parts):
    own_refs, got_refs, out_refs = refs[:parts], refs[parts : 2 * parts], refs[2 * parts :]
    q = out_refs[0].shape[0]
    each = len(out_refs) // parts
    for k, out_ref in enumerate(out_refs):
        rows = slice(k % each * q, (k % each + 1) * q)
        value = own_refs[k // each][rows, :] + got_refs[k // each][rows, :]
        out_ref[...] = value.astype(out_ref.dtype)


def pair_sum(owns, gots, slots):
    q, rank = sum(x.shape[0] for x in owns) // slots, owns[0].shape[1]
    shapes = [jax.ShapeDtypeStruct((q, rank), jnp.float32)]
    shapes += [jax.ShapeDtypeStruct((q, rank), jnp.bfloat16)] * (slots - 1)
    kernel = functools.partial(pair_sum_kernel, parts=len(owns))
    return in_vmem(kernel, shapes, "pair_sum")(*owns, *gots)


def row_sum_kernel(kept_ref, *refs):
    total = kept_ref[...]
    for ref in refs[:-1]:
        total = total + ref[...].astype(jnp.float32)
    low = head(total)
    refs[-1][...] = (low if refs[-1].shape == low.shape else low.T).astype(jnp.bfloat16)


def row_sum(kept, got, flip):
    shape = kept.shape[::-1] if flip else kept.shape
    return in_vmem(row_sum_kernel, jax.ShapeDtypeStruct(shape, jnp.bfloat16), "row_sum")(kept, *got)


def invert_factor(gram, beside):
    n = gram.shape[0]
    pieces = n // SUB
    lane = lax.broadcasted_iota(jnp.int32, (SUB, n), 1)
    sub = lax.broadcasted_iota(jnp.int32, (SUB, n), 0)
    trace = jnp.zeros((SUB, n), jnp.float32)
    for v in range(pieces):
        trace = trace + jnp.where(lane == sub + v * SUB, gram[v * SUB : (v + 1) * SUB, :], 0.0)
    shift = (SHIFT / n) * jnp.sum(trace)
    a = [
        gram[v * SUB : (v + 1) * SUB, :] + jnp.where(lane == sub + v * SUB, shift, 0.0)
        for v in range(pieces)
    ]
    for b in range(pieces):
        beside(b)
        cols = [
            {v: jnp.broadcast_to(a[v][:, b * SUB + c : b * SUB + c + 1], (SUB, n)) for v in range(b, pieces)}
            for c in range(SUB)
        ]
        for c in range(SUB):
            j = b * SUB + c
            pivot = jnp.broadcast_to(cols[c][b][c : c + 1, :], (SUB, n))
            inv = 1.0 / pivot
            row = jnp.broadcast_to(a[b][c : c + 1, :], (SUB, n))
            row = jnp.where(lane == j, 1.0, row)
            nexts = {
                c2: jnp.broadcast_to(cols[c2][b][c : c + 1, :], (SUB, n)) for c2 in range(c + 1, SUB)
            }
            for v in range(b, pieces):
                m = cols[c][v] * inv
                here = lane == j
                if v == b:
                    m = jnp.where(sub > c, m, 0.0)
                    here = here & (sub > c)
                a[v] = jnp.where(here, 0.0, a[v]) - m * row
                for c2 in range(c + 1, SUB):
                    cols[c2][v] = cols[c2][v] - m * nexts[c2]
    out = []
    for v in range(pieces):
        diag = lane == sub + v * SUB
        d = jnp.sum(jnp.where(diag, a[v], 0.0), axis=1, keepdims=True)
        low = jnp.where(lane < sub + v * SUB, a[v], jnp.where(diag, 1.0, 0.0))
        out.append(low * lax.rsqrt(d))
    return jnp.concatenate(out, axis=0)


def gather_low(odd_ref, even_refs, low_all, flip):
    half, q = odd_ref.shape[0], odd_ref.shape[2 if flip else 1]
    pieces = [odd_ref.at[k] for k in range(half)] + list(even_refs)
    for i, ref in enumerate(pieces):
        if flip:
            low_all[:, i * q : (i + 1) * q] = ref[...]
        else:
            low_all[i * q : (i + 1) * q, :] = ref[...]
    return low_all[...] if flip else low_all[...].T


def self_product(low_t):
    return lax.dot_general(low_t, low_t, (((1,), (1,)), ((), ())), preferred_element_type=jnp.float32)


def side_by_side(tile_refs, first, count):
    return jnp.concatenate(
        [jnp.concatenate([ref[first + k] for k in range(count)], axis=1) for ref in tile_refs], axis=0
    )


def first_kernel(order_ref, odd_ref, *refs, panels, half, flip):
    even_refs, tile_refs = refs[:half], refs[half:-3]
    product_ref, gram_ref, low_all = refs[-3:]
    low_t = gather_low(odd_ref, even_refs, low_all, flip)
    gram_ref[...] = self_product(low_t)

    def group(j, carry):
        at = pl.ds(pl.multiple_of(j * HALF, HALF), HALF)
        product_ref[:, at] = jnp.dot(
            low_t, side_by_side(tile_refs, FEW * j, FEW), preferred_element_type=jnp.float32
        )
        return carry

    lax.fori_loop(0, (order_ref[panels] + FEW - 1) // FEW, group, 0)


def first_pass(order, odd, even, tiles, panels, rank, flip):
    rows = sum(t.shape[1] for t in tiles)
    held = tiles[0].shape[0]
    vmem = pl.BlockSpec(memory_space=pltpu.VMEM)
    return pl.pallas_call(
        functools.partial(first_kernel, panels=panels, half=len(even), flip=flip),
        in_specs=[pl.BlockSpec(memory_space=pltpu.SMEM)] + [vmem] * (1 + len(even) + len(tiles)),
        out_specs=[vmem, vmem],
        out_shape=[
            jax.ShapeDtypeStruct((rank, held * WIDTH), jnp.float32),
            jax.ShapeDtypeStruct((rank, rank), jnp.float32),
        ],
        scratch_shapes=[pltpu.VMEM((rank, rows) if flip else (rows, rank), jnp.bfloat16)],
        compiler_params=pltpu.CompilerParams(vmem_limit_bytes=12 * 2**20),
        cost_estimate=pl.CostEstimate(
            flops=2 * rows * panels * WIDTH * rank, bytes_accessed=0, transcendentals=0
        ),
        name="first_pass",
    )(order, odd, *even, *(pltpu.with_memory_space_constraint(x, pltpu.VMEM) for x in tiles))


def project_kernel(order_ref, first_ref, gram_ref, odd_ref, *refs, panels, half, owns, flip):
    own_refs, even_refs = refs[:owns], refs[owns : owns + half]
    tile_refs = refs[owns + half : -4]
    basis_ref, out_ref, low_all, product = refs[-4:]
    count = order_ref[panels]
    low_t = gather_low(odd_ref, even_refs, low_all, flip)
    out_ref[...] = jnp.zeros_like(out_ref)
    pairs = tile_refs[0].shape[0] // 2
    blocks = gram_ref.shape[0] // SUB

    def beside(b):
        for j in range(b * pairs // blocks, (b + 1) * pairs // blocks):
            at = slice(j * PAIR, (j + 1) * PAIR)
            product[:, at] = first_ref[:, at] + jnp.dot(
                low_t, side_by_side(tile_refs, 2 * j, 2), preferred_element_type=jnp.float32
            )

    inverse = three(invert_factor(gram_ref[...] + self_product(low_t), beside))
    rank = inverse[0].shape[0]
    stack = jnp.concatenate(inverse, axis=0).astype(jnp.bfloat16)
    q = own_refs[0].shape[1 if flip else 0]
    for i, ref in enumerate(own_refs):
        own = ref[...] if flip else ref[...].T
        parts = jnp.dot(stack, own, preferred_element_type=jnp.float32)
        basis = parts[:rank] + (parts[rank : 2 * rank] + parts[2 * rank :])
        basis_ref[i * q : (i + 1) * q, :] = basis.T

    def group(j, carry):
        parts = three(product[:, pl.ds(pl.multiple_of(j * HALF, HALF), HALF)])
        cols, rest = 0.0, 0.0
        for k, part in enumerate(parts):
            got = jnp.dot(
                stack[: (3 - k) * rank], part.astype(jnp.bfloat16), preferred_element_type=jnp.float32
            )
            for i in range(3 - k):
                if i + k == 0:
                    cols = got[:rank]
                else:
                    rest = rest + got[i * rank : (i + 1) * rank]
        cols = (cols + rest).astype(jnp.bfloat16)
        for k in range(FEW):

            @pl.when(FEW * j + k < count)
            def _():
                at = pl.multiple_of(order_ref[FEW * j + k] * WIDTH, WIDTH)
                out_ref[0, :, pl.ds(at, WIDTH)] = cols[:, k * WIDTH : (k + 1) * WIDTH]

        return carry

    lax.fori_loop(0, (count + FEW - 1) // FEW, group, 0)


def project_pass(order, first, gram, odd, owns, even, tiles, panels, rank, flip):
    rows = sum(t.shape[1] for t in tiles)
    held = tiles[0].shape[0]
    q = owns[0].shape[1 if flip else 0]
    vmem = pl.BlockSpec(memory_space=pltpu.VMEM)
    return pl.pallas_call(
        functools.partial(
            project_kernel, panels=panels, half=len(even), owns=len(owns), flip=flip
        ),
        in_specs=[pl.BlockSpec(memory_space=pltpu.SMEM)]
        + [vmem] * (3 + len(owns) + len(even) + len(tiles)),
        out_specs=[vmem, vmem],
        out_shape=[
            jax.ShapeDtypeStruct((q * len(owns), rank), jnp.float32),
            jax.ShapeDtypeStruct((1, rank, panels * WIDTH), jnp.bfloat16),
        ],
        scratch_shapes=[
            pltpu.VMEM((rank, rows) if flip else (rows, rank), jnp.bfloat16),
            pltpu.VMEM((rank, held * WIDTH), jnp.float32),
        ],
        compiler_params=pltpu.CompilerParams(vmem_limit_bytes=14 * 2**20),
        name="project_pass",
    )(
        order, first, gram, odd, *owns, *even,
        *(pltpu.with_memory_space_constraint(x, pltpu.VMEM) for x in tiles),
    )


def join_kernel(*refs):
    for k, ref in enumerate(refs[:-1]):
        refs[-1][k] = ref[...]


def join(parts):
    shape = jax.ShapeDtypeStruct((len(parts), *parts[0].shape), parts[0].dtype)
    return in_vmem(join_kernel, shape, "join")(*parts)


def after(x, *deps):
    return lax.optimization_barrier((x, *deps))[0]


def swap(x, k, n):
    return lax.ppermute(x, "tile", [(i, i ^ k) for i in range(n)])


CHUNKS = 2


def local(row_points, source_points, sketch, admissible):
    n = lax.axis_size("tile")
    panels = admissible.shape[1]
    rows = row_points.shape[1] // lax.axis_size("row")
    own_rows = rows // n
    q = own_rows // CHUNKS
    odd, even = list(range(1, n, 2)), list(range(0, n, 2))
    slices = [(k, c * q, q) for c in range(CHUNKS) for k in odd + even]
    place = flip = q % WIDTH == 0
    points = row_points
    if not place:
        me = lax.axis_index("tile")
        points = lax.dynamic_slice_in_dim(row_points, lax.axis_index("row") * rows, rows, 1)
        points = jnp.concatenate(
            [lax.dynamic_slice_in_dim(points, (me ^ k) * own_rows + first, q, 1) for k, first, _ in slices], 1
        )
    order, src_pick, omega_pick, row_mat = prep(
        admissible, points, source_points, sketch, rows, slices, place
    )

    half_rows = rows // CHUNKS // 2

    def sketch_part(first, size, *deps):
        return sketch_pass(after(order, *deps), src_pick, omega_pick, row_mat, first, size, panels)

    def z_swaps(parts, *deps):
        got = []
        for x, k in zip(parts, even[1:]):
            if deps and k == even[-1]:
                x = after(x, *deps, *got)
            got.append(swap(x, k, n))
        return got

    def along_z(low, *deps):
        return [low, *z_swaps([low] * (n // 2 - 1), *deps)]

    theirs, kept0 = sketch_part(0, half_rows)
    got = swap(theirs, 1, n)
    own, kept1 = sketch_part(half_rows, half_rows, theirs)
    kept, *sent = pair_sum([own], [got], n // 2)

    part = half_rows // 2
    start = 2 * half_rows
    theirs_a, kept2 = sketch_part(start, part, own, kept)
    got_z = z_swaps(sent, theirs_a)
    got_a = swap(theirs_a, 1, n)
    theirs_b, kept3 = sketch_part(start + part, part, theirs_a)
    got_b = swap(theirs_b, 1, n)
    low = row_sum(after(kept, theirs_b), got_z, flip)
    own_a, kept4 = sketch_part(start + 2 * part, part, theirs_b, low)
    held = [along_z(low, own_a)]
    own_b, kept5 = sketch_part(start + 3 * part, part, own_a)
    kept, *sent = pair_sum([own_a, after(own_b, *held[0])], [got_a, got_b], n // 2)
    tiles = [kept0, kept1, kept2, kept3, kept4, kept5]
    rank = sketch.shape[1]

    def across(pieces, *deps):
        return swap(join([after(pieces[0], *deps), *pieces[1:]]), 1, n)

    odd = across(held[0], own_b)
    first, gram = first_pass(order, odd, held[0], tiles[:2], panels, rank, flip)
    got_z = z_swaps(sent)
    held.append(along_z(row_sum(after(kept, gram), got_z, flip)))
    owns = [h[0] for h in held]
    return project_pass(
        order, first, gram, across(held[1]), owns, held[1], tiles[2:], panels, rank, flip
    )


def solution(mesh):
    in_specs = (P(), P(None, "tile"), P("tile", None), P("row", "tile"))
    out_specs = (P(("row", "tile"), None), P("row", None, "tile"))
    return jax.shard_map(local, mesh=mesh, in_specs=in_specs, out_specs=out_specs, check_vma=False)
```

```python
import functools
import math

import jax
import jax.numpy as jnp
from jax import lax
from jax.experimental import pallas as pl
from jax.experimental.pallas import tpu as pltpu
from jax.sharding import PartitionSpec as P

DAMPING = 0.25
WAVENUM = 24.0
SHIFT = 0.0001

TURNS = WAVENUM / (2.0 * math.pi)
DECAY = -DAMPING / TURNS / math.log(2.0)
AMP = TURNS / (4.0 * math.pi)
S0, S1, S2 = 6.28127979 * AMP, -41.0952178 * AMP, 73.5851113 * AMP

WIDTH = 128
PAIR = 2 * WIDTH
TERMS = 32
SUB = 8
PIECE = 16
GROUP = 16
FEW = 4
HALF = FEW * WIDTH


def head(x):
    return x.astype(jnp.bfloat16).astype(jnp.float32)


def three(x):
    a = head(x)
    b = head(x - a)
    return a, b, x - a - b


def fill_terms(ref, points, side):
    at = lax.broadcasted_iota(jnp.int32, points.shape, 0)
    x = points - jnp.where(at == 2, -0.5, 3.0)
    scale = TURNS * TURNS
    norm = three(scale * jnp.sum(x * x, axis=0, keepdims=True))
    one = jnp.ones_like(norm[0])
    if side == 0:
        h, m, l = three(x)
        rows = [h, h, m, h, l, m]
        tail = [*norm, one, one, one]
    else:
        h, m, l = three(x * (-2.0 * scale))
        rows = [h, m, h, l, h, m]
        tail = [one, one, one, *norm]
    ref[...] = jnp.zeros_like(ref)
    for at, row in enumerate(rows):
        ref[3 * at : 3 * at + 3, :] = row
    for at, row in enumerate(tail):
        ref[18 + at : 19 + at, :] = row


def near_field(square):
    inv = lax.rsqrt(square)
    t = square * inv
    f = t - jnp.round(t)
    g = 0.25 - jnp.abs(f)
    v = g * g
    wave = ((S2 * v + S1) * v + S0) * g
    amp = jnp.exp2(DECAY * t) * inv
    return (wave * amp).astype(jnp.bfloat16)


def order_panels(flags_ref, order_ref, panels):
    def step(p, count):
        @pl.when(flags_ref[0, p] > 0)
        def _():
            order_ref[count] = p

        return count + (flags_ref[0, p] > 0).astype(jnp.int32)

    count = lax.fori_loop(0, panels, step, jnp.int32(0))
    order_ref[panels] = count
    return count


def prep_kernel(
    flags_hbm, rows_hbm, src_hbm, omega_hbm, order_ref, src_pick, omega_pick, row_mat,
    flags, points, picked, row_terms, src_terms, sources, sems, sem, *, slices, place
):
    panels = flags.shape[1]
    rows = points.shape[1]
    me = lax.axis_index("tile")
    at = pl.multiple_of(lax.axis_index("row") * rows, rows) if place else 0
    copies = [
        pltpu.make_async_copy(flags_hbm, flags, sems.at[0]),
        pltpu.make_async_copy(rows_hbm.at[:, pl.ds(at, rows)], points, sems.at[1]),
        pltpu.make_async_copy(src_hbm, sources, sems.at[2]),
    ]
    for copy in copies:
        copy.start()
    copies[0].wait()
    count = order_panels(flags, order_ref, panels)

    def fetch(slot):
        at = pl.multiple_of(order_ref[slot] * WIDTH, WIDTH)
        to = pl.multiple_of(slot * WIDTH, WIDTH)
        return pltpu.make_async_copy(
            omega_hbm.at[pl.ds(at, WIDTH), :], omega_pick.at[pl.ds(to, WIDTH), :], sem
        )

    def start(slot, carry):
        fetch(slot).start()
        return carry

    lax.fori_loop(0, count, start, 0)
    copies[1].wait()
    if place:
        to = 0
        for k, first, size in slices:
            at = pl.multiple_of((me ^ k) * (rows // lax.axis_size("tile")) + first, WIDTH)
            picked[:, to : to + size] = points[:, pl.ds(at, size)]
            to += size
        fill_terms(row_terms, picked[...], 0)
    else:
        fill_terms(row_terms, points[...], 0)
    step = min(512, rows)
    for r in range(0, rows, step):
        row_mat[r : r + step, :] = row_terms[:, r : r + step].T.astype(jnp.bfloat16)
    copies[2].wait()
    fill_terms(src_terms, sources[...], 1)

    def pick(slot, carry):
        at = pl.multiple_of(order_ref[slot] * WIDTH, WIDTH)
        to = pl.multiple_of(slot * WIDTH, WIDTH)
        src_pick[:, pl.ds(to, WIDTH)] = src_terms[:, pl.ds(at, WIDTH)].astype(jnp.bfloat16)
        return carry

    lax.fori_loop(0, count, pick, 0)
    spare = src_terms[:, :WIDTH].astype(jnp.bfloat16)

    def pad(slot, carry):
        to = pl.multiple_of(slot * WIDTH, WIDTH)
        src_pick[:, pl.ds(to, WIDTH)] = spare
        omega_pick[pl.ds(to, WIDTH), :] = jnp.zeros((WIDTH, omega_pick.shape[1]), jnp.bfloat16)
        return carry

    lax.fori_loop(count, GROUP * ((count + GROUP - 1) // GROUP), pad, 0)

    def finish(slot, carry):
        fetch(slot).wait()
        return carry

    lax.fori_loop(0, count, finish, 0)


def in_hbm(x):
    return pltpu.with_memory_space_constraint(x, pltpu.HBM)


def prep(admissible, points, source_points, sketch, rows, slices, place):
    panels = admissible.shape[1]
    cols, rank = sketch.shape
    spare = GROUP * ((panels + GROUP - 1) // GROUP) * WIDTH
    hbm = pl.BlockSpec(memory_space=pltpu.HBM)
    vmem = pl.BlockSpec(memory_space=pltpu.VMEM)
    return pl.pallas_call(
        functools.partial(prep_kernel, slices=slices, place=place),
        in_specs=[hbm] * 4,
        out_specs=[pl.BlockSpec(memory_space=pltpu.SMEM), vmem, vmem, vmem],
        out_shape=[
            jax.ShapeDtypeStruct((panels + 8,), jnp.int32),
            jax.ShapeDtypeStruct((TERMS, spare), jnp.bfloat16),
            jax.ShapeDtypeStruct((spare, rank), jnp.bfloat16),
            jax.ShapeDtypeStruct((rows, TERMS), jnp.bfloat16),
        ],
        scratch_shapes=[
            pltpu.SMEM((1, panels), jnp.int32),
            pltpu.VMEM((3, rows), jnp.float32),
            pltpu.VMEM((3, rows), jnp.float32),
            pltpu.VMEM((TERMS, rows), jnp.float32),
            pltpu.VMEM((TERMS, cols), jnp.float32),
            pltpu.VMEM((3, cols), jnp.float32),
            pltpu.SemaphoreType.DMA((3,)),
            pltpu.SemaphoreType.DMA,
        ],
        compiler_params=pltpu.CompilerParams(vmem_limit_bytes=16 * 2**20),
        name="prep",
    )(*(in_hbm(x) for x in (admissible, points, source_points, sketch)))


def sketch_kernel(
    order_ref, src_pick, omega_pick, row_mat, part_ref, tiles_ref, total, *, first, panels, rb
):
    groups = (order_ref[panels] + GROUP - 1) // GROUP
    cols = GROUP * WIDTH

    def block(b, carry):
        here = pl.ds(pl.multiple_of(b * rb, rb), rb)
        total[...] = jnp.zeros_like(total)

        def body(j, carry):
            at = pl.ds(pl.multiple_of(j * cols, cols), cols)
            rows = row_mat[pl.ds(pl.multiple_of(first + b * rb, rb), rb), :]
            src = src_pick[:, at]
            omega = omega_pick[at, :]
            sums = total[...]
            near = []
            for c in range(0, cols, PAIR):
                square = jnp.dot(rows, src[:, c : c + PAIR], preferred_element_type=jnp.float32)
                tile = [near_field(square[r : r + PIECE]) for r in range(0, rb, PIECE)]
                tile = jnp.concatenate(tile, axis=0)
                sums += jnp.dot(tile, omega[c : c + PAIR], preferred_element_type=jnp.float32)
                near.append(tile)
            total[...] = sums
            for k in range(GROUP):
                tile = near[k * WIDTH // PAIR]
                at = k * WIDTH % PAIR
                tiles_ref[GROUP * j + k, here, :] = tile[:, at : at + WIDTH]
            return carry

        lax.fori_loop(0, groups, body, 0)
        part_ref[here, :] = total[...]
        return carry

    lax.fori_loop(0, part_ref.shape[0] // rb, block, 0)


def sketch_pass(order, src_pick, omega_pick, row_mat, first, rows, panels):
    rank = omega_pick.shape[1]
    rb = min(512, rows)
    vmem = pl.BlockSpec(memory_space=pltpu.VMEM)
    return pl.pallas_call(
        functools.partial(sketch_kernel, first=first, panels=panels, rb=rb),
        in_specs=[pl.BlockSpec(memory_space=pltpu.SMEM), vmem, vmem, vmem],
        out_specs=[vmem, vmem],
        out_shape=[
            jax.ShapeDtypeStruct((rows, rank), jnp.float32),
            pltpu.VMEM((GROUP * ((panels + GROUP - 1) // GROUP), rows, WIDTH), jnp.bfloat16),
        ],
        scratch_shapes=[
            pltpu.VMEM((rb, rank), jnp.float32),
        ],
        compiler_params=pltpu.CompilerParams(vmem_limit_bytes=10 * 2**20),
        cost_estimate=pl.CostEstimate(
            flops=rows * panels * WIDTH * rank * 16, bytes_accessed=rows * panels * WIDTH * 2, transcendentals=0
        ),
        name="sketch_pass",
    )(order, src_pick, omega_pick, row_mat)


def in_vmem(kernel, out_shape, name):
    def call(*args):
        vmem = pl.BlockSpec(memory_space=pltpu.VMEM)
        return pl.pallas_call(
            kernel,
            in_specs=[vmem] * len(args),
            out_specs=jax.tree.map(lambda _: vmem, out_shape),
            out_shape=out_shape,
            compiler_params=pltpu.CompilerParams(vmem_limit_bytes=8 * 2**20),
            name=name,
        )(*args)

    return call


def pair_sum_kernel(*refs, parts):
    own_refs, got_refs, out_refs = refs[:parts], refs[parts : 2 * parts], refs[2 * parts :]
    q = out_refs[0].shape[0]
    each = len(out_refs) // parts
    for k, out_ref in enumerate(out_refs):
        rows = slice(k % each * q, (k % each + 1) * q)
        value = own_refs[k // each][rows, :] + got_refs[k // each][rows, :]
        out_ref[...] = value.astype(out_ref.dtype)


def pair_sum(owns, gots, slots):
    q, rank = sum(x.shape[0] for x in owns) // slots, owns[0].shape[1]
    shapes = [jax.ShapeDtypeStruct((q, rank), jnp.float32)]
    shapes += [jax.ShapeDtypeStruct((q, rank), jnp.bfloat16)] * (slots - 1)
    kernel = functools.partial(pair_sum_kernel, parts=len(owns))
    return in_vmem(kernel, shapes, "pair_sum")(*owns, *gots)


def row_sum_kernel(kept_ref, *refs):
    total = kept_ref[...]
    for ref in refs[:-1]:
        total = total + ref[...].astype(jnp.float32)
    low = head(total)
    refs[-1][...] = (low if refs[-1].shape == low.shape else low.T).astype(jnp.bfloat16)


def row_sum(kept, got, flip):
    shape = kept.shape[::-1] if flip else kept.shape
    return in_vmem(row_sum_kernel, jax.ShapeDtypeStruct(shape, jnp.bfloat16), "row_sum")(kept, *got)


def invert_factor(gram, beside):
    n = gram.shape[0]
    pieces = n // SUB
    lane = lax.broadcasted_iota(jnp.int32, (SUB, n), 1)
    sub = lax.broadcasted_iota(jnp.int32, (SUB, n), 0)
    trace = jnp.zeros((SUB, n), jnp.float32)
    for v in range(pieces):
        trace = trace + jnp.where(lane == sub + v * SUB, gram[v * SUB : (v + 1) * SUB, :], 0.0)
    shift = (SHIFT / n) * jnp.sum(trace)
    a = [
        gram[v * SUB : (v + 1) * SUB, :] + jnp.where(lane == sub + v * SUB, shift, 0.0)
        for v in range(pieces)
    ]
    for b in range(pieces):
        beside(b)
        cols = [
            {v: jnp.broadcast_to(a[v][:, b * SUB + c : b * SUB + c + 1], (SUB, n)) for v in range(b, pieces)}
            for c in range(SUB)
        ]
        for c in range(SUB):
            j = b * SUB + c
            pivot = jnp.broadcast_to(cols[c][b][c : c + 1, :], (SUB, n))
            inv = 1.0 / pivot
            row = jnp.broadcast_to(a[b][c : c + 1, :], (SUB, n))
            row = jnp.where(lane == j, 1.0, row)
            nexts = {
                c2: jnp.broadcast_to(cols[c2][b][c : c + 1, :], (SUB, n)) for c2 in range(c + 1, SUB)
            }
            for v in range(b, pieces):
                m = cols[c][v] * inv
                here = lane == j
                if v == b:
                    m = jnp.where(sub > c, m, 0.0)
                    here = here & (sub > c)
                a[v] = jnp.where(here, 0.0, a[v]) - m * row
                for c2 in range(c + 1, SUB):
                    cols[c2][v] = cols[c2][v] - m * nexts[c2]
    out = []
    for v in range(pieces):
        diag = lane == sub + v * SUB
        d = jnp.sum(jnp.where(diag, a[v], 0.0), axis=1, keepdims=True)
        low = jnp.where(lane < sub + v * SUB, a[v], jnp.where(diag, 1.0, 0.0))
        out.append(low * lax.rsqrt(d))
    return jnp.concatenate(out, axis=0)


def gather_low(odd_ref, even_refs, low_all, flip):
    half, q = odd_ref.shape[0], odd_ref.shape[2 if flip else 1]
    pieces = [odd_ref.at[k] for k in range(half)] + list(even_refs)
    for i, ref in enumerate(pieces):
        if flip:
            low_all[:, i * q : (i + 1) * q] = ref[...]
        else:
            low_all[i * q : (i + 1) * q, :] = ref[...]
    return low_all[...] if flip else low_all[...].T


def self_product(low_t):
    return lax.dot_general(low_t, low_t, (((1,), (1,)), ((), ())), preferred_element_type=jnp.float32)


def side_by_side(tile_refs, first, count):
    return jnp.concatenate(
        [jnp.concatenate([ref[first + k] for k in range(count)], axis=1) for ref in tile_refs], axis=0
    )


def first_kernel(order_ref, odd_ref, *refs, panels, half, flip):
    even_refs, tile_refs = refs[:half], refs[half:-3]
    product_ref, gram_ref, low_all = refs[-3:]
    low_t = gather_low(odd_ref, even_refs, low_all, flip)
    gram_ref[...] = self_product(low_t)

    def group(j, carry):
        at = pl.ds(pl.multiple_of(j * HALF, HALF), HALF)
        product_ref[:, at] = jnp.dot(
            low_t, side_by_side(tile_refs, FEW * j, FEW), preferred_element_type=jnp.float32
        )
        return carry

    lax.fori_loop(0, (order_ref[panels] + FEW - 1) // FEW, group, 0)


def first_pass(order, odd, even, tiles, panels, rank, flip):
    rows = sum(t.shape[1] for t in tiles)
    held = tiles[0].shape[0]
    vmem = pl.BlockSpec(memory_space=pltpu.VMEM)
    return pl.pallas_call(
        functools.partial(first_kernel, panels=panels, half=len(even), flip=flip),
        in_specs=[pl.BlockSpec(memory_space=pltpu.SMEM)] + [vmem] * (1 + len(even) + len(tiles)),
        out_specs=[vmem, vmem],
        out_shape=[
            jax.ShapeDtypeStruct((rank, held * WIDTH), jnp.float32),
            jax.ShapeDtypeStruct((rank, rank), jnp.float32),
        ],
        scratch_shapes=[pltpu.VMEM((rank, rows) if flip else (rows, rank), jnp.bfloat16)],
        compiler_params=pltpu.CompilerParams(vmem_limit_bytes=12 * 2**20),
        cost_estimate=pl.CostEstimate(
            flops=2 * rows * panels * WIDTH * rank, bytes_accessed=0, transcendentals=0
        ),
        name="first_pass",
    )(order, odd, *even, *(pltpu.with_memory_space_constraint(x, pltpu.VMEM) for x in tiles))


def project_kernel(order_ref, first_ref, gram_ref, odd_ref, *refs, panels, half, owns, flip):
    own_refs, even_refs = refs[:owns], refs[owns : owns + half]
    tile_refs = refs[owns + half : -4]
    basis_ref, out_ref, low_all, product = refs[-4:]
    count = order_ref[panels]
    low_t = gather_low(odd_ref, even_refs, low_all, flip)
    out_ref[...] = jnp.zeros_like(out_ref)
    pairs = tile_refs[0].shape[0] // 2
    blocks = gram_ref.shape[0] // SUB

    def beside(b):
        for j in range(b * pairs // blocks, (b + 1) * pairs // blocks):
            at = slice(j * PAIR, (j + 1) * PAIR)
            product[:, at] = first_ref[:, at] + jnp.dot(
                low_t, side_by_side(tile_refs, 2 * j, 2), preferred_element_type=jnp.float32
            )

    inverse = three(invert_factor(gram_ref[...] + self_product(low_t), beside))
    rank = inverse[0].shape[0]
    stack = jnp.concatenate(inverse, axis=0).astype(jnp.bfloat16)
    q = own_refs[0].shape[1 if flip else 0]
    for i, ref in enumerate(own_refs):
        own = ref[...] if flip else ref[...].T
        parts = jnp.dot(stack, own, preferred_element_type=jnp.float32)
        basis = parts[:rank] + (parts[rank : 2 * rank] + parts[2 * rank :])
        basis_ref[i * q : (i + 1) * q, :] = basis.T

    def group(j, carry):
        parts = three(product[:, pl.ds(pl.multiple_of(j * HALF, HALF), HALF)])
        cols, rest = 0.0, 0.0
        for k, part in enumerate(parts):
            got = jnp.dot(
                stack[: (3 - k) * rank], part.astype(jnp.bfloat16), preferred_element_type=jnp.float32
            )
            for i in range(3 - k):
                if i + k == 0:
                    cols = got[:rank]
                else:
                    rest = rest + got[i * rank : (i + 1) * rank]
        cols = (cols + rest).astype(jnp.bfloat16)
        for k in range(FEW):

            @pl.when(FEW * j + k < count)
            def _():
                at = pl.multiple_of(order_ref[FEW * j + k] * WIDTH, WIDTH)
                out_ref[0, :, pl.ds(at, WIDTH)] = cols[:, k * WIDTH : (k + 1) * WIDTH]

        return carry

    lax.fori_loop(0, (count + FEW - 1) // FEW, group, 0)


def project_pass(order, first, gram, odd, owns, even, tiles, panels, rank, flip):
    rows = sum(t.shape[1] for t in tiles)
    held = tiles[0].shape[0]
    q = owns[0].shape[1 if flip else 0]
    vmem = pl.BlockSpec(memory_space=pltpu.VMEM)
    return pl.pallas_call(
        functools.partial(
            project_kernel, panels=panels, half=len(even), owns=len(owns), flip=flip
        ),
        in_specs=[pl.BlockSpec(memory_space=pltpu.SMEM)]
        + [vmem] * (3 + len(owns) + len(even) + len(tiles)),
        out_specs=[vmem, vmem],
        out_shape=[
            jax.ShapeDtypeStruct((q * len(owns), rank), jnp.float32),
            jax.ShapeDtypeStruct((1, rank, panels * WIDTH), jnp.bfloat16),
        ],
        scratch_shapes=[
            pltpu.VMEM((rank, rows) if flip else (rows, rank), jnp.bfloat16),
            pltpu.VMEM((rank, held * WIDTH), jnp.float32),
        ],
        compiler_params=pltpu.CompilerParams(vmem_limit_bytes=14 * 2**20),
        name="project_pass",
    )(
        order, first, gram, odd, *owns, *even,
        *(pltpu.with_memory_space_constraint(x, pltpu.VMEM) for x in tiles),
    )


def join_kernel(*refs):
    for k, ref in enumerate(refs[:-1]):
        refs[-1][k] = ref[...]


def join(parts):
    shape = jax.ShapeDtypeStruct((len(parts), *parts[0].shape), parts[0].dtype)
    return in_vmem(join_kernel, shape, "join")(*parts)


def after(x, *deps):
    return lax.optimization_barrier((x, *deps))[0]


def swap(x, k, n):
    return lax.ppermute(x, "tile", [(i, i ^ k) for i in range(n)])


CHUNKS = 2


def local(row_points, source_points, sketch, admissible):
    n = lax.axis_size("tile")
    panels = admissible.shape[1]
    rows = row_points.shape[1] // lax.axis_size("row")
    own_rows = rows // n
    q = own_rows // CHUNKS
    odd, even = list(range(1, n, 2)), list(range(0, n, 2))
    slices = [(k, c * q, q) for c in range(CHUNKS) for k in odd + even]
    place = flip = q % WIDTH == 0
    points = row_points
    if not place:
        me = lax.axis_index("tile")
        points = lax.dynamic_slice_in_dim(row_points, lax.axis_index("row") * rows, rows, 1)
        points = jnp.concatenate(
            [lax.dynamic_slice_in_dim(points, (me ^ k) * own_rows + first, q, 1) for k, first, _ in slices], 1
        )
    order, src_pick, omega_pick, row_mat = prep(
        admissible, points, source_points, sketch, rows, slices, place
    )

    half_rows = rows // CHUNKS // 2

    def sketch_part(first, size, *deps):
        return sketch_pass(after(order, *deps), src_pick, omega_pick, row_mat, first, size, panels)

    def z_swaps(parts, *deps):
        got = []
        for x, k in zip(parts, even[1:]):
            if deps and k == even[-1]:
                x = after(x, *deps, *got)
            got.append(swap(x, k, n))
        return got

    def along_z(low, *deps):
        return [low, *z_swaps([low] * (n // 2 - 1), *deps)]

    theirs, kept0 = sketch_part(0, half_rows)
    got = swap(theirs, 1, n)
    own, kept1 = sketch_part(half_rows, half_rows, theirs)
    kept, *sent = pair_sum([own], [got], n // 2)

    part = half_rows // 2
    start = 2 * half_rows
    theirs_a, kept2 = sketch_part(start, part, own, kept)
    got_z = z_swaps(sent, theirs_a)
    got_a = swap(theirs_a, 1, n)
    theirs_b, kept3 = sketch_part(start + part, part, theirs_a)
    got_b = swap(theirs_b, 1, n)
    low = row_sum(after(kept, theirs_b), got_z, flip)
    own_a, kept4 = sketch_part(start + 2 * part, part, theirs_b, low)
    held = [along_z(low, own_a)]
    own_b, kept5 = sketch_part(start + 3 * part, part, own_a)
    kept, *sent = pair_sum([own_a, after(own_b, *held[0])], [got_a, got_b], n // 2)
    tiles = [kept0, kept1, kept2, kept3, kept4, kept5]
    rank = sketch.shape[1]

    def across(pieces, *deps):
        return swap(join([after(pieces[0], *deps), *pieces[1:]]), 1, n)

    odd = across(held[0], own_b)
    first, gram = first_pass(order, odd, held[0], tiles[:2], panels, rank, flip)
    got_z = z_swaps(sent)
    held.append(along_z(row_sum(after(kept, gram), got_z, flip)))
    owns = [h[0] for h in held]
    return project_pass(
        order, first, gram, across(held[1]), owns, held[1], tiles[2:], panels, rank, flip
    )


def solution(mesh):
    in_specs = (P(), P(None, "tile"), P("tile", None), P("row", "tile"))
    out_specs = (P(("row", "tile"), None), P("row", None, "tile"))
    return jax.shard_map(local, mesh=mesh, in_specs=in_specs, out_specs=out_specs, check_vma=False)
```
